32 devices in a mesh: groups: 2 (over y), hid: 4 (over z), rows: 2 (over x), mp: 2 (over core).
Axes of the slice: x: 2, y: 2, z: 4, core: 2. Of those that a mesh axis runs over, the one named last changes fastest.
Arguments:
- tokens: bfloat16 [1024, 4096], P(('groups', 'rows'), 'hid'), parts along dimension 0, may hold values from -6 to 6
- norm_gain: float32 [2, 4096], P('mp'), may hold values from 0.1 to 1.9
- gate_weight: bfloat16 [2, 4096, 14336], P('mp', 'rows', 'hid'), may hold values from -0.09375 to 0.09375
- up_weight: bfloat16 [2, 4096, 14336], P('mp', 'rows', 'hid'), may hold values from -0.09375 to 0.09375
- down_weight: bfloat16 [2, 14336, 4096], P('mp', 'hid', 'rows'), may hold values from -0.046875 to 0.046875
- enc_weight: bfloat16 [2, 4096, 16384], P('mp', 'rows', 'hid'), may hold values from -0.0625 to 0.0625
- enc_bias: float32 [16384], P('hid'), may hold values from -3 to 3
- adjoint: bfloat16 [1024, 16384], P(('groups', 'rows', 'mp'), 'hid'), parts along dimension 0, may hold values from -6 to 6
Outputs:
- gated: bfloat16 [1024, 16384], P(('groups', 'rows', 'mp'), 'hid'), parts along dimension 0
The draws below stay inside these ranges and needn't reach their ends.
There are 2 independent parts, one for each index of `groups`. The reference program is written for one: setup_inputs(seed, part) draws one part's arguments, and reference() takes and returns one part's arrays. A program takes and returns all parts, laid end to end along the dimension named above; an argument that names none is the same for every part. Nothing has to cross between parts.
All inputs are finite; a program needn't handle non-finite values.
Results may differ from the reference program's by a relative error of at most 0.0058.
Values may be sent and summed in bfloat16 or wider, within the bound.
No kernel may reach another device: no remote copies, remote signals or barrier semaphores. Data moves between devices by JAX's collectives and lax.ppermute only.
A program may use at most 128 MiB of HBM per device.

```python
import jax
import jax.numpy as jnp
from jax import lax

D = 4096
FF = 14336
FEATURES = 16384
TOKENS = 512


def levels(stream_key, dims, split, smallest, top_value):
    def one(axis_at, shards_of):
        steps = jax.random.uniform(jax.random.fold_in(jax.random.fold_in(stream_key, 6), axis_at), (shards_of,), jnp.float32, smallest / len(split), top_value / len(split))
        return jnp.repeat(jnp.exp(steps), dims[axis_at] // shards_of).reshape((-1,) + (1,) * (len(dims) - axis_at - 1))

    loudness = one(*split[0])
    for cut in split[1:]:
        loudness = loudness * one(*cut)
    return loudness


def scatter_about(key, dims, spread, reach, pieces=(), kind=jnp.bfloat16):
    values = spread * jax.random.normal(key, dims, jnp.float32)
    if pieces:
        values = values * levels(key, dims, pieces, -0.22, 0.18)
    return jnp.clip(values, -reach, reach).astype(kind)


def setup_inputs(seed: int = 0, part: int = 0) -> dict:
    splits = jax.random.split(jax.random.key(seed), 9)
    own_keys = jax.random.split(jax.random.fold_in(splits[8], part), 9)
    return {
        "tokens": scatter_about(own_keys[0], (TOKENS, D), 1.0, 6.0, ((0, 2), (1, 4))),
        "norm_gain": jnp.clip(1.0 + 0.18 * jax.random.normal(splits[1], (2, D), jnp.float32), 0.1, 1.9),
        "gate_weight": scatter_about(splits[2], (2, D, FF), D ** -0.5, 0.09375, ((0, 2), (1, 2), (2, 4))),
        "up_weight": scatter_about(splits[3], (2, D, FF), D ** -0.5, 0.09375, ((0, 2), (1, 2), (2, 4))),
        "down_weight": scatter_about(splits[4], (2, FF, D), FF ** -0.5, 0.046875, ((0, 2), (1, 4), (2, 2))),
        "enc_weight": scatter_about(splits[5], (2, D, FEATURES), (2 * D) ** -0.5, 0.0625, ((0, 2), (1, 2), (2, 4))),
        "enc_bias": scatter_about(splits[6], (FEATURES,), 0.5, 3.0, ((0, 4),), jnp.float32),
        "adjoint": scatter_about(own_keys[7], (TOKENS, FEATURES), 1.0, 6.0, ((0, 4), (1, 4))),
    }


def reference(tokens, norm_gain, gate_weight, up_weight, down_weight, enc_weight, enc_bias, adjoint):
    tokens_float = tokens.astype(jnp.float32)
    inverse_rms = lax.rsqrt(lax.optimization_barrier(jnp.mean(tokens_float * tokens_float, axis=-1, keepdims=True)) + 1e-05)
    outputs = []
    for member in range(2):
        normed = (tokens_float * inverse_rms * norm_gain[member][None, :]).astype(jnp.bfloat16)
        gate_acts = jnp.dot(normed, gate_weight[member], preferred_element_type=jnp.float32)
        up_acts = jnp.dot(normed, up_weight[member], preferred_element_type=jnp.float32)
        hidden = (jax.nn.silu(gate_acts) * up_acts).astype(jnp.bfloat16)
        outputs.append(jnp.dot(hidden, down_weight[member], preferred_element_type=jnp.float32).astype(jnp.bfloat16))
    joined = jnp.concatenate(outputs, axis=1)
    pre = jnp.dot(joined, enc_weight.reshape(2 * D, FEATURES), preferred_element_type=jnp.float32) + enc_bias[None, :]
    return (jnp.maximum(pre, 0.0) * adjoint.astype(jnp.float32)).astype(jnp.bfloat16)
```

```python
import functools

import jax
import jax.numpy as jnp
from jax import lax
from jax.experimental import pallas as pl
from jax.experimental.pallas import tpu as pltpu
from jax.sharding import PartitionSpec as P

BF16 = jnp.bfloat16
F32 = jnp.float32
VMEM_BYTES = 40 * 1024 * 1024


def shift(value, axis, size, hop):
    return lax.ppermute(value, axis, [((d + hop) % size, d) for d in range(size)])


def send(value, axis, size, hop):
    return lax.ppermute(value, axis, [(d, (d + hop) % size) for d in range(size)])


def tile_of(width, most):
    tile = most
    while tile > 128 and width % tile:
        tile //= 2
    return tile if width % tile == 0 else width


def whole(shape):
    return pl.BlockSpec(shape, lambda j, *_: (0,) * len(shape))


def params():
    return pltpu.CompilerParams(
        dimension_semantics=("arbitrary",), vmem_limit_bytes=VMEM_BYTES
    )


def cost(rows, depth, width):
    return pl.CostEstimate(
        flops=2 * rows * depth * width,
        bytes_accessed=2 * (rows * depth + depth * width + rows * width),
        transcendentals=0,
    )


def gate_up_body(owners, x_ref, gate_ref, up_ref, own_ref, *send_refs):
    rows = x_ref.shape[0] // owners
    x = x_ref[...]
    for at, weight_ref in enumerate((gate_ref, up_ref)):
        acts = jnp.dot(x, weight_ref[0], preferred_element_type=F32)
        own_ref[at] = acts[:rows]
        for hop in range(1, owners):
            send_refs[hop - 1][at] = acts[hop * rows : (hop + 1) * rows].astype(BF16)


def gate_up(x, gate_weight, up_weight, owners, piece, pieces):
    rows, depth = x.shape
    width = gate_weight.shape[2] // pieces
    tile = tile_of(width, 256)
    tiles = width // tile
    own_rows = rows // owners
    weight_spec = pl.BlockSpec((1, depth, tile), lambda j: (0, 0, j + piece * tiles))
    out_spec = pl.BlockSpec((2, own_rows, tile), lambda j: (0, 0, j))
    return pl.pallas_call(
        functools.partial(gate_up_body, owners),
        grid=(tiles,),
        in_specs=[whole((rows, depth)), weight_spec, weight_spec],
        out_specs=[out_spec] * owners,
        out_shape=[jax.ShapeDtypeStruct((2, own_rows, width), F32)]
        + [jax.ShapeDtypeStruct((2, own_rows, width), BF16)] * (owners - 1),
        compiler_params=params(),
        cost_estimate=cost(rows, depth, 2 * width),
    )(x, gate_weight, up_weight)


def down_body(owners, members, pieces, ranks, rank_ref, *refs):
    hidden_refs = refs[: owners * pieces]
    weight_ref = refs[owners * pieces]
    out_refs = refs[owners * pieces + 1 : -2]
    lhs_ref, acc_ref = refs[-2:]
    q = hidden_refs[0].shape[0] // members
    part = hidden_refs[0].shape[1]
    block = acc_ref.shape[0] // ranks

    @pl.when(pl.program_id(0) == 0)
    def _():
        for owner in range(owners):
            for piece in range(pieces):
                for member in range(members):
                    row = (member * owners + owner) * q
                    lhs_ref[row : row + q, piece * part : (piece + 1) * part] = hidden_refs[
                        owner * pieces + piece
                    ][member * q : (member + 1) * q]

    acc_ref[...] = jnp.dot(lhs_ref[...], weight_ref[0], preferred_element_type=F32)
    for hop in range(ranks):
        at = lax.rem(rank_ref[0] + hop, ranks) * block
        taken = acc_ref[pl.ds(pl.multiple_of(at, block), block), :]
        out_refs[hop][...] = taken.astype(out_refs[hop].dtype)


def down(rank, hidden, down_weight, members, ranks):
    owners, pieces = len(hidden), len(hidden[0])
    rows_each, part = hidden[0][0].shape
    rows, depth, width = owners * rows_each, pieces * part, down_weight.shape[2]
    tile = tile_of(width, 256)
    block = rows // ranks
    out_spec = pl.BlockSpec((block, tile), lambda j, *_: (0, j))
    return pl.pallas_call(
        functools.partial(down_body, owners, members, pieces, ranks),
        grid_spec=pltpu.PrefetchScalarGridSpec(
            num_scalar_prefetch=1,
            grid=(width // tile,),
            in_specs=[whole((rows_each, part))] * (owners * pieces)
            + [pl.BlockSpec((1, depth, tile), lambda j, *_: (0, 0, j))],
            out_specs=[out_spec] * ranks,
            scratch_shapes=[pltpu.VMEM((rows, depth), BF16), pltpu.VMEM((rows, tile), F32)],
        ),
        out_shape=[jax.ShapeDtypeStruct((block, width), F32)]
        + [jax.ShapeDtypeStruct((block, width), BF16)] * (ranks - 1),
        compiler_params=params(),
        cost_estimate=cost(rows, depth, width),
    )(rank, *[piece for of_owner in hidden for piece in of_owner], down_weight)


def encode_body(members, ranks, rank_ref, *refs):
    block_refs = refs[:ranks]
    weight_ref = refs[ranks]
    out_refs = refs[ranks + 1 : -1]
    lhs_ref = refs[-1]
    block = block_refs[0].shape[0]

    @pl.when(pl.program_id(0) == 0)
    def _():
        for hop in range(ranks):
            at = lax.rem(rank_ref[0] + hop, ranks) * block
            lhs_ref[pl.ds(pl.multiple_of(at, block), block), :] = block_refs[hop][...]

    pre = jnp.dot(lhs_ref[...], weight_ref[0], preferred_element_type=F32)
    rows = pre.shape[0] // members
    for member in range(members):
        taken = pre[member * rows : (member + 1) * rows]
        out_refs[member][...] = taken.astype(out_refs[member].dtype)


def encode(rank, blocks, enc_weight, members):
    ranks = len(blocks)
    block, depth = blocks[0].shape
    width = enc_weight.shape[2]
    rows = block * ranks
    rows_each = rows // members
    tile = tile_of(width, 512)
    out_spec = pl.BlockSpec((rows_each, tile), lambda j, *_: (0, j))
    return pl.pallas_call(
        functools.partial(encode_body, members, ranks),
        grid_spec=pltpu.PrefetchScalarGridSpec(
            num_scalar_prefetch=1,
            grid=(width // tile,),
            in_specs=[whole((block, depth))] * ranks
            + [pl.BlockSpec((1, depth, tile), lambda j, *_: (0, 0, j))],
            out_specs=[out_spec] * members,
            scratch_shapes=[pltpu.VMEM((rows, depth), BF16)],
        ),
        out_shape=[jax.ShapeDtypeStruct((rows_each, width), F32)] * members,
        compiler_params=params(),
        cost_estimate=cost(rows, depth, width),
    )(rank, *blocks, enc_weight)


def on_device(
    owners, members, ranks, tokens, norm_gain, gate_weight, up_weight, down_weight, enc_weight,
    enc_bias, adjoint,
):
    row_at = lax.axis_index("rows")
    member_at = lax.axis_index("mp")
    rank_at = lax.axis_index("hid")
    rank = rank_at.astype(jnp.int32).reshape(1)
    per_device = adjoint.shape[0]
    cut = tokens.shape[1]
    half_cuts = ranks // owners
    model_width = cut * ranks

    tokens_float = tokens.astype(F32)
    local_squares = jnp.sum(tokens_float * tokens_float, axis=1)
    squares = local_squares
    for hop in range(1, ranks):
        squares = squares + shift(local_squares, "hid", ranks, hop)
    inverse = lax.rsqrt(squares / model_width + 1e-05).reshape(members, per_device)
    inverses = [inverse] + [shift(inverse, "rows", owners, hop) for hop in range(1, owners)]
    inverses = jnp.stack(inverses)
    turned = jnp.concatenate((inverses, inverses), axis=1)
    inverses = lax.dynamic_slice_in_dim(turned, member_at, members, 1)
    gain = lax.dynamic_slice_in_dim(
        norm_gain[0], row_at * (model_width // owners), model_width // owners, 0
    )

    own_tokens = lax.dynamic_slice_in_dim(tokens, member_at * per_device, per_device, 0)

    chunks = max(1, 16 // ranks)
    pieces = 1
    q = per_device // chunks

    def normed_rows(start, q):
        mine = own_tokens[start : start + q]
        gathered = jnp.zeros((ranks, q, cut), BF16)
        gathered = lax.dynamic_update_slice(gathered, mine[None], (rank_at, 0, 0))
        for hop in range(1, ranks):
            there = lax.rem(rank_at + hop, ranks)
            gathered = lax.dynamic_update_slice(
                gathered, shift(mine, "hid", ranks, hop)[None], (there, 0, 0)
            )
        columns = []
        for hop in range(owners):
            target = lax.rem(row_at + owners - hop, owners)
            half = lax.dynamic_slice_in_dim(gathered, target * half_cuts, half_cuts, 0)
            columns.append(half if hop == 0 else shift(half, "rows", owners, hop))
        columns = jnp.stack(columns)
        columns = [columns] + [shift(columns, "mp", members, hop) for hop in range(1, members)]
        columns = jnp.stack(columns, axis=1).astype(F32)
        scale = inverses[:, :, None, start : start + q, None]
        normed = (columns * scale * gain.reshape(half_cuts, 1, cut)).astype(BF16)
        return normed.transpose(0, 1, 3, 2, 4).reshape(owners * members * q, half_cuts * cut)

    def layer(x):
        hidden = [[] for _ in range(owners)]
        for piece in range(pieces):
            own, *sends = gate_up(x, gate_weight, up_weight, owners, piece, pieces)
            acts = own
            for hop in range(1, owners):
                acts = acts + send(sends[hop - 1], "rows", owners, hop).astype(F32)
            mine = (jax.nn.silu(acts[0]) * acts[1]).astype(BF16)
            hidden[0].append(mine)
            for hop in range(1, owners):
                hidden[hop].append(shift(mine, "rows", owners, hop))
        own, *sends = down(rank, hidden, down_weight, members, ranks)
        total = own
        for hop in range(1, ranks):
            total = total + send(sends[hop - 1], "hid", ranks, hop).astype(F32)
        block = total.astype(BF16)
        return [block] + [shift(block, "hid", ranks, hop) for hop in range(1, ranks)]

    def features(blocks, start, q):
        own, *sends = encode(rank, blocks, enc_weight, members)
        total = own
        for hop in range(1, members):
            total = total + send(sends[hop - 1], "mp", members, hop)
        pre = total[:q]
        for hop in range(1, owners):
            going = total[hop * q : (hop + 1) * q].astype(BF16)
            pre = pre + send(going, "rows", owners, hop).astype(F32)
        pre = pre + enc_bias[None, :]
        factor = adjoint[start : start + q].astype(F32)
        return (jnp.maximum(pre, 0.0) * factor).astype(BF16)

    outs = []
    for chunk in range(chunks):
        x = normed_rows(chunk * q, q)
        blocks = layer(x)
        outs.append(features(blocks, chunk * q, q))
    return jnp.concatenate(outs, axis=0)


def solution(mesh):
    placed = (
        P(("groups", "rows"), "hid"),
        P("mp", None),
        P("mp", "rows", "hid"),
        P("mp", "rows", "hid"),
        P("mp", "hid", "rows"),
        P("mp", "rows", "hid"),
        P("hid"),
        P(("groups", "rows", "mp"), "hid"),
    )
    sizes = (mesh.shape["rows"], mesh.shape["mp"], mesh.shape["hid"])
    return jax.shard_map(
        functools.partial(on_device, *sizes),
        mesh=mesh,
        in_specs=placed,
        out_specs=P(("groups", "rows", "mp"), "hid"),
        check_vma=False,
    )
```

```python
import functools

import jax
import jax.numpy as jnp
from jax import lax
from jax.experimental import pallas as pl
from jax.experimental.pallas import tpu as pltpu
from jax.sharding import PartitionSpec as P

BF16 = jnp.bfloat16
F32 = jnp.float32
VMEM_BYTES = 28 * 1024 * 1024
BUFFERS = 4


def shift(value, axis, size, hop):
    return lax.ppermute(value, axis, [((d + hop) % size, d) for d in range(size)])


def send(value, axis, size, hop):
    return lax.ppermute(value, axis, [(d, (d + hop) % size) for d in range(size)])


def tile_of(width, most):
    tile = most
    while tile > 128 and width % tile:
        tile //= 2
    return tile if width % tile == 0 else width


def whole(shape):
    return pl.BlockSpec(shape, lambda j, *_: (0,) * len(shape))


def slots_of(tiles):
    return min(BUFFERS, tiles)


def slots(depth, tile, tiles):
    count = slots_of(tiles)
    return [pltpu.VMEM((count, depth, tile), BF16), pltpu.SemaphoreType.DMA((count,))]


def next_block(weight_ref, slot_ref, slot_sems, tiles, first=0):
    step = pl.program_id(0)
    count, _, tile = slot_ref.shape

    def copy(block, slot):
        columns = pl.ds(pl.multiple_of((first + block) * tile, 128), tile)
        return pltpu.make_async_copy(
            weight_ref.at[0, :, columns], slot_ref.at[slot], slot_sems.at[slot]
        )

    @pl.when(step == 0)
    def _():
        for block in range(count - 1):
            copy(block, block).start()

    ahead = step + count - 1

    @pl.when(ahead < tiles)
    def _():
        copy(ahead, lax.rem(ahead, count)).start()

    slot = lax.rem(step, count)
    copy(step, slot).wait()
    return slot_ref.at[slot]


def in_place(count):
    return [pl.BlockSpec(memory_space=pl.ANY)] * count


def params():
    return pltpu.CompilerParams(
        dimension_semantics=("arbitrary",), vmem_limit_bytes=VMEM_BYTES
    )


def cost(rows, depth, width):
    return pl.CostEstimate(
        flops=2 * rows * depth * width,
        bytes_accessed=2 * (rows * depth + depth * width + rows * width),
        transcendentals=0,
    )


def gate_up_body(owners, tiles, first, x_ref, gate_ref, up_ref, *refs):
    out_refs = refs[-4 - owners : -4]
    rows = x_ref.shape[0] // owners
    blocks = [
        next_block(gate_ref, refs[-4], refs[-3], tiles, first),
        next_block(up_ref, refs[-2], refs[-1], tiles, first),
    ]
    x = x_ref[...]
    for at, block_ref in enumerate(blocks):
        acts = jnp.dot(x, block_ref[...], preferred_element_type=F32)
        for hop in range(owners):
            taken = acts[hop * rows : (hop + 1) * rows]
            out_refs[hop][at] = taken.astype(out_refs[hop].dtype)


def gate_up(x, gate_weight, up_weight, owners, piece, pieces, after):
    rows, depth = x.shape
    width = gate_weight.shape[2] // pieces
    tile = tile_of(width, 256)
    tiles = width // tile
    own_rows = rows // owners
    return pl.pallas_call(
        functools.partial(gate_up_body, owners, tiles, piece * tiles),
        grid=(tiles,),
        in_specs=[whole((rows, depth))] + in_place(2 + len(after)),
        out_specs=[pl.BlockSpec((2, own_rows, tile), lambda j: (0, 0, j))] * owners,
        out_shape=[jax.ShapeDtypeStruct((2, own_rows, width), F32)]
        + [jax.ShapeDtypeStruct((2, own_rows, width), BF16)] * (owners - 1),
        scratch_shapes=slots(depth, tile, tiles) * 2,
        compiler_params=params(),
        cost_estimate=cost(rows, depth, 2 * width),
    )(x, gate_weight, up_weight, *after)


def down_body(owners, members, pieces, ranks, tiles, rank_ref, *refs):
    hidden_refs = refs[: owners * pieces]
    weight_ref = refs[owners * pieces]
    out_refs = refs[-4 - ranks : -4]
    lhs_ref, acc_ref, slot_ref, slot_sems = refs[-4:]
    block_ref = next_block(weight_ref, slot_ref, slot_sems, tiles)
    q = hidden_refs[0].shape[0] // members
    part = hidden_refs[0].shape[1]
    block = acc_ref.shape[0] // ranks

    @pl.when(pl.program_id(0) == 0)
    def _():
        for owner in range(owners):
            for piece in range(pieces):
                for member in range(members):
                    row = (member * owners + owner) * q
                    lhs_ref[row : row + q, piece * part : (piece + 1) * part] = hidden_refs[
                        owner * pieces + piece
                    ][member * q : (member + 1) * q]

    acc_ref[...] = jnp.dot(lhs_ref[...], block_ref[...], preferred_element_type=F32)
    for hop in range(ranks):
        at = lax.rem(rank_ref[0] + hop, ranks) * block
        taken = acc_ref[pl.ds(pl.multiple_of(at, block), block), :]
        out_refs[hop][...] = taken.astype(out_refs[hop].dtype)


def down(rank, hidden, down_weight, members, ranks, after):
    owners, pieces = len(hidden), len(hidden[0])
    rows_each, part = hidden[0][0].shape
    rows, depth, width = owners * rows_each, pieces * part, down_weight.shape[2]
    tile = tile_of(width, 256)
    block = rows // ranks
    return pl.pallas_call(
        functools.partial(down_body, owners, members, pieces, ranks, width // tile),
        grid_spec=pltpu.PrefetchScalarGridSpec(
            num_scalar_prefetch=1,
            grid=(width // tile,),
            in_specs=[whole((rows_each, part))] * (owners * pieces)
            + in_place(1 + len(after)),
            out_specs=[pl.BlockSpec((block, tile), lambda j, *_: (0, j))] * ranks,
            scratch_shapes=[pltpu.VMEM((rows, depth), BF16), pltpu.VMEM((rows, tile), F32)]
            + slots(depth, tile, width // tile),
        ),
        out_shape=[jax.ShapeDtypeStruct((block, width), F32)]
        + [jax.ShapeDtypeStruct((block, width), BF16)] * (ranks - 1),
        compiler_params=params(),
        cost_estimate=cost(rows, depth, width),
    )(rank, *[piece for of_owner in hidden for piece in of_owner], down_weight, *after)


def encode_body(members, ranks, tiles, rank_ref, *refs):
    block_refs = refs[:ranks]
    weight_ref = refs[ranks]
    out_refs = refs[-3 - members : -3]
    lhs_ref, slot_ref, slot_sems = refs[-3:]
    weight_block = next_block(weight_ref, slot_ref, slot_sems, tiles)
    block = block_refs[0].shape[0]

    @pl.when(pl.program_id(0) == 0)
    def _():
        for hop in range(ranks):
            at = lax.rem(rank_ref[0] + hop, ranks) * block
            lhs_ref[pl.ds(pl.multiple_of(at, block), block), :] = block_refs[hop][...]

    pre = jnp.dot(lhs_ref[...], weight_block[...], preferred_element_type=F32)
    rows = pre.shape[0] // members
    for member in range(members):
        taken = pre[member * rows : (member + 1) * rows]
        out_refs[member][...] = taken.astype(out_refs[member].dtype)


def encode(rank, blocks, enc_weight, members, after):
    ranks = len(blocks)
    block, depth = blocks[0].shape
    width = enc_weight.shape[2]
    rows = block * ranks
    rows_each = rows // members
    tile = tile_of(width, 512)
    return pl.pallas_call(
        functools.partial(encode_body, members, ranks, width // tile),
        grid_spec=pltpu.PrefetchScalarGridSpec(
            num_scalar_prefetch=1,
            grid=(width // tile,),
            in_specs=[whole((block, depth))] * ranks
            + in_place(1 + len(after)),
            out_specs=[pl.BlockSpec((rows_each, tile), lambda j, *_: (0, j))] * members,
            scratch_shapes=[pltpu.VMEM((rows, depth), BF16)] + slots(depth, tile, width // tile),
        ),
        out_shape=[jax.ShapeDtypeStruct((rows_each, width), F32)]
        + [jax.ShapeDtypeStruct((rows_each, width), BF16)] * (members - 1),
        compiler_params=params(),
        cost_estimate=cost(rows, depth, width),
    )(rank, *blocks, enc_weight, *after)


def chunk_rows(total, unit):
    units = total // unit
    if units < 8:
        return [total]
    eighth = units // 8
    sizes = [2 * eighth, 3 * eighth, 2 * eighth]
    return [size * unit for size in sizes + [units - sum(sizes)]]


def on_device(
    owners, members, ranks, tokens, norm_gain, gate_weight, up_weight, down_weight, enc_weight,
    enc_bias, adjoint,
):
    row_at = lax.axis_index("rows")
    member_at = lax.axis_index("mp")
    rank_at = lax.axis_index("hid")
    rank = rank_at.astype(jnp.int32).reshape(1)
    per_device = adjoint.shape[0]
    cut = tokens.shape[1]
    half_cuts = ranks // owners
    model_width = cut * ranks

    gain = lax.dynamic_slice_in_dim(
        norm_gain[0], row_at * (model_width // owners), model_width // owners, 0
    ).reshape(half_cuts, 1, cut)
    own_tokens = lax.dynamic_slice_in_dim(tokens, member_at * per_device, per_device, 0)

    def from_all(value, axis, size):
        return jnp.stack([value] + [shift(value, axis, size, hop) for hop in range(1, size)])

    def normed_rows(gathered, first, q):
        wide = gathered.astype(F32)
        squares = jnp.sum(wide * wide, axis=(0, 2))
        inverse = lax.rsqrt(squares / model_width + 1e-05)
        doubled = jnp.concatenate((gathered, gathered))
        columns = []
        for hop in range(owners):
            target = lax.rem(row_at + owners - hop, owners)
            start = lax.rem(target * half_cuts + ranks - first, ranks)
            half = lax.dynamic_slice_in_dim(doubled, start, half_cuts, 0)
            columns.append(half if hop == 0 else shift(half, "rows", owners, hop))
        inverses = from_all(from_all(inverse, "rows", owners), "mp", members)
        columns = from_all(jnp.stack(columns), "mp", members)
        return columns, inverses

    def normed(columns, inverses):
        scaled = columns.astype(F32) * inverses[:, :, None, :, None] * gain
        ordered = scaled.astype(BF16).transpose(1, 0, 3, 2, 4)
        return ordered.reshape(-1, half_cuts * cut)

    sizes = chunk_rows(per_device, 16 * max(1, ranks // (owners * members)))
    starts = [sum(sizes[:at]) for at in range(len(sizes))]
    chunks = len(sizes)
    head = sizes[0]

    xs = []
    first_columns, first_inverses = normed_rows(
        from_all(own_tokens[:head], "hid", ranks), rank_at, head
    )
    xs.append(normed(first_columns, first_inverses))
    if chunks > 1:
        rest = lax.all_gather(own_tokens[head:], "hid", axis=0)
        rest_columns, rest_inverses = normed_rows(rest, 0, per_device - head)
        for start, q in zip(starts[1:], sizes[1:]):
            rows = slice(start - head, start - head + q)
            xs.append(normed(rest_columns[:, :, :, rows], rest_inverses[:, :, rows]))

    sums, mine, hidden, layer, blocks, outs = ({} for _ in range(6))
    last = []

    def gate_up_of(t):
        pieces = 2 if t == 0 and gate_weight.shape[2] % 512 == 0 else 1
        sums[t] = []
        for piece in range(pieces):
            own, *sends = gate_up(
                xs[t], gate_weight, up_weight, owners, piece, pieces, list(last)
            )
            last[:] = [own]
            others = [send(sends[hop - 1], "rows", owners, hop) for hop in range(1, owners)]
            sums[t].append((own, others))

    def hidden_of(t):
        hidden[t] = [[] for _ in range(owners)]
        for own, others in sums[t]:
            acts = own
            for other in others:
                acts = acts + other.astype(F32)
            units = (jax.nn.silu(acts[0]) * acts[1]).astype(BF16)
            hidden[t][0].append(units)
            for hop in range(1, owners):
                hidden[t][hop].append(shift(units, "rows", owners, hop))
        last[:] = [hidden[t][0][-1]]

    def down_of(t):
        own, *sends = down(rank, hidden[t], down_weight, members, ranks, list(last))
        last[:] = [own]
        layer[t] = (own, [send(sends[hop - 1], "hid", ranks, hop) for hop in range(1, ranks)])

    def blocks_of(t):
        total, others = layer[t]
        for other in others:
            total = total + other.astype(F32)
        block = total.astype(BF16)
        blocks[t] = [block] + [shift(block, "hid", ranks, hop) for hop in range(1, ranks)]
        last[:] = [block]

    def features_of(t):
        own, *sends = encode(rank, blocks[t], enc_weight, members, list(last))
        last[:] = [own]
        start, q = starts[t], sizes[t]
        total = own
        for hop in range(1, members):
            total = total + send(sends[hop - 1], "mp", members, hop).astype(F32)
        pre = total[:q]
        for hop in range(1, owners):
            going = total[hop * q : (hop + 1) * q].astype(BF16)
            pre = pre + send(going, "rows", owners, hop).astype(F32)
        pre = pre + enc_bias[None, :]
        factor = adjoint[start : start + q].astype(F32)
        outs[t] = (jnp.maximum(pre, 0.0) * factor).astype(BF16)

    gate_up_of(0)
    if chunks > 1:
        gate_up_of(1)
    for step in range(chunks + 3):
        for stage, ahead in (
            (hidden_of, 0), (gate_up_of, 2), (down_of, -1), (blocks_of, -2), (features_of, -3)
        ):
            if 0 <= step + ahead < chunks:
                stage(step + ahead)
    return jnp.concatenate([outs[t] for t in range(chunks)], axis=0)


def solution(mesh):
    placed = (
        P(("groups", "rows"), "hid"),
        P("mp", None),
        P("mp", "rows", "hid"),
        P("mp", "rows", "hid"),
        P("mp", "hid", "rows"),
        P("mp", "rows", "hid"),
        P("hid"),
        P(("groups", "rows", "mp"), "hid"),
    )
    sizes = (mesh.shape["rows"], mesh.shape["mp"], mesh.shape["hid"])
    return jax.shard_map(
        functools.partial(on_device, *sizes),
        mesh=mesh,
        in_specs=placed,
        out_specs=P(("groups", "rows", "mp"), "hid"),
        check_vma=False,
    )
```

```python
import functools

import jax
import jax.numpy as jnp
from jax import lax
from jax.experimental import pallas as pl
from jax.experimental.pallas import tpu as pltpu
from jax.sharding import PartitionSpec as P

BF16 = jnp.bfloat16
F32 = jnp.float32
VMEM_BYTES = 52 * 1024 * 1024
BUFFERS = 4


def shift(value, axis, size, hop):
    return lax.ppermute(value, axis, [((d + hop) % size, d) for d in range(size)])


def send(value, axis, size, hop):
    return lax.ppermute(value, axis, [(d, (d + hop) % size) for d in range(size)])


def swap(value, axis, size, bit):
    return lax.ppermute(value, axis, [(d, d ^ bit) for d in range(size)])


def doubling(size):
    bits = [1 << at for at in reversed(range(size.bit_length() - 1))]
    order = [0]
    for bit in bits:
        order = order + [offset ^ bit for offset in order]
    return bits, order


def tile_of(width, most):
    tile = most
    while tile > 128 and width % tile:
        tile //= 2
    return tile if width % tile == 0 else width


def whole(shape):
    return pl.BlockSpec(shape, lambda j, *_: (0,) * len(shape))


def slots_of(tiles):
    return min(BUFFERS, tiles)


def slots(depth, tile, tiles):
    count = slots_of(tiles)
    return [pltpu.VMEM((count, depth, tile), BF16), pltpu.SemaphoreType.DMA((count,))]


def next_block(weight_ref, slot_ref, slot_sems, tiles, first=0):
    step = pl.program_id(0)
    count, _, tile = slot_ref.shape

    def copy(block, slot):
        columns = pl.ds(pl.multiple_of((first + block) * tile, 128), tile)
        return pltpu.make_async_copy(
            weight_ref.at[0, :, columns], slot_ref.at[slot], slot_sems.at[slot]
        )

    @pl.when(step == 0)
    def _():
        for block in range(count - 1):
            copy(block, block).start()

    ahead = step + count - 1

    @pl.when(ahead < tiles)
    def _():
        copy(ahead, lax.rem(ahead, count)).start()

    slot = lax.rem(step, count)
    copy(step, slot).wait()
    return slot_ref.at[slot]


def in_hbm(count):
    return [pl.BlockSpec(memory_space=pltpu.HBM)] * count


def unread(after):
    return [pl.BlockSpec(memory_space=pl.ANY)] * len(after)


def params():
    return pltpu.CompilerParams(
        dimension_semantics=("arbitrary",), vmem_limit_bytes=VMEM_BYTES
    )


def cost(rows, depth, width):
    return pl.CostEstimate(
        flops=2 * rows * depth * width,
        bytes_accessed=2 * (rows * depth + depth * width + rows * width),
        transcendentals=0,
    )


def gate_up_body(tiles, first, x_ref, gate_ref, up_ref, *refs):
    members, owners, cuts, q, cut = x_ref.shape
    out_refs = refs[-5 - owners : -5]
    lhs_ref = refs[-5]
    blocks = [
        next_block(gate_ref, refs[-4], refs[-3], tiles, first),
        next_block(up_ref, refs[-2], refs[-1], tiles, first),
    ]

    @pl.when(pl.program_id(0) == 0)
    def _():
        for owner in range(owners):
            for member in range(members):
                row = (owner * members + member) * q
                for at in range(cuts):
                    lhs_ref[row : row + q, at * cut : (at + 1) * cut] = x_ref[member, owner, at]

    rows = members * q
    for at, block_ref in enumerate(blocks):
        acts = jnp.dot(lhs_ref[...], block_ref[...], preferred_element_type=F32)
        for hop in range(owners):
            taken = acts[hop * rows : (hop + 1) * rows]
            out_refs[hop][at] = taken.astype(out_refs[hop].dtype)


def gate_up(x, gate_weight, up_weight, piece, pieces, after):
    members, owners, cuts, q, cut = x.shape
    rows, depth, own_rows = members * owners * q, cuts * cut, members * q
    width = gate_weight.shape[2] // pieces
    tile = tile_of(width, 256)
    tiles = width // tile
    return pl.pallas_call(
        functools.partial(gate_up_body, tiles, piece * tiles),
        grid=(tiles,),
        in_specs=[whole(x.shape)] + in_hbm(2) + unread(after),
        out_specs=[pl.BlockSpec((2, own_rows, tile), lambda j: (0, 0, j))] * owners,
        out_shape=[jax.ShapeDtypeStruct((2, own_rows, width), F32)]
        + [jax.ShapeDtypeStruct((2, own_rows, width), BF16)] * (owners - 1),
        scratch_shapes=[pltpu.VMEM((rows, depth), BF16)] + slots(depth, tile, tiles) * 2,
        compiler_params=params(),
        cost_estimate=cost(rows, depth, 2 * width),
    )(x, gate_weight, up_weight, *after)


def down_body(owners, members, pieces, order, tiles, rank_ref, *refs):
    hidden_refs = refs[: owners * pieces]
    weight_ref = refs[owners * pieces]
    out_refs = refs[-6:-4]
    lhs_ref, acc_ref, slot_ref, slot_sems = refs[-4:]
    block_ref = next_block(weight_ref, slot_ref, slot_sems, tiles)
    q = hidden_refs[0].shape[0] // members
    part = hidden_refs[0].shape[1]
    block = acc_ref.shape[0] // len(order)

    @pl.when(pl.program_id(0) == 0)
    def _():
        for owner in range(owners):
            for piece in range(pieces):
                for member in range(members):
                    row = (member * owners + owner) * q
                    lhs_ref[row : row + q, piece * part : (piece + 1) * part] = hidden_refs[
                        owner * pieces + piece
                    ][member * q : (member + 1) * q]

    acc_ref[...] = jnp.dot(lhs_ref[...], block_ref[...], preferred_element_type=F32)
    half = len(order) // 2
    for slot, offset in enumerate(order):
        at = (rank_ref[0] ^ offset) * block
        taken = acc_ref[pl.ds(pl.multiple_of(at, block), block), :]
        out_ref = out_refs[slot // half]
        row = (slot % half) * block
        out_ref[row : row + block] = taken.astype(out_ref.dtype)


def down(rank, hidden, down_weight, members, order, after):
    owners, pieces = len(hidden), len(hidden[0])
    rows_each, part = hidden[0][0].shape
    rows, depth, width = owners * rows_each, pieces * part, down_weight.shape[2]
    tile = tile_of(width, 256)
    return pl.pallas_call(
        functools.partial(down_body, owners, members, pieces, order, width // tile),
        grid_spec=pltpu.PrefetchScalarGridSpec(
            num_scalar_prefetch=1,
            grid=(width // tile,),
            in_specs=[whole((rows_each, part))] * (owners * pieces)
            + in_hbm(1)
            + unread(after),
            out_specs=[pl.BlockSpec((rows // 2, tile), lambda j, *_: (0, j))] * 2,
            scratch_shapes=[pltpu.VMEM((rows, depth), BF16), pltpu.VMEM((rows, tile), F32)]
            + slots(depth, tile, width // tile),
        ),
        out_shape=[jax.ShapeDtypeStruct((rows // 2, width), kind) for kind in (F32, BF16)],
        compiler_params=params(),
        cost_estimate=cost(rows, depth, width),
    )(rank, *[piece for of_owner in hidden for piece in of_owner], down_weight, *after)


def encode_body(members, order, tiles, rank_ref, near_ref, far_ref, weight_ref, *refs):
    out_refs = refs[-3 - members : -3]
    lhs_ref, slot_ref, slot_sems = refs[-3:]
    weight_block = next_block(weight_ref, slot_ref, slot_sems, tiles)
    block = lhs_ref.shape[0] // len(order)
    half = len(order) // 2

    @pl.when(pl.program_id(0) == 0)
    def _():
        for slot, offset in enumerate(order):
            at = (rank_ref[0] ^ offset) * block
            row = (slot % half) * block
            from_ref = far_ref if slot >= half else near_ref
            lhs_ref[pl.ds(pl.multiple_of(at, block), block), :] = from_ref[row : row + block]

    pre = jnp.dot(lhs_ref[...], weight_block[...], preferred_element_type=F32)
    rows = pre.shape[0] // members
    for member in range(members):
        taken = pre[member * rows : (member + 1) * rows]
        out_refs[member][...] = taken.astype(out_refs[member].dtype)


def encode(rank, near, far, enc_weight, members, order, after):
    rows, depth = 2 * near.shape[0], near.shape[1]
    width = enc_weight.shape[2]
    rows_each = rows // members
    tile = tile_of(width, 512)
    return pl.pallas_call(
        functools.partial(encode_body, members, order, width // tile),
        grid_spec=pltpu.PrefetchScalarGridSpec(
            num_scalar_prefetch=1,
            grid=(width // tile,),
            in_specs=[whole(near.shape)] * 2 + in_hbm(1) + unread(after),
            out_specs=[pl.BlockSpec((rows_each, tile), lambda j, *_: (0, j))] * members,
            scratch_shapes=[pltpu.VMEM((rows, depth), BF16)] + slots(depth, tile, width // tile),
        ),
        out_shape=[jax.ShapeDtypeStruct((rows_each, width), F32)]
        + [jax.ShapeDtypeStruct((rows_each, width), BF16)] * (members - 1),
        compiler_params=params(),
        cost_estimate=cost(rows, depth, width),
    )(rank, near, far, enc_weight, *after)


def chunk_rows(total, unit):
    units = total // unit
    if units < 8:
        return [total]
    eighth = units // 8
    sizes = [2 * eighth, 3 * eighth, 2 * eighth]
    return [size * unit for size in sizes + [units - sum(sizes)]]


def on_device(
    owners, members, ranks, tokens, norm_gain, gate_weight, up_weight, down_weight, enc_weight,
    enc_bias, adjoint,
):
    row_at = lax.axis_index("rows")
    member_at = lax.axis_index("mp")
    rank_at = lax.axis_index("hid")
    rank = rank_at.astype(jnp.int32).reshape(1)
    per_device = adjoint.shape[0]
    cut = tokens.shape[1]
    half_cuts = ranks // owners
    model_width = cut * ranks

    gain = lax.dynamic_slice_in_dim(
        norm_gain[0], row_at * (model_width // owners), model_width // owners, 0
    ).reshape(half_cuts, 1, cut)
    own_tokens = lax.dynamic_slice_in_dim(tokens, member_at * per_device, per_device, 0)

    bits, order = doubling(ranks)

    def from_all(value, axis, size):
        return jnp.stack([value] + [shift(value, axis, size, hop) for hop in range(1, size)])

    def place_of(offset):
        place = 0
        for at in range(len(bits)):
            place = place + ((offset >> at) & 1) * bits[at]
        return place

    def gathered_rows(mine, after=None):
        gathered = mine[None]
        for bit in bits:
            gathered = jnp.concatenate((gathered, swap(gathered, "hid", ranks, bit)))
        if after is not None:
            gathered, _ = lax.optimization_barrier((gathered, after))
        wide = gathered.astype(F32)
        squares = jnp.sum(wide * wide, axis=(0, 2))
        inverse = lax.rsqrt(squares / model_width + 1e-05)
        columns = []
        for hop in range(owners):
            target = lax.rem(row_at + owners - hop, owners)
            half = jnp.concatenate(
                [
                    lax.dynamic_slice_in_dim(
                        gathered, place_of(rank_at ^ (target * half_cuts + at)), 1, 0
                    )
                    for at in range(half_cuts)
                ]
            )
            columns.append(half if hop == 0 else shift(half, "rows", owners, hop))
        inverses = from_all(from_all(inverse, "rows", owners), "mp", members)
        return from_all(jnp.stack(columns), "mp", members), inverses

    def normed(columns, inverses):
        return (columns.astype(F32) * inverses[:, :, None, :, None] * gain).astype(BF16)

    sizes = chunk_rows(per_device, 16 * max(1, ranks // (owners * members)))
    starts = [sum(sizes[:at]) for at in range(len(sizes))]
    chunks = len(sizes)
    head = sizes[0]

    xs = [normed(*gathered_rows(own_tokens[:head]))]
    if chunks > 1:
        columns, inverses = gathered_rows(own_tokens[head:], xs[0])
        for start, q in zip(starts[1:], sizes[1:]):
            rows = slice(start - head, start - head + q)
            xs.append(normed(columns[:, :, :, rows], inverses[:, :, rows]))

    sums, hidden, layer, blocks, outs = ({} for _ in range(5))
    last = []

    def gate_up_of(t):
        pieces = 2 if t == 0 and gate_weight.shape[2] % 512 == 0 else 1
        sums[t] = []
        for piece in range(pieces):
            own, *sends = gate_up(
                xs[t], gate_weight, up_weight, piece, pieces, list(last)
            )
            last[:] = [own]
            others = [send(sends[hop - 1], "rows", owners, hop) for hop in range(1, owners)]
            sums[t].append((own, others))

    def hidden_of(t):
        hidden[t] = [[] for _ in range(owners)]
        for own, others in sums[t]:
            acts = own
            for other in others:
                acts = acts + other.astype(F32)
            units = (jax.nn.silu(acts[0]) * acts[1]).astype(BF16)
            hidden[t][0].append(units)
            for hop in range(1, owners):
                hidden[t][hop].append(shift(units, "rows", owners, hop))
        last.append(hidden[t][0][-1])

    def down_of(t):
        total, going = down(rank, hidden[t], down_weight, members, order, list(last))
        last[:] = [total]
        layer[t] = (total, swap(going, "hid", ranks, 1))

    def halve_of(t):
        total, arrived = layer[t]
        for bit in reversed(bits[:-1]):
            total = total + arrived.astype(F32)
            kept = total.shape[0] // 2
            going = total[kept:].astype(BF16)
            last.append(going)
            total, arrived = total[:kept], swap(going, "hid", ranks, bit)
        layer[t] = (total, arrived)

    def settle_of(t):
        total, arrived = layer[t]
        block = (total + arrived.astype(F32)).astype(BF16)
        last.append(block)
        layer[t] = (block, swap(block, "hid", ranks, bits[0]))

    def double_of(t):
        near, far = layer[t]
        for bit in bits[1:]:
            near = jnp.concatenate((near, far))
            last.append(near)
            far = swap(near, "hid", ranks, bit)
        blocks[t] = (near, far)

    def features_of(t):
        own, *sends = encode(rank, *blocks[t], enc_weight, members, order, list(last))
        last[:] = [own]
        sums[t] = (own, [send(sends[hop - 1], "mp", members, hop) for hop in range(1, members)])

    def share_of(t):
        total, others = sums[t]
        for other in others:
            total = total + other.astype(F32)
        start, q = starts[t], sizes[t]
        pre = total[:q]
        for hop in range(1, owners):
            going = total[hop * q : (hop + 1) * q].astype(BF16)
            last.append(going)
            pre = pre + send(going, "rows", owners, hop).astype(F32)
        pre = pre + enc_bias[None, :]
        factor = adjoint[start : start + q].astype(F32)
        outs[t] = (jnp.maximum(pre, 0.0) * factor).astype(BF16)

    end = chunks
    stages = [(gate_up_of, 0), (gate_up_of, 1)]
    for step in range(end):
        stages += [
            (hidden_of, step), (gate_up_of, step + 2), (double_of, step - 3), (halve_of, step - 2),
            (down_of, step - 1), (settle_of, step - 2),
        ]
    stages += [(double_of, end - 3), (down_of, end - 1), (halve_of, end - 2)]
    for t in range(end - 3):
        stages += [(features_of, t), (share_of, t)]
    stages += [
        (settle_of, end - 2), (halve_of, end - 1), (features_of, end - 3),
        (share_of, end - 3), (double_of, end - 2), (settle_of, end - 1), (features_of, end - 2),
        (share_of, end - 2), (double_of, end - 1), (features_of, end - 1), (share_of, end - 1),
    ]
    for stage, t in stages:
        if 0 <= t < chunks:
            stage(t)
    return jnp.concatenate([outs[t] for t in range(chunks)], axis=0)


def solution(mesh):
    placed = (
        P(("groups", "rows"), "hid"),
        P("mp", None),
        P("mp", "rows", "hid"),
        P("mp", "rows", "hid"),
        P("mp", "hid", "rows"),
        P("mp", "rows", "hid"),
        P("hid"),
        P(("groups", "rows", "mp"), "hid"),
    )
    sizes = (mesh.shape["rows"], mesh.shape["mp"], mesh.shape["hid"])
    return jax.shard_map(
        functools.partial(on_device, *sizes),
        mesh=mesh,
        in_specs=placed,
        out_specs=P(("groups", "rows", "mp"), "hid"),
        check_vma=False,
    )
```

```python
import functools

import jax
import jax.numpy as jnp
from jax import lax
from jax.experimental import pallas as pl
from jax.experimental.pallas import tpu as pltpu
from jax.sharding import PartitionSpec as P

BF16 = jnp.bfloat16
F32 = jnp.float32
VMEM_BYTES = 52 * 1024 * 1024
GATE_UP_VMEM_BYTES = 44 * 1024 * 1024
BUFFERS = 4


def shift(value, axis, size, hop):
    return lax.ppermute(value, axis, [((d + hop) % size, d) for d in range(size)])


def send(value, axis, size, hop):
    return lax.ppermute(value, axis, [(d, (d + hop) % size) for d in range(size)])


def swap(value, axis, size, bit):
    return lax.ppermute(value, axis, [(d, d ^ bit) for d in range(size)])


def doubling(size):
    bits = [1 << at for at in reversed(range(size.bit_length() - 1))]
    order = [0]
    for bit in bits:
        order = order + [offset ^ bit for offset in order]
    return bits, order


def tile_of(width, most):
    tile = most
    while tile > 128 and width % tile:
        tile //= 2
    return tile if width % tile == 0 else width


def whole(shape):
    return pl.BlockSpec(shape, lambda j, *_: (0,) * len(shape))


def slots_of(tiles):
    return min(BUFFERS, tiles)


def slots(depth, tile, tiles):
    count = slots_of(tiles)
    return [pltpu.VMEM((count, depth, tile), BF16), pltpu.SemaphoreType.DMA((count,))]


def next_block(weight_ref, slot_ref, slot_sems, tiles, first=0):
    step = pl.program_id(0)
    count, _, tile = slot_ref.shape

    def copy(block, slot):
        columns = pl.ds(pl.multiple_of((first + block) * tile, 128), tile)
        return pltpu.make_async_copy(
            weight_ref.at[0, :, columns], slot_ref.at[slot], slot_sems.at[slot]
        )

    @pl.when(step == 0)
    def _():
        for block in range(count - 1):
            copy(block, block).start()

    ahead = step + count - 1

    @pl.when(ahead < tiles)
    def _():
        copy(ahead, lax.rem(ahead, count)).start()

    slot = lax.rem(step, count)
    copy(step, slot).wait()
    return slot_ref.at[slot]


def in_hbm(count):
    return [pl.BlockSpec(memory_space=pltpu.HBM)] * count


def unread(after):
    return [pl.BlockSpec(memory_space=pl.ANY)] * len(after)


def params(vmem_bytes=VMEM_BYTES):
    return pltpu.CompilerParams(
        dimension_semantics=("arbitrary",), vmem_limit_bytes=vmem_bytes
    )


NO_COST = pl.CostEstimate(flops=1, bytes_accessed=1, transcendentals=0)


def gate_up_body(tiles, first, x_ref, gate_ref, up_ref, *refs):
    members, owners, cuts, q, cut = x_ref.shape
    out_refs = refs[-5 - owners : -5]
    lhs_ref = refs[-5]
    blocks = [
        next_block(gate_ref, refs[-4], refs[-3], tiles, first),
        next_block(up_ref, refs[-2], refs[-1], tiles, first),
    ]

    @pl.when(pl.program_id(0) == 0)
    def _():
        for owner in range(owners):
            for member in range(members):
                row = (owner * members + member) * q
                for at in range(cuts):
                    lhs_ref[row : row + q, at * cut : (at + 1) * cut] = x_ref[member, owner, at]

    rows = members * q
    for at, block_ref in enumerate(blocks):
        acts = jnp.dot(lhs_ref[...], block_ref[...], preferred_element_type=F32)
        for hop in range(owners):
            taken = acts[hop * rows : (hop + 1) * rows]
            out_refs[hop][at] = taken.astype(out_refs[hop].dtype)


def gate_up(x, gate_weight, up_weight, piece, pieces, after):
    members, owners, cuts, q, cut = x.shape
    rows, depth, own_rows = members * owners * q, cuts * cut, members * q
    width = gate_weight.shape[2] // pieces
    tile = tile_of(width, 256)
    tiles = width // tile
    return pl.pallas_call(
        functools.partial(gate_up_body, tiles, piece * tiles),
        grid=(tiles,),
        in_specs=[whole(x.shape)] + in_hbm(2) + unread(after),
        out_specs=[pl.BlockSpec((2, own_rows, tile), lambda j: (0, 0, j))] * owners,
        out_shape=[jax.ShapeDtypeStruct((2, own_rows, width), F32)]
        + [jax.ShapeDtypeStruct((2, own_rows, width), BF16)] * (owners - 1),
        scratch_shapes=[pltpu.VMEM((rows, depth), BF16)] + slots(depth, tile, tiles) * 2,
        compiler_params=params(GATE_UP_VMEM_BYTES),
        cost_estimate=NO_COST,
    )(x, gate_weight, up_weight, *after)


def down_body(owners, members, pieces, order, tiles, rank_ref, *refs):
    hidden_refs = refs[: owners * pieces]
    weight_ref = refs[owners * pieces]
    out_refs = refs[-6:-4]
    lhs_ref, acc_ref, slot_ref, slot_sems = refs[-4:]
    block_ref = next_block(weight_ref, slot_ref, slot_sems, tiles)
    q = hidden_refs[0].shape[0] // members
    part = hidden_refs[0].shape[1]
    block = acc_ref.shape[0] // len(order)

    @pl.when(pl.program_id(0) == 0)
    def _():
        for owner in range(owners):
            for piece in range(pieces):
                for member in range(members):
                    row = (member * owners + owner) * q
                    lhs_ref[row : row + q, piece * part : (piece + 1) * part] = hidden_refs[
                        owner * pieces + piece
                    ][member * q : (member + 1) * q]

    acc_ref[...] = jnp.dot(lhs_ref[...], block_ref[...], preferred_element_type=F32)
    half = len(order) // 2
    for slot, offset in enumerate(order):
        at = (rank_ref[0] ^ offset) * block
        taken = acc_ref[pl.ds(pl.multiple_of(at, block), block), :]
        out_ref = out_refs[slot // half]
        row = (slot % half) * block
        out_ref[row : row + block] = taken.astype(out_ref.dtype)


def down(rank, hidden, down_weight, members, order, after):
    owners, pieces = len(hidden), len(hidden[0])
    rows_each, part = hidden[0][0].shape
    rows, depth, width = owners * rows_each, pieces * part, down_weight.shape[2]
    tile = tile_of(width, 256)
    return pl.pallas_call(
        functools.partial(down_body, owners, members, pieces, order, width // tile),
        grid_spec=pltpu.PrefetchScalarGridSpec(
            num_scalar_prefetch=1,
            grid=(width // tile,),
            in_specs=[whole((rows_each, part))] * (owners * pieces)
            + in_hbm(1)
            + unread(after),
            out_specs=[pl.BlockSpec((rows // 2, tile), lambda j, *_: (0, j))] * 2,
            scratch_shapes=[pltpu.VMEM((rows, depth), BF16), pltpu.VMEM((rows, tile), F32)]
            + slots(depth, tile, width // tile),
        ),
        out_shape=[jax.ShapeDtypeStruct((rows // 2, width), kind) for kind in (F32, BF16)],
        compiler_params=params(),
        cost_estimate=NO_COST,
    )(rank, *[piece for of_owner in hidden for piece in of_owner], down_weight, *after)


def encode_body(members, order, tiles, rank_ref, near_ref, far_ref, weight_ref, *refs):
    out_refs = refs[-3 - members : -3]
    lhs_ref, slot_ref, slot_sems = refs[-3:]
    weight_block = next_block(weight_ref, slot_ref, slot_sems, tiles)
    block = lhs_ref.shape[0] // len(order)
    half = len(order) // 2

    @pl.when(pl.program_id(0) == 0)
    def _():
        for slot, offset in enumerate(order):
            at = (rank_ref[0] ^ offset) * block
            row = (slot % half) * block
            from_ref = far_ref if slot >= half else near_ref
            lhs_ref[pl.ds(pl.multiple_of(at, block), block), :] = from_ref[row : row + block]

    pre = jnp.dot(lhs_ref[...], weight_block[...], preferred_element_type=F32)
    rows = pre.shape[0] // members
    for member in range(members):
        taken = pre[member * rows : (member + 1) * rows]
        out_refs[member][...] = taken.astype(out_refs[member].dtype)


def encode(rank, near, far, enc_weight, members, order, after):
    rows, depth = 2 * near.shape[0], near.shape[1]
    width = enc_weight.shape[2]
    rows_each = rows // members
    tile = tile_of(width, 512)
    return pl.pallas_call(
        functools.partial(encode_body, members, order, width // tile),
        grid_spec=pltpu.PrefetchScalarGridSpec(
            num_scalar_prefetch=1,
            grid=(width // tile,),
            in_specs=[whole(near.shape)] * 2 + in_hbm(1) + unread(after),
            out_specs=[pl.BlockSpec((rows_each, tile), lambda j, *_: (0, j))] * members,
            scratch_shapes=[pltpu.VMEM((rows, depth), BF16)] + slots(depth, tile, width // tile),
        ),
        out_shape=[jax.ShapeDtypeStruct((rows_each, width), F32)]
        + [jax.ShapeDtypeStruct((rows_each, width), BF16)] * (members - 1),
        compiler_params=params(),
        cost_estimate=NO_COST,
    )(rank, near, far, enc_weight, *after)


def chunk_rows(total, unit):
    units = total // unit
    if units < 8:
        return [total]
    most = 3 * (units // 8)
    return [most * unit, most * unit, (units - 2 * most) * unit]


def on_device(
    owners, members, ranks, tokens, norm_gain, gate_weight, up_weight, down_weight, enc_weight,
    enc_bias, adjoint,
):
    row_at = lax.axis_index("rows")
    member_at = lax.axis_index("mp")
    rank_at = lax.axis_index("hid")
    rank = rank_at.astype(jnp.int32).reshape(1)
    per_device = adjoint.shape[0]
    cut = tokens.shape[1]
    half_cuts = ranks // owners
    model_width = cut * ranks

    gain = lax.dynamic_slice_in_dim(
        norm_gain[0], row_at * (model_width // owners), model_width // owners, 0
    ).reshape(half_cuts, 1, cut)
    own_tokens = lax.dynamic_slice_in_dim(tokens, member_at * per_device, per_device, 0)

    bits, order = doubling(ranks)

    def from_all(value, axis, size):
        return jnp.stack([value] + [shift(value, axis, size, hop) for hop in range(1, size)])

    def place_of(offset):
        place = 0
        for at in range(len(bits)):
            place = place + ((offset >> at) & 1) * bits[at]
        return place

    def all_columns(mine):
        gathered = mine[None]
        for bit in bits:
            gathered = jnp.concatenate((gathered, swap(gathered, "hid", ranks, bit)))
        return gathered

    def from_owners(gathered):
        wide = gathered.astype(F32)
        squares = jnp.sum(wide * wide, axis=(0, 2))
        inverse = lax.rsqrt(squares / model_width + 1e-05)
        columns, going = [], []
        for hop in range(owners):
            target = lax.rem(row_at + owners - hop, owners)
            half = jnp.concatenate(
                [
                    lax.dynamic_slice_in_dim(
                        gathered, place_of(rank_at ^ (target * half_cuts + at)), 1, 0
                    )
                    for at in range(half_cuts)
                ]
            )
            going.append(half)
            columns.append(half if hop == 0 else shift(half, "rows", owners, hop))
        return columns, from_all(inverse, "rows", owners), going

    def from_members(columns, inverses):
        return from_all(jnp.stack(columns), "mp", members), from_all(inverses, "mp", members)

    def normed(columns, inverses):
        return (columns.astype(F32) * inverses[:, :, None, :, None] * gain).astype(BF16)

    sizes = chunk_rows(per_device, 16 * max(1, ranks // (owners * members)))
    starts = [sum(sizes[:at]) for at in range(len(sizes))]
    chunks = len(sizes)
    head = sizes[0]

    columns, inverses, going = from_owners(all_columns(own_tokens[:head]))
    xs = [normed(*from_members(columns, inverses))]
    rest = None
    if chunks > 1:
        rest, _ = lax.optimization_barrier((all_columns(own_tokens[head:]), going))
        rest = from_owners(rest)

    sums, hidden, layer, blocks, outs = ({} for _ in range(5))
    last = []

    def gate_up_of(t):
        pieces = 2 if t == 0 and gate_weight.shape[2] % 512 == 0 else 1
        sums[t] = []
        for piece in range(pieces):
            own, *sends = gate_up(
                xs[t], gate_weight, up_weight, piece, pieces, list(last)
            )
            last[:] = [own]
            if t == 0 and rest is not None:
                last.extend(rest[2])
            others = [send(sends[hop - 1], "rows", owners, hop) for hop in range(1, owners)]
            sums[t].append((own, others))

    def rest_of(_):
        if rest is None:
            return
        (columns, inverses), _ = lax.optimization_barrier((rest[:2], sums[0][0][0]))
        columns, inverses = from_members(columns, inverses)
        for start, q in zip(starts[1:], sizes[1:]):
            rows = slice(start - head, start - head + q)
            xs.append(normed(columns[:, :, :, rows], inverses[:, :, rows]))

    def ordered(values):
        return lax.optimization_barrier((values, last[0]))[0]

    def hidden_of(t):
        hidden[t] = [[] for _ in range(owners)]
        for own, others in sums[t]:
            acts = own
            for other in others:
                acts = acts + other.astype(F32)
            units = (jax.nn.silu(acts[0]) * acts[1]).astype(BF16)
            hidden[t][0].append(units)
            for hop in range(1, owners):
                hidden[t][hop].append(shift(units, "rows", owners, hop))
        last.append(hidden[t][0][-1])

    def down_of(t):
        total, going = down(rank, hidden[t], down_weight, members, order, list(last))
        last[:] = [total]
        layer[t] = (total, swap(going, "hid", ranks, 1))

    def halve_of(t):
        total, arrived = ordered(layer[t])
        for bit in reversed(bits[:-1]):
            total = total + arrived.astype(F32)
            kept = total.shape[0] // 2
            going = total[kept:].astype(BF16)
            last.append(going)
            total, arrived = total[:kept], swap(going, "hid", ranks, bit)
        layer[t] = (total, arrived)

    def settle_of(t):
        total, arrived = ordered(layer[t])
        block = (total + arrived.astype(F32)).astype(BF16)
        last.append(block)
        layer[t] = (block, swap(block, "hid", ranks, bits[0]))

    def double_of(t):
        near, far = ordered(layer[t])
        for bit in bits[1:]:
            near = jnp.concatenate((near, far))
            last.append(near)
            far = swap(near, "hid", ranks, bit)
        blocks[t] = (near, far)

    def features_of(t):
        own, *sends = encode(rank, *blocks[t], enc_weight, members, order, list(last))
        last[:] = [own]
        sums[t] = (own, [send(sends[hop - 1], "mp", members, hop) for hop in range(1, members)])

    def share_of(t):
        total, others = ordered(sums[t])
        for other in others:
            total = total + other.astype(F32)
        q = sizes[t]
        others = []
        for hop in range(1, owners):
            going = total[hop * q : (hop + 1) * q].astype(BF16)
            last.append(going)
            others.append(send(going, "rows", owners, hop))
        sums[t] = (total[:q], others)

    def finish_of(t):
        pre, others = sums[t]
        for other in others:
            pre = pre + other.astype(F32)
        pre = pre + enc_bias[None, :]
        factor = adjoint[starts[t] : starts[t] + sizes[t]].astype(F32)
        outs[t] = (jnp.maximum(pre, 0.0) * factor).astype(BF16)
        last.append(outs[t])

    stages = (
        (gate_up_of, 0), (rest_of, 0), (gate_up_of, 1), (hidden_of, 0), (hidden_of, 1), (gate_up_of, 2),
        (down_of, 0), (down_of, 1), (halve_of, 0), (halve_of, 1), (settle_of, 0), (hidden_of, 2),
        (settle_of, 1), (double_of, 0), (double_of, 1), (down_of, 2), (features_of, 0),
        (halve_of, 2), (share_of, 0), (features_of, 1), (settle_of, 2), (share_of, 1),
        (double_of, 2), (finish_of, 0), (features_of, 2), (share_of, 2), (finish_of, 1),
        (finish_of, 2),
    )
    for stage, t in stages:
        if t < chunks:
            stage(t)
    return jnp.concatenate([outs[t] for t in range(chunks)], axis=0)


def solution(mesh):
    placed = (
        P(("groups", "rows"), "hid"),
        P("mp", None),
        P("mp", "rows", "hid"),
        P("mp", "rows", "hid"),
        P("mp", "hid", "rows"),
        P("mp", "rows", "hid"),
        P("hid"),
        P(("groups", "rows", "mp"), "hid"),
    )
    sizes = (mesh.shape["rows"], mesh.shape["mp"], mesh.shape["hid"])
    return jax.shard_map(
        functools.partial(on_device, *sizes),
        mesh=mesh,
        in_specs=placed,
        out_specs=P(("groups", "rows", "mp"), "hid"),
        check_vma=False,
    )
```

```python
import functools

import jax
import jax.numpy as jnp
from jax import lax
from jax.experimental import pallas as pl
from jax.experimental.pallas import tpu as pltpu
from jax.sharding import PartitionSpec as P

BF16 = jnp.bfloat16
F32 = jnp.float32
VMEM_BYTES = 52 * 1024 * 1024
GATE_UP_VMEM_BYTES = 44 * 1024 * 1024
BUFFERS = 4


def shift(value, axis, size, hop):
    return lax.ppermute(value, axis, [((d + hop) % size, d) for d in range(size)])


def send(value, axis, size, hop):
    return lax.ppermute(value, axis, [(d, (d + hop) % size) for d in range(size)])


def swap(value, axis, size, bit):
    return lax.ppermute(value, axis, [(d, d ^ bit) for d in range(size)])


def doubling(size):
    bits = [1 << at for at in reversed(range(size.bit_length() - 1))]
    order = [0]
    for bit in bits:
        order = order + [offset ^ bit for offset in order]
    return bits, order


def tile_of(width, most):
    tile = most
    while tile > 128 and width % tile:
        tile //= 2
    return tile if width % tile == 0 else width


def whole(shape):
    return pl.BlockSpec(shape, lambda j, *_: (0,) * len(shape))


def slots_of(tiles):
    return min(BUFFERS, tiles)


def slots(depth, tile, tiles):
    count = slots_of(tiles)
    return [pltpu.VMEM((count, depth, tile), BF16), pltpu.SemaphoreType.DMA((count,))]


def next_block(weight_ref, slot_ref, slot_sems, tiles, first=0):
    step = pl.program_id(0)
    count, _, tile = slot_ref.shape

    def copy(block, slot):
        columns = pl.ds(pl.multiple_of((first + block) * tile, 128), tile)
        return pltpu.make_async_copy(
            weight_ref.at[0, :, columns], slot_ref.at[slot], slot_sems.at[slot]
        )

    @pl.when(step == 0)
    def _():
        for block in range(count - 1):
            copy(block, block).start()

    ahead = step + count - 1

    @pl.when(ahead < tiles)
    def _():
        copy(ahead, lax.rem(ahead, count)).start()

    slot = lax.rem(step, count)
    copy(step, slot).wait()
    return slot_ref.at[slot]


def in_hbm(count):
    return [pl.BlockSpec(memory_space=pltpu.HBM)] * count


def unread(after):
    return [pl.BlockSpec(memory_space=pl.ANY)] * len(after)


def params(vmem_bytes=VMEM_BYTES):
    return pltpu.CompilerParams(
        dimension_semantics=("arbitrary",), vmem_limit_bytes=vmem_bytes
    )


NO_COST = pl.CostEstimate(flops=1, bytes_accessed=1, transcendentals=0)


def gate_up_body(tiles, first, x_ref, gate_ref, up_ref, *refs):
    members, owners, cuts, q, cut = x_ref.shape
    out_refs = refs[-5 - owners : -5]
    lhs_ref = refs[-5]
    blocks = [
        next_block(gate_ref, refs[-4], refs[-3], tiles, first),
        next_block(up_ref, refs[-2], refs[-1], tiles, first),
    ]

    @pl.when(pl.program_id(0) == 0)
    def _():
        for owner in range(owners):
            for member in range(members):
                row = (owner * members + member) * q
                for at in range(cuts):
                    lhs_ref[row : row + q, at * cut : (at + 1) * cut] = x_ref[member, owner, at]

    rows = members * q
    for at, block_ref in enumerate(blocks):
        acts = jnp.dot(lhs_ref[...], block_ref[...], preferred_element_type=F32)
        for hop in range(owners):
            taken = acts[hop * rows : (hop + 1) * rows]
            out_refs[hop][at] = taken.astype(out_refs[hop].dtype)


def gate_up(x, gate_weight, up_weight, piece, pieces, after):
    members, owners, cuts, q, cut = x.shape
    rows, depth, own_rows = members * owners * q, cuts * cut, members * q
    width = gate_weight.shape[2] // pieces
    tile = tile_of(width, 256)
    tiles = width // tile
    return pl.pallas_call(
        functools.partial(gate_up_body, tiles, piece * tiles),
        grid=(tiles,),
        in_specs=[whole(x.shape)] + in_hbm(2) + unread(after),
        out_specs=[pl.BlockSpec((2, own_rows, tile), lambda j: (0, 0, j))] * owners,
        out_shape=[jax.ShapeDtypeStruct((2, own_rows, width), F32)]
        + [jax.ShapeDtypeStruct((2, own_rows, width), BF16)] * (owners - 1),
        scratch_shapes=[pltpu.VMEM((rows, depth), BF16)] + slots(depth, tile, tiles) * 2,
        compiler_params=params(GATE_UP_VMEM_BYTES),
        cost_estimate=NO_COST,
    )(x, gate_weight, up_weight, *after)


def down_body(owners, members, pieces, order, tiles, rank_ref, *refs):
    hidden_refs = refs[: owners * pieces]
    weight_ref = refs[owners * pieces]
    out_refs = refs[-6:-4]
    lhs_ref, acc_ref, slot_ref, slot_sems = refs[-4:]
    block_ref = next_block(weight_ref, slot_ref, slot_sems, tiles)
    q = hidden_refs[0].shape[0] // members
    part = hidden_refs[0].shape[1]
    block = acc_ref.shape[0] // len(order)

    @pl.when(pl.program_id(0) == 0)
    def _():
        for owner in range(owners):
            for piece in range(pieces):
                for member in range(members):
                    row = (member * owners + owner) * q
                    lhs_ref[row : row + q, piece * part : (piece + 1) * part] = hidden_refs[
                        owner * pieces + piece
                    ][member * q : (member + 1) * q]

    acc_ref[...] = jnp.dot(lhs_ref[...], block_ref[...], preferred_element_type=F32)
    half = len(order) // 2
    for slot, offset in enumerate(order):
        at = (rank_ref[0] ^ offset) * block
        taken = acc_ref[pl.ds(pl.multiple_of(at, block), block), :]
        out_ref = out_refs[slot // half]
        row = (slot % half) * block
        out_ref[row : row + block] = taken.astype(out_ref.dtype)


def down(rank, hidden, down_weight, members, order, after):
    owners, pieces = len(hidden), len(hidden[0])
    rows_each, part = hidden[0][0].shape
    rows, depth, width = owners * rows_each, pieces * part, down_weight.shape[2]
    tile = tile_of(width, 256)
    return pl.pallas_call(
        functools.partial(down_body, owners, members, pieces, order, width // tile),
        grid_spec=pltpu.PrefetchScalarGridSpec(
            num_scalar_prefetch=1,
            grid=(width // tile,),
            in_specs=[whole((rows_each, part))] * (owners * pieces)
            + in_hbm(1)
            + unread(after),
            out_specs=[pl.BlockSpec((rows // 2, tile), lambda j, *_: (0, j))] * 2,
            scratch_shapes=[pltpu.VMEM((rows, depth), BF16), pltpu.VMEM((rows, tile), F32)]
            + slots(depth, tile, width // tile),
        ),
        out_shape=[jax.ShapeDtypeStruct((rows // 2, width), kind) for kind in (F32, BF16)],
        compiler_params=params(),
        cost_estimate=NO_COST,
    )(rank, *[piece for of_owner in hidden for piece in of_owner], down_weight, *after)


def encode_body(members, order, tiles, rank_ref, near_ref, far_ref, weight_ref, *refs):
    out_refs = refs[-3 - members : -3]
    lhs_ref, slot_ref, slot_sems = refs[-3:]
    weight_block = next_block(weight_ref, slot_ref, slot_sems, tiles)
    block = lhs_ref.shape[0] // len(order)
    half = len(order) // 2

    @pl.when(pl.program_id(0) == 0)
    def _():
        for slot, offset in enumerate(order):
            at = (rank_ref[0] ^ offset) * block
            row = (slot % half) * block
            from_ref = far_ref if slot >= half else near_ref
            lhs_ref[pl.ds(pl.multiple_of(at, block), block), :] = from_ref[row : row + block]

    pre = jnp.dot(lhs_ref[...], weight_block[...], preferred_element_type=F32)
    rows = pre.shape[0] // members
    for member in range(members):
        taken = pre[member * rows : (member + 1) * rows]
        out_refs[member][...] = taken.astype(out_refs[member].dtype)


def encode(rank, near, far, enc_weight, members, order, after):
    rows, depth = 2 * near.shape[0], near.shape[1]
    width = enc_weight.shape[2]
    rows_each = rows // members
    tile = tile_of(width, 512)
    return pl.pallas_call(
        functools.partial(encode_body, members, order, width // tile),
        grid_spec=pltpu.PrefetchScalarGridSpec(
            num_scalar_prefetch=1,
            grid=(width // tile,),
            in_specs=[whole(near.shape)] * 2 + in_hbm(1) + unread(after),
            out_specs=[pl.BlockSpec((rows_each, tile), lambda j, *_: (0, j))] * members,
            scratch_shapes=[pltpu.VMEM((rows, depth), BF16)] + slots(depth, tile, width // tile),
        ),
        out_shape=[jax.ShapeDtypeStruct((rows_each, width), F32)]
        + [jax.ShapeDtypeStruct((rows_each, width), BF16)] * (members - 1),
        compiler_params=params(),
        cost_estimate=NO_COST,
    )(rank, near, far, enc_weight, *after)


def chunk_rows(total, unit):
    units = total // unit
    if units < 8:
        return [total]
    most = 3 * (units // 8)
    return [most * unit, most * unit, (units - 2 * most) * unit]


def on_device(
    owners, members, ranks, tokens, norm_gain, gate_weight, up_weight, down_weight, enc_weight,
    enc_bias, adjoint,
):
    row_at = lax.axis_index("rows")
    member_at = lax.axis_index("mp")
    rank_at = lax.axis_index("hid")
    rank = rank_at.astype(jnp.int32).reshape(1)
    per_device = adjoint.shape[0]
    cut = tokens.shape[1]
    half_cuts = ranks // owners
    model_width = cut * ranks

    gain = lax.dynamic_slice_in_dim(
        norm_gain[0], row_at * (model_width // owners), model_width // owners, 0
    ).reshape(half_cuts, 1, cut)
    own_tokens = lax.dynamic_slice_in_dim(tokens, member_at * per_device, per_device, 0)

    bits, order = doubling(ranks)

    def from_all(value, axis, size):
        return jnp.stack([value] + [shift(value, axis, size, hop) for hop in range(1, size)])

    def place_of(offset):
        place = 0
        for at in range(len(bits)):
            place = place + ((offset >> at) & 1) * bits[at]
        return place

    def after(values, others):
        return lax.optimization_barrier((values, others))[0]

    def doubled(gathered, bit):
        return jnp.concatenate((gathered, swap(gathered, "hid", ranks, bit)))

    def from_owners(gathered):
        wide = gathered.astype(F32)
        squares = jnp.sum(wide * wide, axis=(0, 2))
        inverse = lax.rsqrt(squares / model_width + 1e-05)
        columns = []
        for hop in range(owners):
            target = lax.rem(row_at + owners - hop, owners)
            half = jnp.concatenate(
                [
                    lax.dynamic_slice_in_dim(
                        gathered, place_of(rank_at ^ (target * half_cuts + at)), 1, 0
                    )
                    for at in range(half_cuts)
                ]
            )
            columns.append(half if hop == 0 else shift(half, "rows", owners, hop))
        return columns, inverse

    def from_members(columns, inverses):
        return from_all(jnp.stack(columns), "mp", members), from_all(inverses, "mp", members)

    def normed(columns, inverses):
        return (columns.astype(F32) * inverses[:, :, None, :, None] * gain).astype(BF16)

    sizes = chunk_rows(per_device, 16 * max(1, ranks // (owners * members)))
    starts = [sum(sizes[:at]) for at in range(len(sizes))]
    chunks = len(sizes)
    head = sizes[0]

    gathered = own_tokens[:head][None]
    rest = own_tokens[head:][None] if chunks > 1 else None
    for bit in bits:
        gathered = doubled(gathered, bit)
        if rest is not None:
            rest = doubled(after(rest, gathered), bit)
    first = from_owners(gathered)
    if rest is not None:
        rest = from_owners(after(rest, first))
    xs = [normed(*from_members(first[0], from_all(first[1], "rows", owners)))]

    sums, hidden, layer, blocks, outs = ({} for _ in range(5))
    last = []

    def gate_up_of(t):
        pieces = 2 if t == 0 and gate_weight.shape[2] % 512 == 0 else 1
        sums[t] = []
        for piece in range(pieces):
            own, *sends = gate_up(xs[t], gate_weight, up_weight, piece, pieces, list(last))
            last[:] = [own]
            if t == 0 and rest is not None:
                last.extend(rest[0])
            others = [send(sends[hop - 1], "rows", owners, hop) for hop in range(1, owners)]
            sums[t].append((own, others))

    def rest_of(_):
        if rest is None:
            return
        inverses = from_all(after(rest[1], sums[0][-1][0]), "rows", owners)
        columns, inverses = from_members(*after((rest[0], inverses), hidden[0][0]))
        for start, q in zip(starts[1:], sizes[1:]):
            rows = slice(start - head, start - head + q)
            xs.append(normed(columns[:, :, :, rows], inverses[:, :, rows]))

    def hidden_of(t):
        units = []
        for own, others in sums[t]:
            acts = own
            for other in others:
                acts = acts + other.astype(F32)
            units.append((jax.nn.silu(acts[0]) * acts[1]).astype(BF16))
        units = jnp.concatenate(units, axis=1)
        hidden[t] = [units] + [shift(units, "rows", owners, hop) for hop in range(1, owners)]
        last.append(units)

    def ordered(values):
        return after(values, last[0])

    def at_once(t):
        return t == chunks - 1 and ranks == 4

    def down_of(t):
        total, going = down(rank, [[units] for units in hidden[t]], down_weight, members, order, list(last))
        last[:] = [total]
        if at_once(t):
            block = total.shape[0] // 2
            far = total[block:].astype(BF16)
            arrived = [
                swap(part, "hid", ranks, offset)
                for part, offset in ((going[block:], 3), (far, 2), (going[:block], 1))
            ]
            layer[t] = (total[:block], arrived)
        else:
            layer[t] = (total, swap(going, "hid", ranks, 1))

    def halve_of(t):
        if at_once(t):
            return
        total, arrived = ordered(layer[t])
        for bit in reversed(bits[:-1]):
            total = total + arrived.astype(F32)
            kept = total.shape[0] // 2
            going = total[kept:].astype(BF16)
            last.append(going)
            total, arrived = total[:kept], swap(going, "hid", ranks, bit)
        layer[t] = (total, arrived)

    def settle_of(t):
        total, arrived = ordered(layer[t])
        for part in arrived if at_once(t) else [arrived]:
            total = total + part.astype(F32)
        block = total.astype(BF16)
        last.append(block)
        if at_once(t):
            third, second, first = (swap(block, "hid", ranks, offset) for offset in (3, 2, 1))
            blocks[t] = (jnp.concatenate((block, second)), jnp.concatenate((first, third)))
        else:
            layer[t] = (block, swap(block, "hid", ranks, bits[0]))

    def double_of(t):
        if at_once(t):
            return
        near, far = ordered(layer[t])
        for bit in bits[1:]:
            near = jnp.concatenate((near, far))
            last.append(near)
            far = swap(near, "hid", ranks, bit)
        blocks[t] = (near, far)

    def features_of(t):
        own, *sends = encode(rank, *blocks[t], enc_weight, members, order, list(last))
        last[:] = [own]
        sums[t] = (own, [send(sends[hop - 1], "mp", members, hop) for hop in range(1, members)])

    def share_of(t):
        total, others = ordered(sums[t])
        for other in others:
            total = total + other.astype(F32)
        q = sizes[t]
        others = []
        for hop in range(1, owners):
            going = total[hop * q : (hop + 1) * q].astype(BF16)
            last.append(going)
            others.append(send(going, "rows", owners, hop))
        sums[t] = (total[:q], others)

    def finish_of(t):
        pre, others = sums[t]
        for other in others:
            pre = pre + other.astype(F32)
        pre = pre + enc_bias[None, :]
        factor = adjoint[starts[t] : starts[t] + sizes[t]].astype(F32)
        outs[t] = (jnp.maximum(pre, 0.0) * factor).astype(BF16)
        last.append(outs[t])

    stages = (
        (gate_up_of, 0), (hidden_of, 0), (rest_of, 0), (gate_up_of, 1), (down_of, 0),
        (halve_of, 0), (hidden_of, 1), (gate_up_of, 2), (settle_of, 0), (down_of, 1),
        (double_of, 0), (hidden_of, 2), (halve_of, 1), (features_of, 0), (down_of, 2),
        (settle_of, 1), (share_of, 0), (settle_of, 2), (double_of, 1), (finish_of, 0),
        (features_of, 1), (share_of, 1), (features_of, 2), (share_of, 2), (finish_of, 1),
        (finish_of, 2),
    )
    for stage, t in stages:
        if t < chunks:
            stage(t)
    return jnp.concatenate([outs[t] for t in range(chunks)], axis=0)


def solution(mesh):
    placed = (
        P(("groups", "rows"), "hid"),
        P("mp", None),
        P("mp", "rows", "hid"),
        P("mp", "rows", "hid"),
        P("mp", "hid", "rows"),
        P("mp", "rows", "hid"),
        P("hid"),
        P(("groups", "rows", "mp"), "hid"),
    )
    sizes = (mesh.shape["rows"], mesh.shape["mp"], mesh.shape["hid"])
    return jax.shard_map(
        functools.partial(on_device, *sizes),
        mesh=mesh,
        in_specs=placed,
        out_specs=P(("groups", "rows", "mp"), "hid"),
        check_vma=False,
    )
```

```python
import functools

import jax
import jax.numpy as jnp
from jax import lax
from jax.experimental import pallas as pl
from jax.experimental.pallas import tpu as pltpu
from jax.sharding import PartitionSpec as P

BF16 = jnp.bfloat16
F32 = jnp.float32
VMEM_BYTES = 52 * 1024 * 1024
GATE_UP_VMEM_BYTES = 44 * 1024 * 1024
BUFFERS = 4


def shift(value, axis, size, hop):
    return lax.ppermute(value, axis, [((d + hop) % size, d) for d in range(size)])


def send(value, axis, size, hop):
    return lax.ppermute(value, axis, [(d, (d + hop) % size) for d in range(size)])


def swap(value, axis, size, bit):
    return lax.ppermute(value, axis, [(d, d ^ bit) for d in range(size)])


def doubling(size):
    bits = [1 << at for at in reversed(range(size.bit_length() - 1))]
    order = [0]
    for bit in bits:
        order = order + [offset ^ bit for offset in order]
    return bits, order


def tile_of(width, most):
    tile = most
    while tile > 128 and width % tile:
        tile //= 2
    return tile if width % tile == 0 else width


def whole(shape):
    return pl.BlockSpec(shape, lambda j, *_: (0,) * len(shape))


def slots_of(tiles):
    return min(BUFFERS, tiles)


def slots(depth, tile, tiles):
    count = slots_of(tiles)
    return [pltpu.VMEM((count, depth, tile), BF16), pltpu.SemaphoreType.DMA((count,))]


def next_block(weight_ref, slot_ref, slot_sems, tiles, first=0):
    step = pl.program_id(0)
    count, _, tile = slot_ref.shape

    def copy(block, slot):
        columns = pl.ds(pl.multiple_of((first + block) * tile, 128), tile)
        return pltpu.make_async_copy(
            weight_ref.at[0, :, columns], slot_ref.at[slot], slot_sems.at[slot]
        )

    @pl.when(step == 0)
    def _():
        for block in range(count - 1):
            copy(block, block).start()

    ahead = step + count - 1

    @pl.when(ahead < tiles)
    def _():
        copy(ahead, lax.rem(ahead, count)).start()

    slot = lax.rem(step, count)
    copy(step, slot).wait()
    return slot_ref.at[slot]


def in_hbm(count):
    return [pl.BlockSpec(memory_space=pltpu.HBM)] * count


def unread(after):
    return [pl.BlockSpec(memory_space=pl.ANY)] * len(after)


def params(vmem_bytes=VMEM_BYTES):
    return pltpu.CompilerParams(
        dimension_semantics=("arbitrary",), vmem_limit_bytes=vmem_bytes
    )


NO_COST = pl.CostEstimate(flops=1, bytes_accessed=1, transcendentals=0)


def gate_up_body(tiles, first, x_ref, gate_ref, up_ref, *refs):
    members, owners, cuts, q, cut = x_ref.shape
    out_refs = refs[-5 - owners : -5]
    lhs_ref = refs[-5]
    blocks = [
        next_block(gate_ref, refs[-4], refs[-3], tiles, first),
        next_block(up_ref, refs[-2], refs[-1], tiles, first),
    ]

    @pl.when(pl.program_id(0) == 0)
    def _():
        for owner in range(owners):
            for member in range(members):
                row = (owner * members + member) * q
                for at in range(cuts):
                    lhs_ref[row : row + q, at * cut : (at + 1) * cut] = x_ref[member, owner, at]

    rows = members * q
    for at, block_ref in enumerate(blocks):
        acts = jnp.dot(lhs_ref[...], block_ref[...], preferred_element_type=F32)
        for hop in range(owners):
            taken = acts[hop * rows : (hop + 1) * rows]
            out_refs[hop][at] = taken.astype(out_refs[hop].dtype)


def gate_up(x, gate_weight, up_weight, piece, pieces, after):
    members, owners, cuts, q, cut = x.shape
    rows, depth, own_rows = members * owners * q, cuts * cut, members * q
    width = gate_weight.shape[2] // pieces
    tile = tile_of(width, 256)
    tiles = width // tile
    return pl.pallas_call(
        functools.partial(gate_up_body, tiles, piece * tiles),
        grid=(tiles,),
        in_specs=[whole(x.shape)] + in_hbm(2) + unread(after),
        out_specs=[pl.BlockSpec((2, own_rows, tile), lambda j: (0, 0, j))] * owners,
        out_shape=[jax.ShapeDtypeStruct((2, own_rows, width), F32)]
        + [jax.ShapeDtypeStruct((2, own_rows, width), BF16)] * (owners - 1),
        scratch_shapes=[pltpu.VMEM((rows, depth), BF16)] + slots(depth, tile, tiles) * 2,
        compiler_params=params(GATE_UP_VMEM_BYTES),
        cost_estimate=NO_COST,
    )(x, gate_weight, up_weight, *after)


def down_body(owners, members, pieces, order, tiles, rank_ref, *refs):
    hidden_refs = refs[: owners * pieces]
    weight_ref = refs[owners * pieces]
    out_refs = refs[-6:-4]
    lhs_ref, acc_ref, slot_ref, slot_sems = refs[-4:]
    block_ref = next_block(weight_ref, slot_ref, slot_sems, tiles)
    q = hidden_refs[0].shape[0] // members
    part = hidden_refs[0].shape[1]
    block = acc_ref.shape[0] // len(order)

    @pl.when(pl.program_id(0) == 0)
    def _():
        for owner in range(owners):
            for piece in range(pieces):
                for member in range(members):
                    row = (member * owners + owner) * q
                    lhs_ref[row : row + q, piece * part : (piece + 1) * part] = hidden_refs[
                        owner * pieces + piece
                    ][member * q : (member + 1) * q]

    acc_ref[...] = jnp.dot(lhs_ref[...], block_ref[...], preferred_element_type=F32)
    half = len(order) // 2
    for slot, offset in enumerate(order):
        at = (rank_ref[0] ^ offset) * block
        taken = acc_ref[pl.ds(pl.multiple_of(at, block), block), :]
        out_ref = out_refs[slot // half]
        row = (slot % half) * block
        out_ref[row : row + block] = taken.astype(out_ref.dtype)


def down(rank, hidden, down_weight, members, order, after):
    owners, pieces = len(hidden), len(hidden[0])
    rows_each, part = hidden[0][0].shape
    rows, depth, width = owners * rows_each, pieces * part, down_weight.shape[2]
    tile = tile_of(width, 256)
    return pl.pallas_call(
        functools.partial(down_body, owners, members, pieces, order, width // tile),
        grid_spec=pltpu.PrefetchScalarGridSpec(
            num_scalar_prefetch=1,
            grid=(width // tile,),
            in_specs=[whole((rows_each, part))] * (owners * pieces)
            + in_hbm(1)
            + unread(after),
            out_specs=[pl.BlockSpec((rows // 2, tile), lambda j, *_: (0, j))] * 2,
            scratch_shapes=[pltpu.VMEM((rows, depth), BF16), pltpu.VMEM((rows, tile), F32)]
            + slots(depth, tile, width // tile),
        ),
        out_shape=[jax.ShapeDtypeStruct((rows // 2, width), kind) for kind in (F32, BF16)],
        compiler_params=params(),
        cost_estimate=NO_COST,
    )(rank, *[piece for of_owner in hidden for piece in of_owner], down_weight, *after)


def encode_body(members, order, tiles, rank_ref, near_ref, far_ref, weight_ref, *refs):
    out_refs = refs[-3 - members : -3]
    lhs_ref, slot_ref, slot_sems = refs[-3:]
    weight_block = next_block(weight_ref, slot_ref, slot_sems, tiles)
    block = lhs_ref.shape[0] // len(order)
    half = len(order) // 2

    @pl.when(pl.program_id(0) == 0)
    def _():
        for slot, offset in enumerate(order):
            at = (rank_ref[0] ^ offset) * block
            row = (slot % half) * block
            from_ref = far_ref if slot >= half else near_ref
            lhs_ref[pl.ds(pl.multiple_of(at, block), block), :] = from_ref[row : row + block]

    pre = jnp.dot(lhs_ref[...], weight_block[...], preferred_element_type=F32)
    rows = pre.shape[0] // members
    for member in range(members):
        taken = pre[member * rows : (member + 1) * rows]
        out_refs[member][...] = taken.astype(out_refs[member].dtype)


def encode(rank, near, far, enc_weight, members, order, after):
    rows, depth = 2 * near.shape[0], near.shape[1]
    width = enc_weight.shape[2]
    rows_each = rows // members
    tile = tile_of(width, 512)
    return pl.pallas_call(
        functools.partial(encode_body, members, order, width // tile),
        grid_spec=pltpu.PrefetchScalarGridSpec(
            num_scalar_prefetch=1,
            grid=(width // tile,),
            in_specs=[whole(near.shape)] * 2 + in_hbm(1) + unread(after),
            out_specs=[pl.BlockSpec((rows_each, tile), lambda j, *_: (0, j))] * members,
            scratch_shapes=[pltpu.VMEM((rows, depth), BF16)] + slots(depth, tile, width // tile),
        ),
        out_shape=[jax.ShapeDtypeStruct((rows_each, width), F32)]
        + [jax.ShapeDtypeStruct((rows_each, width), BF16)] * (members - 1),
        compiler_params=params(),
        cost_estimate=NO_COST,
    )(rank, near, far, enc_weight, *after)


def chunk_rows(total, unit):
    units = total // unit
    if units < 8:
        return [total]
    most = 3 * (units // 8)
    return [most * unit, most * unit, (units - 2 * most) * unit]


def on_device(
    owners, members, ranks, tokens, norm_gain, gate_weight, up_weight, down_weight, enc_weight,
    enc_bias, adjoint,
):
    row_at = lax.axis_index("rows")
    member_at = lax.axis_index("mp")
    rank_at = lax.axis_index("hid")
    rank = rank_at.astype(jnp.int32).reshape(1)
    per_device = adjoint.shape[0]
    cut = tokens.shape[1]
    half_cuts = ranks // owners
    model_width = cut * ranks

    gain = lax.dynamic_slice_in_dim(
        norm_gain[0], row_at * (model_width // owners), model_width // owners, 0
    ).reshape(half_cuts, 1, cut)
    own_tokens = lax.dynamic_slice_in_dim(tokens, member_at * per_device, per_device, 0)

    bits, order = doubling(ranks)

    def from_all(value, axis, size):
        return jnp.stack([value] + [shift(value, axis, size, hop) for hop in range(1, size)])

    def place_of(offset):
        place = 0
        for at in range(len(bits)):
            place = place + ((offset >> at) & 1) * bits[at]
        return place

    def after(values, others):
        return lax.optimization_barrier((values, others))[0]

    def doubled(gathered, bit):
        return jnp.concatenate((gathered, swap(gathered, "hid", ranks, bit)))

    def from_owners(gathered):
        wide = gathered.astype(F32)
        squares = jnp.sum(wide * wide, axis=(0, 2))
        inverse = lax.rsqrt(squares / model_width + 1e-05)
        columns = []
        for hop in range(owners):
            target = lax.rem(row_at + owners - hop, owners)
            half = jnp.concatenate(
                [
                    lax.dynamic_slice_in_dim(
                        gathered, place_of(rank_at ^ (target * half_cuts + at)), 1, 0
                    )
                    for at in range(half_cuts)
                ]
            )
            columns.append(half if hop == 0 else shift(half, "rows", owners, hop))
        return columns, from_all(inverse, "mp", members)

    def scales(inverse):
        return from_all(inverse, "rows", owners).transpose(1, 0, 2)

    def from_members(columns):
        return from_all(jnp.stack(columns), "mp", members)

    def normed(columns, inverses):
        return (columns.astype(F32) * inverses[:, :, None, :, None] * gain).astype(BF16)

    sizes = chunk_rows(per_device, 16 * max(1, ranks // (owners * members)))
    starts = [sum(sizes[:at]) for at in range(len(sizes))]
    chunks = len(sizes)
    head = sizes[0]

    gathered = own_tokens[:head][None]
    rest = own_tokens[head:][None] if chunks > 1 else None
    for bit in bits:
        gathered = doubled(gathered, bit)
        if rest is not None:
            rest = doubled(after(rest, gathered), bit)
    first = from_owners(gathered)
    if rest is not None:
        rest = from_owners(after(rest, first))
    xs = [normed(from_members(first[0]), scales(first[1]))]

    sums, hidden, layer, blocks, outs = ({} for _ in range(5))
    last = []

    def gate_up_of(t):
        pieces = 2 if t == 0 and gate_weight.shape[2] % 512 == 0 else 1
        sums[t] = []
        for piece in range(pieces):
            own, *sends = gate_up(xs[t], gate_weight, up_weight, piece, pieces, list(last))
            last[:] = [own]
            if t == 0 and rest is not None:
                last.extend(rest[0])
            others = [send(sends[hop - 1], "rows", owners, hop) for hop in range(1, owners)]
            sums[t].append((own, others))

    def rest_of(_):
        if rest is None:
            return
        columns = from_members(rest[0])
        inverses = scales(after(rest[1], sums[0][-1][0]))
        for start, q in zip(starts[1:], sizes[1:]):
            rows = slice(start - head, start - head + q)
            xs.append(normed(columns[:, :, :, rows], inverses[:, :, rows]))

    def hidden_of(t):
        units = []
        for own, others in sums[t]:
            acts = own
            for other in others:
                acts = acts + other.astype(F32)
            units.append((jax.nn.silu(acts[0]) * acts[1]).astype(BF16))
        units = jnp.concatenate(units, axis=1)
        hidden[t] = [units] + [shift(units, "rows", owners, hop) for hop in range(1, owners)]
        last.append(units)

    def ordered(values):
        return after(values, last[0])

    def at_once(t):
        return t == chunks - 1 and ranks == 4

    def down_of(t):
        total, going = down(rank, [[units] for units in hidden[t]], down_weight, members, order, list(last))
        last[:] = [total]
        if at_once(t):
            block = total.shape[0] // 2
            far = total[block:].astype(BF16)
            arrived = [
                swap(part, "hid", ranks, offset)
                for part, offset in ((going[block:], 3), (far, 2), (going[:block], 1))
            ]
            layer[t] = (total[:block], arrived)
        else:
            layer[t] = (total, swap(going, "hid", ranks, 1))

    def halve_of(t):
        if at_once(t):
            return
        total, arrived = ordered(layer[t])
        for bit in reversed(bits[:-1]):
            total = total + arrived.astype(F32)
            kept = total.shape[0] // 2
            going = total[kept:].astype(BF16)
            last.append(going)
            total, arrived = total[:kept], swap(going, "hid", ranks, bit)
        layer[t] = (total, arrived)

    def settle_of(t):
        total, arrived = ordered(layer[t])
        for part in arrived if at_once(t) else [arrived]:
            total = total + part.astype(F32)
        block = total.astype(BF16)
        last.append(block)
        if at_once(t):
            third, second, first = (swap(block, "hid", ranks, offset) for offset in (3, 2, 1))
            blocks[t] = (jnp.concatenate((block, second)), jnp.concatenate((first, third)))
            last.extend(blocks[t])
        else:
            layer[t] = (block, swap(block, "hid", ranks, bits[0]))

    def double_of(t):
        if at_once(t):
            return
        near, far = ordered(layer[t])
        if t > 0:
            near, far = after((near, far), sums[t - 1][0])
        for bit in bits[1:]:
            near = jnp.concatenate((near, far))
            last.append(near)
            far = swap(near, "hid", ranks, bit)
        blocks[t] = (near, far)

    def features_of(t):
        own, *sends = encode(rank, *blocks[t], enc_weight, members, order, list(last))
        last[:] = [own]
        sums[t] = (own, [send(sends[hop - 1], "mp", members, hop) for hop in range(1, members)])

    def share_of(t):
        total, others = ordered(sums[t])
        for other in others:
            total = total + other.astype(F32)
        q = sizes[t]
        others = []
        for hop in range(1, owners):
            going = total[hop * q : (hop + 1) * q].astype(BF16)
            last.append(going)
            others.append(send(going, "rows", owners, hop))
        sums[t] = (total[:q], others)

    def shared_of(t):
        last.extend(sums[t][1])

    def finish_of(t):
        pre, others = sums[t]
        for other in others:
            pre = pre + other.astype(F32)
        pre = pre + enc_bias[None, :]
        factor = adjoint[starts[t] : starts[t] + sizes[t]].astype(F32)
        outs[t] = (jnp.maximum(pre, 0.0) * factor).astype(BF16)

    stages = (
        (gate_up_of, 0), (rest_of, 0), (hidden_of, 0), (gate_up_of, 1), (down_of, 0),
        (halve_of, 0), (hidden_of, 1), (gate_up_of, 2), (settle_of, 0), (down_of, 1),
        (double_of, 0), (hidden_of, 2), (halve_of, 1), (features_of, 0), (down_of, 2),
        (settle_of, 1), (share_of, 0), (settle_of, 2), (double_of, 1), (shared_of, 0),
        (features_of, 1), (share_of, 1), (features_of, 2), (share_of, 2), (finish_of, 0),
        (finish_of, 1), (finish_of, 2),
    )
    for stage, t in stages:
        if t < chunks:
            stage(t)
    return jnp.concatenate([outs[t] for t in range(chunks)], axis=0)


def solution(mesh):
    placed = (
        P(("groups", "rows"), "hid"),
        P("mp", None),
        P("mp", "rows", "hid"),
        P("mp", "rows", "hid"),
        P("mp", "hid", "rows"),
        P("mp", "rows", "hid"),
        P("hid"),
        P(("groups", "rows", "mp"), "hid"),
    )
    sizes = (mesh.shape["rows"], mesh.shape["mp"], mesh.shape["hid"])
    return jax.shard_map(
        functools.partial(on_device, *sizes),
        mesh=mesh,
        in_specs=placed,
        out_specs=P(("groups", "rows", "mp"), "hid"),
        check_vma=False,
    )
```

```python
import functools

import jax
import jax.numpy as jnp
from jax import lax
from jax.experimental import pallas as pl
from jax.experimental.pallas import tpu as pltpu
from jax.sharding import PartitionSpec as P

BF16 = jnp.bfloat16
F32 = jnp.float32
VMEM_BYTES = 51 * 1024 * 1024
GATE_UP_VMEM_BYTES = 44 * 1024 * 1024
BUFFERS = 4


def shift(value, axis, size, hop):
    return lax.ppermute(value, axis, [((d + hop) % size, d) for d in range(size)])


def send(value, axis, size, hop):
    return lax.ppermute(value, axis, [(d, (d + hop) % size) for d in range(size)])


def swap(value, axis, size, bit):
    return lax.ppermute(value, axis, [(d, d ^ bit) for d in range(size)])


def doubling(size):
    bits = [1 << at for at in reversed(range(size.bit_length() - 1))]
    order = [0]
    for bit in bits:
        order = order + [offset ^ bit for offset in order]
    return bits, order


def tile_of(width, most):
    tile = most
    while tile > 128 and width % tile:
        tile //= 2
    return tile if width % tile == 0 else width


def whole(shape):
    return pl.BlockSpec(shape, lambda j, *_: (0,) * len(shape))


def slots_of(tiles):
    return min(BUFFERS, tiles)


def slots(depth, tile, tiles):
    count = slots_of(tiles)
    return [pltpu.VMEM((count, depth, tile), BF16), pltpu.SemaphoreType.DMA((count,))]


def next_block(weight_ref, slot_ref, slot_sems, tiles, first=0):
    step = pl.program_id(0)
    count, _, tile = slot_ref.shape

    def copy(block, slot):
        columns = pl.ds(pl.multiple_of((first + block) * tile, 128), tile)
        return pltpu.make_async_copy(
            weight_ref.at[0, :, columns], slot_ref.at[slot], slot_sems.at[slot]
        )

    @pl.when(step == 0)
    def _():
        for block in range(count - 1):
            copy(block, block).start()

    ahead = step + count - 1

    @pl.when(ahead < tiles)
    def _():
        copy(ahead, lax.rem(ahead, count)).start()

    slot = lax.rem(step, count)
    copy(step, slot).wait()
    return slot_ref.at[slot]


def in_hbm(count):
    return [pl.BlockSpec(memory_space=pltpu.HBM)] * count


def unread(after):
    return [pl.BlockSpec(memory_space=pl.ANY)] * len(after)


def params(vmem_bytes=VMEM_BYTES):
    return pltpu.CompilerParams(
        dimension_semantics=("arbitrary",), vmem_limit_bytes=vmem_bytes
    )


NO_COST = pl.CostEstimate(flops=1, bytes_accessed=1, transcendentals=0)


def gate_up_body(tiles, first, x_ref, gate_ref, up_ref, *refs):
    members, owners, cuts, q, cut = x_ref.shape
    out_refs = refs[-5 - owners : -5]
    lhs_ref = refs[-5]
    blocks = [
        next_block(gate_ref, refs[-4], refs[-3], tiles, first),
        next_block(up_ref, refs[-2], refs[-1], tiles, first),
    ]

    @pl.when(pl.program_id(0) == 0)
    def _():
        for owner in range(owners):
            for member in range(members):
                row = (owner * members + member) * q
                for at in range(cuts):
                    lhs_ref[row : row + q, at * cut : (at + 1) * cut] = x_ref[member, owner, at]

    rows = members * q
    for at, block_ref in enumerate(blocks):
        acts = jnp.dot(lhs_ref[...], block_ref[...], preferred_element_type=F32)
        for hop in range(owners):
            taken = acts[hop * rows : (hop + 1) * rows]
            out_refs[hop][at] = taken.astype(out_refs[hop].dtype)


def gate_up(x, gate_weight, up_weight, piece, pieces, after):
    members, owners, cuts, q, cut = x.shape
    rows, depth, own_rows = members * owners * q, cuts * cut, members * q
    width = gate_weight.shape[2] // pieces
    tile = tile_of(width, 256)
    tiles = width // tile
    return pl.pallas_call(
        functools.partial(gate_up_body, tiles, piece * tiles),
        grid=(tiles,),
        in_specs=[whole(x.shape)] + in_hbm(2) + unread(after),
        out_specs=[pl.BlockSpec((2, own_rows, tile), lambda j: (0, 0, j))] * owners,
        out_shape=[jax.ShapeDtypeStruct((2, own_rows, width), F32)]
        + [jax.ShapeDtypeStruct((2, own_rows, width), BF16)] * (owners - 1),
        scratch_shapes=[pltpu.VMEM((rows, depth), BF16)] + slots(depth, tile, tiles) * 2,
        compiler_params=params(GATE_UP_VMEM_BYTES),
        cost_estimate=NO_COST,
    )(x, gate_weight, up_weight, *after)


def down_body(owners, members, pieces, order, tiles, rank_ref, *refs):
    hidden_refs = refs[: owners * pieces]
    weight_ref = refs[owners * pieces]
    out_refs = refs[-6:-4]
    lhs_ref, acc_ref, slot_ref, slot_sems = refs[-4:]
    block_ref = next_block(weight_ref, slot_ref, slot_sems, tiles)
    q = hidden_refs[0].shape[0] // members
    part = hidden_refs[0].shape[1]
    block = acc_ref.shape[0] // len(order)

    @pl.when(pl.program_id(0) == 0)
    def _():
        for owner in range(owners):
            for piece in range(pieces):
                for member in range(members):
                    row = (member * owners + owner) * q
                    lhs_ref[row : row + q, piece * part : (piece + 1) * part] = hidden_refs[
                        owner * pieces + piece
                    ][member * q : (member + 1) * q]

    acc_ref[...] = jnp.dot(lhs_ref[...], block_ref[...], preferred_element_type=F32)
    half = len(order) // 2
    for slot, offset in enumerate(order):
        at = (rank_ref[0] ^ offset) * block
        taken = acc_ref[pl.ds(pl.multiple_of(at, block), block), :]
        out_ref = out_refs[slot // half]
        row = (slot % half) * block
        out_ref[row : row + block] = taken.astype(out_ref.dtype)


def down(rank, hidden, down_weight, members, order, after):
    owners, pieces = len(hidden), len(hidden[0])
    rows_each, part = hidden[0][0].shape
    rows, depth, width = owners * rows_each, pieces * part, down_weight.shape[2]
    tile = tile_of(width, 256)
    return pl.pallas_call(
        functools.partial(down_body, owners, members, pieces, order, width // tile),
        grid_spec=pltpu.PrefetchScalarGridSpec(
            num_scalar_prefetch=1,
            grid=(width // tile,),
            in_specs=[whole((rows_each, part))] * (owners * pieces)
            + in_hbm(1)
            + unread(after),
            out_specs=[pl.BlockSpec((rows // 2, tile), lambda j, *_: (0, j))] * 2,
            scratch_shapes=[pltpu.VMEM((rows, depth), BF16), pltpu.VMEM((rows, tile), F32)]
            + slots(depth, tile, width // tile),
        ),
        out_shape=[jax.ShapeDtypeStruct((rows // 2, width), kind) for kind in (F32, BF16)],
        compiler_params=params(),
        cost_estimate=NO_COST,
    )(rank, *[piece for of_owner in hidden for piece in of_owner], down_weight, *after)


def encode_body(members, order, tiles, rank_ref, near_ref, far_ref, weight_ref, *refs):
    out_refs = refs[-3 - members : -3]
    lhs_ref, slot_ref, slot_sems = refs[-3:]
    weight_block = next_block(weight_ref, slot_ref, slot_sems, tiles)
    block = lhs_ref.shape[0] // len(order)
    half = len(order) // 2

    @pl.when(pl.program_id(0) == 0)
    def _():
        for slot, offset in enumerate(order):
            at = (rank_ref[0] ^ offset) * block
            row = (slot % half) * block
            from_ref = far_ref if slot >= half else near_ref
            lhs_ref[pl.ds(pl.multiple_of(at, block), block), :] = from_ref[row : row + block]

    pre = jnp.dot(lhs_ref[...], weight_block[...], preferred_element_type=F32)
    rows = pre.shape[0] // members
    for member in range(members):
        taken = pre[member * rows : (member + 1) * rows]
        out_refs[member][...] = taken.astype(out_refs[member].dtype)


def encode(rank, near, far, enc_weight, members, order, after):
    rows, depth = 2 * near.shape[0], near.shape[1]
    width = enc_weight.shape[2]
    rows_each = rows // members
    tile = tile_of(width, 512)
    return pl.pallas_call(
        functools.partial(encode_body, members, order, width // tile),
        grid_spec=pltpu.PrefetchScalarGridSpec(
            num_scalar_prefetch=1,
            grid=(width // tile,),
            in_specs=[whole(near.shape)] * 2 + in_hbm(1) + unread(after),
            out_specs=[pl.BlockSpec((rows_each, tile), lambda j, *_: (0, j))] * members,
            scratch_shapes=[pltpu.VMEM((rows, depth), BF16)] + slots(depth, tile, width // tile),
        ),
        out_shape=[jax.ShapeDtypeStruct((rows_each, width), F32)]
        + [jax.ShapeDtypeStruct((rows_each, width), BF16)] * (members - 1),
        compiler_params=params(),
        cost_estimate=NO_COST,
    )(rank, near, far, enc_weight, *after)


def chunk_rows(total, unit):
    units = total // unit
    if units < 8:
        return [total]
    most = 3 * (units // 8)
    return [most * unit, most * unit, (units - 2 * most) * unit]


def on_device(
    owners, members, ranks, tokens, norm_gain, gate_weight, up_weight, down_weight, enc_weight,
    enc_bias, adjoint,
):
    row_at = lax.axis_index("rows")
    member_at = lax.axis_index("mp")
    rank_at = lax.axis_index("hid")
    rank = rank_at.astype(jnp.int32).reshape(1)
    per_device = adjoint.shape[0]
    cut = tokens.shape[1]
    half_cuts = ranks // owners
    model_width = cut * ranks

    gain = lax.dynamic_slice_in_dim(
        norm_gain[0], row_at * (model_width // owners), model_width // owners, 0
    ).reshape(half_cuts, 1, cut)
    own_tokens = lax.dynamic_slice_in_dim(tokens, member_at * per_device, per_device, 0)

    bits, order = doubling(ranks)

    def from_all(value, axis, size):
        return jnp.stack([value] + [shift(value, axis, size, hop) for hop in range(1, size)])

    def place_of(offset):
        place = 0
        for at in range(len(bits)):
            place = place + ((offset >> at) & 1) * bits[at]
        return place

    def after(values, others):
        return lax.optimization_barrier((values, others))[0]

    def doubled(gathered, bit):
        return jnp.concatenate((gathered, swap(gathered, "hid", ranks, bit)))

    def from_owners(gathered):
        wide = gathered.astype(F32)
        squares = jnp.sum(wide * wide, axis=(0, 2))
        inverse = lax.rsqrt(squares / model_width + 1e-05)
        columns = []
        for hop in range(owners):
            target = lax.rem(row_at + owners - hop, owners)
            half = jnp.concatenate(
                [
                    lax.dynamic_slice_in_dim(
                        gathered, place_of(rank_at ^ (target * half_cuts + at)), 1, 0
                    )
                    for at in range(half_cuts)
                ]
            )
            columns.append(half if hop == 0 else shift(half, "rows", owners, hop))
        return columns, inverse

    def from_members(columns):
        return from_all(jnp.stack(columns), "mp", members)

    def normed(columns, inverses):
        return (columns.astype(F32) * inverses[:, :, None, :, None] * gain).astype(BF16)

    sizes = chunk_rows(per_device, 16 * max(1, ranks // (owners * members)))
    starts = [sum(sizes[:at]) for at in range(len(sizes))]
    chunks = len(sizes)
    head = sizes[0]

    gathered = own_tokens[:head][None]
    for bit in bits:
        gathered = doubled(gathered, bit)
    columns, inverse = from_owners(gathered)
    inverses = from_all(inverse, "rows", owners)
    columns, inverses = after((columns, inverses), (columns, inverses))
    xs = [normed(from_members(columns), from_all(inverses, "mp", members))]
    rest = None
    if chunks > 1:
        rest = after(own_tokens[head:][None], gathered)
        rest = [rest, swap(rest, "hid", ranks, bits[0])]

    sums, hidden, layer, blocks, outs = ({} for _ in range(5))
    last = []

    def gate_up_of(t):
        pieces = 2 if t == 0 and gate_weight.shape[2] % 512 == 0 else 1
        sums[t] = []
        for piece in range(pieces):
            own, *sends = gate_up(xs[t], gate_weight, up_weight, piece, pieces, list(last))
            last[:] = [own]
            others = [send(sends[hop - 1], "rows", owners, hop) for hop in range(1, owners)]
            sums[t].append((own, others))

    def rest_of(units):
        gathered = jnp.concatenate(after(rest, sums[0][-1][0]))
        for bit in bits[1:]:
            gathered = doubled(after(gathered, sums[0][-1][0]), bit)
        columns, inverse = from_owners(after(gathered, units))
        inverses = from_all(inverse, "rows", owners)
        columns, inverses = after((columns, inverses), (columns, inverses))
        columns, inverses = from_members(columns), from_all(inverses, "mp", members)
        for start, q in zip(starts[1:], sizes[1:]):
            rows = slice(start - head, start - head + q)
            xs.append(normed(columns[:, :, :, rows], inverses[:, :, rows]))

    def hidden_of(t):
        units = []
        parts = ordered(sums[t]) if 0 < t == chunks - 1 else sums[t]
        for own, others in parts:
            acts = own
            for other in others:
                acts = acts + other.astype(F32)
            units.append((jax.nn.silu(acts[0]) * acts[1]).astype(BF16))
            if t == 0 and rest is not None and len(units) == 1:
                rest_of(units[0])
        units = jnp.concatenate(units, axis=1)
        hidden[t] = [units] + [shift(units, "rows", owners, hop) for hop in range(1, owners)]
        last.append(units)

    def ordered(values):
        return after(values, last[0])

    def at_once(t):
        return t == chunks - 1 and ranks == 4

    def down_of(t):
        total, going = down(rank, [[units] for units in hidden[t]], down_weight, members, order, list(last))
        last[:] = [total]
        if at_once(t):
            block = total.shape[0] // 2
            far = total[block:].astype(BF16)
            arrived = [
                swap(part, "hid", ranks, offset)
                for part, offset in ((going[block:], 3), (far, 2), (going[:block], 1))
            ]
            layer[t] = (total[:block], arrived)
        else:
            layer[t] = (total, swap(going, "hid", ranks, 1))

    def halve_of(t):
        if at_once(t):
            return
        total, arrived = ordered(layer[t])
        for bit in reversed(bits[:-1]):
            total = total + arrived.astype(F32)
            kept = total.shape[0] // 2
            going = total[kept:].astype(BF16)
            last.append(going)
            total, arrived = total[:kept], swap(going, "hid", ranks, bit)
        layer[t] = (total, arrived)

    def settle_of(t):
        total, arrived = ordered(layer[t])
        for part in arrived if at_once(t) else [arrived]:
            total = total + part.astype(F32)
        block = total.astype(BF16)
        last.append(block)
        if at_once(t):
            blocks[t] = [block] + [swap(block, "hid", ranks, offset) for offset in (1, 2, 3)]
        else:
            layer[t] = (block, swap(block, "hid", ranks, bits[0]))

    def double_of(t):
        if at_once(t):
            return
        near, far = ordered(layer[t])
        if t > 0:
            near, far = after((near, far), sums[t - 1][0])
        elif chunks > 1:
            near, far = after((near, far), hidden[1])
        for bit in bits[1:]:
            near = jnp.concatenate((near, far))
            last.append(near)
            far = swap(near, "hid", ranks, bit)
        blocks[t] = (near, far)

    def features_of(t):
        near_far = blocks[t]
        if at_once(t):
            parts = ordered(near_far) if t else near_far
            near_far = (jnp.concatenate(parts[0::2]), jnp.concatenate(parts[1::2]))
        own, *sends = encode(rank, *near_far, enc_weight, members, order, list(last))
        last[:] = [own]
        sums[t] = (own, [send(sends[hop - 1], "mp", members, hop) for hop in range(1, members)])

    def share_of(t):
        total, others = ordered(sums[t])
        for other in others:
            total = total + other.astype(F32)
        q = sizes[t]
        others = []
        for hop in range(1, owners):
            going = total[hop * q : (hop + 1) * q].astype(BF16)
            last.append(going)
            others.append(send(going, "rows", owners, hop))
        sums[t] = (total[:q], others)

    def shared_of(t):
        last.extend(sums[t][1])

    def finish_of(t):
        pre, others = sums[t]
        for other in others:
            pre = pre + other.astype(F32)
        pre = pre + enc_bias[None, :]
        factor = adjoint[starts[t] : starts[t] + sizes[t]].astype(F32)
        outs[t] = (jnp.maximum(pre, 0.0) * factor).astype(BF16)

    stages = (
        (gate_up_of, 0), (hidden_of, 0), (gate_up_of, 1), (down_of, 0), (halve_of, 0),
        (hidden_of, 1), (settle_of, 0), (gate_up_of, 2), (double_of, 0), (down_of, 1),
        (features_of, 0), (hidden_of, 2), (halve_of, 1), (settle_of, 1), (down_of, 2),
        (share_of, 0), (settle_of, 2), (double_of, 1), (shared_of, 0), (features_of, 1),
        (features_of, 2), (share_of, 1), (share_of, 2), (finish_of, 0), (finish_of, 1),
        (finish_of, 2),
    )
    for stage, t in stages:
        if t < chunks:
            stage(t)
    return jnp.concatenate([outs[t] for t in range(chunks)], axis=0)


def solution(mesh):
    placed = (
        P(("groups", "rows"), "hid"),
        P("mp", None),
        P("mp", "rows", "hid"),
        P("mp", "rows", "hid"),
        P("mp", "hid", "rows"),
        P("mp", "rows", "hid"),
        P("hid"),
        P(("groups", "rows", "mp"), "hid"),
    )
    sizes = (mesh.shape["rows"], mesh.shape["mp"], mesh.shape["hid"])
    return jax.shard_map(
        functools.partial(on_device, *sizes),
        mesh=mesh,
        in_specs=placed,
        out_specs=P(("groups", "rows", "mp"), "hid"),
        check_vma=False,
    )
```

```python
import functools

import jax
import jax.numpy as jnp
from jax import lax
from jax.experimental import pallas as pl
from jax.experimental.pallas import tpu as pltpu
from jax.sharding import PartitionSpec as P

BF16 = jnp.bfloat16
F32 = jnp.float32
VMEM_BYTES = 51 * 1024 * 1024
GATE_UP_VMEM_BYTES = 44 * 1024 * 1024
BUFFERS = 4


def shift(value, axis, size, hop):
    return lax.ppermute(value, axis, [((d + hop) % size, d) for d in range(size)])


def send(value, axis, size, hop):
    return lax.ppermute(value, axis, [(d, (d + hop) % size) for d in range(size)])


def swap(value, axis, size, bit):
    return lax.ppermute(value, axis, [(d, d ^ bit) for d in range(size)])


def doubling(size):
    bits = [1 << at for at in reversed(range(size.bit_length() - 1))]
    order = [0]
    for bit in bits:
        order = order + [offset ^ bit for offset in order]
    return bits, order


def tile_of(width, most):
    tile = most
    while tile > 128 and width % tile:
        tile //= 2
    return tile if width % tile == 0 else width


def whole(shape):
    return pl.BlockSpec(shape, lambda j, *_: (0,) * len(shape))


def slots_of(tiles):
    return min(BUFFERS, tiles)


def slots(depth, tile, tiles):
    count = slots_of(tiles)
    return [pltpu.VMEM((count, depth, tile), BF16), pltpu.SemaphoreType.DMA((count,))]


def next_block(weight_ref, slot_ref, slot_sems, tiles, first=0):
    step = pl.program_id(0)
    count, _, tile = slot_ref.shape

    def copy(block, slot):
        columns = pl.ds(pl.multiple_of((first + block) * tile, 128), tile)
        return pltpu.make_async_copy(
            weight_ref.at[0, :, columns], slot_ref.at[slot], slot_sems.at[slot]
        )

    @pl.when(step == 0)
    def _():
        for block in range(count - 1):
            copy(block, block).start()

    ahead = step + count - 1

    @pl.when(ahead < tiles)
    def _():
        copy(ahead, lax.rem(ahead, count)).start()

    slot = lax.rem(step, count)
    copy(step, slot).wait()
    return slot_ref.at[slot]


def in_hbm(count):
    return [pl.BlockSpec(memory_space=pltpu.HBM)] * count


def unread(after):
    return [pl.BlockSpec(memory_space=pl.ANY)] * len(after)


def params(vmem_bytes=VMEM_BYTES):
    return pltpu.CompilerParams(
        dimension_semantics=("arbitrary",), vmem_limit_bytes=vmem_bytes
    )


NO_COST = pl.CostEstimate(flops=1, bytes_accessed=1, transcendentals=0)


def gate_up_body(tiles, first, x_ref, gate_ref, up_ref, *refs):
    members, owners, cuts, q, cut = x_ref.shape
    out_refs = refs[-5 - owners : -5]
    lhs_ref = refs[-5]
    blocks = [
        next_block(gate_ref, refs[-4], refs[-3], tiles, first),
        next_block(up_ref, refs[-2], refs[-1], tiles, first),
    ]

    @pl.when(pl.program_id(0) == 0)
    def _():
        for owner in range(owners):
            for member in range(members):
                row = (owner * members + member) * q
                for at in range(cuts):
                    lhs_ref[row : row + q, at * cut : (at + 1) * cut] = x_ref[member, owner, at]

    rows = members * q
    for at, block_ref in enumerate(blocks):
        acts = jnp.dot(lhs_ref[...], block_ref[...], preferred_element_type=F32)
        for hop in range(owners):
            taken = acts[hop * rows : (hop + 1) * rows]
            out_refs[hop][at] = taken.astype(out_refs[hop].dtype)


def gate_up(x, gate_weight, up_weight, first, tiles, after):
    members, owners, cuts, q, cut = x.shape
    rows, depth, own_rows = members * owners * q, cuts * cut, members * q
    tile = tile_of(gate_weight.shape[2], 256)
    width = tiles * tile
    return pl.pallas_call(
        functools.partial(gate_up_body, tiles, first),
        grid=(tiles,),
        in_specs=[whole(x.shape)] + in_hbm(2) + unread(after),
        out_specs=[pl.BlockSpec((2, own_rows, tile), lambda j: (0, 0, j))] * owners,
        out_shape=[jax.ShapeDtypeStruct((2, own_rows, width), F32)]
        + [jax.ShapeDtypeStruct((2, own_rows, width), BF16)] * (owners - 1),
        scratch_shapes=[pltpu.VMEM((rows, depth), BF16)] + slots(depth, tile, tiles) * 2,
        compiler_params=params(GATE_UP_VMEM_BYTES),
        cost_estimate=NO_COST,
    )(x, gate_weight, up_weight, *after)


def down_body(owners, members, pieces, order, tiles, rank_ref, *refs):
    hidden_refs = refs[: owners * pieces]
    weight_ref = refs[owners * pieces]
    out_refs = refs[-6:-4]
    lhs_ref, acc_ref, slot_ref, slot_sems = refs[-4:]
    block_ref = next_block(weight_ref, slot_ref, slot_sems, tiles)
    q = hidden_refs[0].shape[0] // members
    part = hidden_refs[0].shape[1]
    block = acc_ref.shape[0] // len(order)

    @pl.when(pl.program_id(0) == 0)
    def _():
        for owner in range(owners):
            for piece in range(pieces):
                for member in range(members):
                    row = (member * owners + owner) * q
                    lhs_ref[row : row + q, piece * part : (piece + 1) * part] = hidden_refs[
                        owner * pieces + piece
                    ][member * q : (member + 1) * q]

    acc_ref[...] = jnp.dot(lhs_ref[...], block_ref[...], preferred_element_type=F32)
    half = len(order) // 2
    for slot, offset in enumerate(order):
        at = (rank_ref[0] ^ offset) * block
        taken = acc_ref[pl.ds(pl.multiple_of(at, block), block), :]
        out_ref = out_refs[slot // half]
        row = (slot % half) * block
        out_ref[row : row + block] = taken.astype(out_ref.dtype)


def down(rank, hidden, down_weight, members, order, after):
    owners, pieces = len(hidden), len(hidden[0])
    rows_each, part = hidden[0][0].shape
    rows, depth, width = owners * rows_each, pieces * part, down_weight.shape[2]
    tile = tile_of(width, 256)
    return pl.pallas_call(
        functools.partial(down_body, owners, members, pieces, order, width // tile),
        grid_spec=pltpu.PrefetchScalarGridSpec(
            num_scalar_prefetch=1,
            grid=(width // tile,),
            in_specs=[whole((rows_each, part))] * (owners * pieces)
            + in_hbm(1)
            + unread(after),
            out_specs=[pl.BlockSpec((rows // 2, tile), lambda j, *_: (0, j))] * 2,
            scratch_shapes=[pltpu.VMEM((rows, depth), BF16), pltpu.VMEM((rows, tile), F32)]
            + slots(depth, tile, width // tile),
        ),
        out_shape=[jax.ShapeDtypeStruct((rows // 2, width), kind) for kind in (F32, BF16)],
        compiler_params=params(),
        cost_estimate=NO_COST,
    )(rank, *[piece for of_owner in hidden for piece in of_owner], down_weight, *after)


def encode_body(members, order, tiles, rank_ref, near_ref, far_ref, weight_ref, *refs):
    out_refs = refs[-3 - members : -3]
    lhs_ref, slot_ref, slot_sems = refs[-3:]
    weight_block = next_block(weight_ref, slot_ref, slot_sems, tiles)
    block = lhs_ref.shape[0] // len(order)
    half = len(order) // 2

    @pl.when(pl.program_id(0) == 0)
    def _():
        for slot, offset in enumerate(order):
            at = (rank_ref[0] ^ offset) * block
            row = (slot % half) * block
            from_ref = far_ref if slot >= half else near_ref
            lhs_ref[pl.ds(pl.multiple_of(at, block), block), :] = from_ref[row : row + block]

    pre = jnp.dot(lhs_ref[...], weight_block[...], preferred_element_type=F32)
    rows = pre.shape[0] // members
    for member in range(members):
        taken = pre[member * rows : (member + 1) * rows]
        out_refs[member][...] = taken.astype(out_refs[member].dtype)


def encode(rank, near, far, enc_weight, members, order, after):
    rows, depth = 2 * near.shape[0], near.shape[1]
    width = enc_weight.shape[2]
    rows_each = rows // members
    tile = tile_of(width, 512)
    return pl.pallas_call(
        functools.partial(encode_body, members, order, width // tile),
        grid_spec=pltpu.PrefetchScalarGridSpec(
            num_scalar_prefetch=1,
            grid=(width // tile,),
            in_specs=[whole(near.shape)] * 2 + in_hbm(1) + unread(after),
            out_specs=[pl.BlockSpec((rows_each, tile), lambda j, *_: (0, j))] * members,
            scratch_shapes=[pltpu.VMEM((rows, depth), BF16)] + slots(depth, tile, width // tile),
        ),
        out_shape=[jax.ShapeDtypeStruct((rows_each, width), F32)]
        + [jax.ShapeDtypeStruct((rows_each, width), BF16)] * (members - 1),
        compiler_params=params(),
        cost_estimate=NO_COST,
    )(rank, near, far, enc_weight, *after)


def chunk_rows(total, unit):
    units = total // unit
    if units < 8:
        return [total]
    most = 3 * (units // 8)
    return [most * unit, most * unit, (units - 2 * most) * unit]


def on_device(
    owners, members, ranks, tokens, norm_gain, gate_weight, up_weight, down_weight, enc_weight,
    enc_bias, adjoint,
):
    row_at = lax.axis_index("rows")
    member_at = lax.axis_index("mp")
    rank_at = lax.axis_index("hid")
    rank = rank_at.astype(jnp.int32).reshape(1)
    per_device = adjoint.shape[0]
    cut = tokens.shape[1]
    half_cuts = ranks // owners
    model_width = cut * ranks

    gain = lax.dynamic_slice_in_dim(
        norm_gain[0], row_at * (model_width // owners), model_width // owners, 0
    ).reshape(half_cuts, 1, cut)
    own_tokens = lax.dynamic_slice_in_dim(tokens, member_at * per_device, per_device, 0)

    bits, order = doubling(ranks)

    def from_all(value, axis, size):
        return jnp.stack([value] + [shift(value, axis, size, hop) for hop in range(1, size)])

    def place_of(offset):
        place = 0
        for at in range(len(bits)):
            place = place + ((offset >> at) & 1) * bits[at]
        return place

    def after(values, others):
        return lax.optimization_barrier((values, others))[0]

    def doubled(gathered, bit):
        return jnp.concatenate((gathered, swap(gathered, "hid", ranks, bit)))

    def from_owners(gathered):
        wide = gathered.astype(F32)
        squares = jnp.sum(wide * wide, axis=(0, 2))
        inverse = lax.rsqrt(squares / model_width + 1e-05)
        columns = []
        for hop in range(owners):
            target = lax.rem(row_at + owners - hop, owners)
            half = jnp.concatenate(
                [
                    lax.dynamic_slice_in_dim(
                        gathered, place_of(rank_at ^ (target * half_cuts + at)), 1, 0
                    )
                    for at in range(half_cuts)
                ]
            )
            columns.append(half if hop == 0 else shift(half, "rows", owners, hop))
        return columns, inverse

    def from_members(columns):
        return from_all(jnp.stack(columns), "mp", members)

    def normed(columns, inverses):
        return (columns.astype(F32) * inverses[:, :, None, :, None] * gain).astype(BF16)

    sizes = chunk_rows(per_device, 16 * max(1, ranks // (owners * members)))
    starts = [sum(sizes[:at]) for at in range(len(sizes))]
    chunks = len(sizes)
    head = sizes[0]

    gathered = own_tokens[:head][None]
    for bit in bits:
        gathered = doubled(gathered, bit)
    columns, inverse = from_owners(gathered)
    inverses = from_all(inverse, "rows", owners)
    columns, inverses = after((columns, inverses), (columns, inverses))
    xs = [normed(from_members(columns), from_all(inverses, "mp", members))]
    rest = None
    if chunks > 1:
        rest = after(own_tokens[head:][None], gathered)
        rest = [rest, swap(rest, "hid", ranks, bits[0])]

    sums, hidden, layer, blocks, outs = ({} for _ in range(5))
    last = []

    def gate_up_of(t):
        tiles = gate_weight.shape[2] // tile_of(gate_weight.shape[2], 256)
        early = tiles * 5 // 14 if t == 0 and chunks > 1 else 0
        sums[t] = []
        for first, count in ((0, early), (early, tiles - early)):
            if not count:
                continue
            own, *sends = gate_up(xs[t], gate_weight, up_weight, first, count, list(last))
            last[:] = [own]
            others = [send(sends[hop - 1], "rows", owners, hop) for hop in range(1, owners)]
            sums[t].append((own, others))

    def rest_of(units):
        gathered = jnp.concatenate(after(rest, sums[0][-1][0]))
        for bit in bits[1:]:
            gathered = doubled(after(gathered, sums[0][-1][0]), bit)
        gathered = after(gathered, units)
        columns, inverse = from_owners(gathered)
        inverses = from_all(inverse, "rows", owners)
        columns, inverses = after((columns, inverses), (columns, inverses))
        columns, inverses = from_members(columns), from_all(inverses, "mp", members)
        for start, q in zip(starts[1:], sizes[1:]):
            rows = slice(start - head, start - head + q)
            xs.append(normed(columns[:, :, :, rows], inverses[:, :, rows]))

    def hidden_of(t):
        units = []
        parts = ordered(sums[t]) if 0 < t == chunks - 1 else sums[t]
        for own, others in parts:
            acts = own
            for other in others:
                acts = acts + other.astype(F32)
            units.append((jax.nn.silu(acts[0]) * acts[1]).astype(BF16))
            if t == 0 and chunks > 1 and len(units) == 1:
                rest_of(units[0])
        units = jnp.concatenate(units, axis=1)
        hidden[t] = [units] + [shift(units, "rows", owners, hop) for hop in range(1, owners)]
        last.append(units)

    def ordered(values):
        return after(values, last[0])

    def at_once(t):
        return t == chunks - 1 and ranks == 4

    def down_of(t):
        total, going = down(rank, [[units] for units in hidden[t]], down_weight, members, order, list(last))
        last[:] = [total]
        if at_once(t):
            block = total.shape[0] // 2
            far = total[block:].astype(BF16)
            arrived = [
                swap(part, "hid", ranks, offset)
                for part, offset in ((going[block:], 3), (far, 2), (going[:block], 1))
            ]
            layer[t] = (total[:block], arrived)
        else:
            layer[t] = (total, swap(going, "hid", ranks, 1))

    def halve_of(t):
        if at_once(t):
            return
        total, arrived = ordered(layer[t])
        if chunks > 1 and t == chunks - 2:
            total, arrived = after((total, arrived), hidden[t + 1][0])
        for bit in reversed(bits[:-1]):
            total = total + arrived.astype(F32)
            kept = total.shape[0] // 2
            going = total[kept:].astype(BF16)
            last.append(going)
            total, arrived = total[:kept], swap(going, "hid", ranks, bit)
        layer[t] = (total, arrived)

    def settle_of(t):
        total, arrived = ordered(layer[t])
        for part in arrived if at_once(t) else [arrived]:
            total = total + part.astype(F32)
        block = total.astype(BF16)
        last.append(block)
        if at_once(t):
            blocks[t] = [block] + [swap(block, "hid", ranks, offset) for offset in (1, 2, 3)]
        else:
            layer[t] = (block, swap(block, "hid", ranks, bits[0]))

    def double_of(t):
        if at_once(t):
            return
        near, far = ordered(layer[t])
        if t > 0:
            near, far = after((near, far), sums[t - 1][0])
        elif chunks > 1:
            near, far = after((near, far), hidden[1])
        for bit in bits[1:]:
            near = jnp.concatenate((near, far))
            last.append(near)
            far = swap(near, "hid", ranks, bit)
        blocks[t] = (near, far)

    def features_of(t):
        near_far = blocks[t]
        if at_once(t):
            parts = ordered(near_far)
            near_far = (jnp.concatenate(parts[0::2]), jnp.concatenate(parts[1::2]))
        own, *sends = encode(rank, *near_far, enc_weight, members, order, list(last))
        last[:] = [own]
        sums[t] = (own, [send(sends[hop - 1], "mp", members, hop) for hop in range(1, members)])

    def share_of(t):
        total, others = ordered(sums[t])
        for other in others:
            total = total + other.astype(F32)
        q = sizes[t]
        others = []
        for hop in range(1, owners):
            going = total[hop * q : (hop + 1) * q].astype(BF16)
            last.append(going)
            others.append(send(going, "rows", owners, hop))
        sums[t] = (total[:q], others)

    def shared_of(t):
        last.extend(sums[t][1])

    def finish_of(t):
        pre, others = sums[t]
        for other in others:
            pre = pre + other.astype(F32)
        pre = pre + enc_bias[None, :]
        factor = adjoint[starts[t] : starts[t] + sizes[t]].astype(F32)
        outs[t] = (jnp.maximum(pre, 0.0) * factor).astype(BF16)

    stages = (
        (gate_up_of, 0), (hidden_of, 0), (gate_up_of, 1), (down_of, 0), (halve_of, 0),
        (hidden_of, 1), (settle_of, 0), (gate_up_of, 2), (double_of, 0), (down_of, 1),
        (features_of, 0), (hidden_of, 2), (halve_of, 1), (settle_of, 1), (down_of, 2),
        (share_of, 0), (settle_of, 2), (double_of, 1), (shared_of, 0), (features_of, 1),
        (features_of, 2), (share_of, 1), (share_of, 2), (finish_of, 0), (finish_of, 1),
        (finish_of, 2),
    )
    for stage, t in stages:
        if t < chunks:
            stage(t)
    return jnp.concatenate([outs[t] for t in range(chunks)], axis=0)


def solution(mesh):
    placed = (
        P(("groups", "rows"), "hid"),
        P("mp", None),
        P("mp", "rows", "hid"),
        P("mp", "rows", "hid"),
        P("mp", "hid", "rows"),
        P("mp", "rows", "hid"),
        P("hid"),
        P(("groups", "rows", "mp"), "hid"),
    )
    sizes = (mesh.shape["rows"], mesh.shape["mp"], mesh.shape["hid"])
    return jax.shard_map(
        functools.partial(on_device, *sizes),
        mesh=mesh,
        in_specs=placed,
        out_specs=P(("groups", "rows", "mp"), "hid"),
        check_vma=False,
    )
```

```python
import functools

import jax
import jax.numpy as jnp
from jax import lax
from jax.experimental import pallas as pl
from jax.experimental.pallas import tpu as pltpu
from jax.sharding import PartitionSpec as P

BF16 = jnp.bfloat16
F32 = jnp.float32
VMEM_BYTES = 51 * 1024 * 1024
GATE_UP_VMEM_BYTES = 44 * 1024 * 1024
BUFFERS = 3


def shift(value, axis, size, hop):
    return lax.ppermute(value, axis, [((d + hop) % size, d) for d in range(size)])


def send(value, axis, size, hop):
    return lax.ppermute(value, axis, [(d, (d + hop) % size) for d in range(size)])


def swap(value, axis, size, bit):
    return lax.ppermute(value, axis, [(d, d ^ bit) for d in range(size)])


def doubling(size):
    bits = [1 << at for at in reversed(range(size.bit_length() - 1))]
    order = [0]
    for bit in bits:
        order = order + [offset ^ bit for offset in order]
    return bits, order


def tile_of(width, most):
    tile = most
    while tile > 128 and width % tile:
        tile //= 2
    return tile if width % tile == 0 else width


def whole(shape):
    return pl.BlockSpec(shape, lambda j, *_: (0,) * len(shape))


def slots_of(tiles):
    return min(BUFFERS, tiles)


def slots(depth, tile, tiles):
    count = slots_of(tiles)
    return [pltpu.VMEM((count, depth, tile), BF16), pltpu.SemaphoreType.DMA((count,))]


def next_block(weight_ref, slot_ref, slot_sems, tiles, first=0):
    step = pl.program_id(0)
    count, _, tile = slot_ref.shape

    def copy(block, slot):
        columns = pl.ds(pl.multiple_of((first + block) * tile, 128), tile)
        return pltpu.make_async_copy(
            weight_ref.at[0, :, columns], slot_ref.at[slot], slot_sems.at[slot]
        )

    @pl.when(step == 0)
    def _():
        for block in range(count - 1):
            copy(block, block).start()

    ahead = step + count - 1

    @pl.when(ahead < tiles)
    def _():
        copy(ahead, lax.rem(ahead, count)).start()

    slot = lax.rem(step, count)
    copy(step, slot).wait()
    return slot_ref.at[slot]


def in_hbm(count):
    return [pl.BlockSpec(memory_space=pltpu.HBM)] * count


def unread(after):
    return [pl.BlockSpec(memory_space=pl.ANY)] * len(after)


def params(vmem_bytes=VMEM_BYTES):
    return pltpu.CompilerParams(
        dimension_semantics=("arbitrary",), vmem_limit_bytes=vmem_bytes
    )


NO_COST = pl.CostEstimate(flops=1, bytes_accessed=1, transcendentals=0)


def gate_up_body(tiles, first, x_ref, gate_ref, up_ref, *refs):
    members, owners, cuts, q, cut = x_ref.shape
    out_refs = refs[-5 - owners : -5]
    lhs_ref = refs[-5]
    blocks = [
        next_block(gate_ref, refs[-4], refs[-3], tiles, first),
        next_block(up_ref, refs[-2], refs[-1], tiles, first),
    ]

    @pl.when(pl.program_id(0) == 0)
    def _():
        for owner in range(owners):
            for member in range(members):
                row = (owner * members + member) * q
                for at in range(cuts):
                    lhs_ref[row : row + q, at * cut : (at + 1) * cut] = x_ref[member, owner, at]

    rows = members * q
    for at, block_ref in enumerate(blocks):
        acts = jnp.dot(lhs_ref[...], block_ref[...], preferred_element_type=F32)
        for hop in range(owners):
            taken = acts[hop * rows : (hop + 1) * rows]
            out_refs[hop][at] = taken.astype(out_refs[hop].dtype)


def gate_up(x, gate_weight, up_weight, first, tiles, after):
    members, owners, cuts, q, cut = x.shape
    rows, depth, own_rows = members * owners * q, cuts * cut, members * q
    tile = tile_of(gate_weight.shape[2], 256)
    width = tiles * tile
    return pl.pallas_call(
        functools.partial(gate_up_body, tiles, first),
        grid=(tiles,),
        in_specs=[whole(x.shape)] + in_hbm(2) + unread(after),
        out_specs=[pl.BlockSpec((2, own_rows, tile), lambda j: (0, 0, j))] * owners,
        out_shape=[pltpu.HBM((2, own_rows, width), F32)]
        + [jax.ShapeDtypeStruct((2, own_rows, width), BF16)] * (owners - 1),
        scratch_shapes=[pltpu.VMEM((rows, depth), BF16)] + slots(depth, tile, tiles) * 2,
        compiler_params=params(GATE_UP_VMEM_BYTES),
        cost_estimate=NO_COST,
    )(x, gate_weight, up_weight, *after)


def down_body(owners, members, pieces, order, tiles, rank_ref, *refs):
    hidden_refs = refs[: owners * pieces]
    weight_ref = refs[owners * pieces]
    out_refs = refs[-6:-4]
    lhs_ref, acc_ref, slot_ref, slot_sems = refs[-4:]
    block_ref = next_block(weight_ref, slot_ref, slot_sems, tiles)
    q = hidden_refs[0].shape[0] // members
    part = hidden_refs[0].shape[1]
    block = acc_ref.shape[0] // len(order)

    @pl.when(pl.program_id(0) == 0)
    def _():
        for owner in range(owners):
            for piece in range(pieces):
                for member in range(members):
                    row = (member * owners + owner) * q
                    lhs_ref[row : row + q, piece * part : (piece + 1) * part] = hidden_refs[
                        owner * pieces + piece
                    ][member * q : (member + 1) * q]

    acc_ref[...] = jnp.dot(lhs_ref[...], block_ref[...], preferred_element_type=F32)
    half = len(order) // 2
    for slot, offset in enumerate(order):
        at = (rank_ref[0] ^ offset) * block
        taken = acc_ref[pl.ds(pl.multiple_of(at, block), block), :]
        out_ref = out_refs[slot // half]
        row = (slot % half) * block
        out_ref[row : row + block] = taken.astype(out_ref.dtype)


def down(rank, hidden, down_weight, members, order, after):
    owners, pieces = len(hidden), len(hidden[0])
    rows_each, part = hidden[0][0].shape
    rows, depth, width = owners * rows_each, pieces * part, down_weight.shape[2]
    tile = tile_of(width, 256)
    return pl.pallas_call(
        functools.partial(down_body, owners, members, pieces, order, width // tile),
        grid_spec=pltpu.PrefetchScalarGridSpec(
            num_scalar_prefetch=1,
            grid=(width // tile,),
            in_specs=[whole((rows_each, part))] * (owners * pieces)
            + in_hbm(1)
            + unread(after),
            out_specs=[pl.BlockSpec((rows // 2, tile), lambda j, *_: (0, j))] * 2,
            scratch_shapes=[pltpu.VMEM((rows, depth), BF16), pltpu.VMEM((rows, tile), F32)]
            + slots(depth, tile, width // tile),
        ),
        out_shape=[jax.ShapeDtypeStruct((rows // 2, width), kind) for kind in (F32, BF16)],
        compiler_params=params(),
        cost_estimate=NO_COST,
    )(rank, *[piece for of_owner in hidden for piece in of_owner], down_weight, *after)


def encode_body(members, order, tiles, rank_ref, near_ref, far_ref, weight_ref, *refs):
    out_refs = refs[-3 - members : -3]
    lhs_ref, slot_ref, slot_sems = refs[-3:]
    weight_block = next_block(weight_ref, slot_ref, slot_sems, tiles)
    block = lhs_ref.shape[0] // len(order)
    half = len(order) // 2

    @pl.when(pl.program_id(0) == 0)
    def _():
        for slot, offset in enumerate(order):
            at = (rank_ref[0] ^ offset) * block
            row = (slot % half) * block
            from_ref = far_ref if slot >= half else near_ref
            lhs_ref[pl.ds(pl.multiple_of(at, block), block), :] = from_ref[row : row + block]

    pre = jnp.dot(lhs_ref[...], weight_block[...], preferred_element_type=F32)
    rows = pre.shape[0] // members
    for member in range(members):
        taken = pre[member * rows : (member + 1) * rows]
        out_refs[member][...] = taken.astype(out_refs[member].dtype)


def encode(rank, near, far, enc_weight, members, order, after):
    rows, depth = 2 * near.shape[0], near.shape[1]
    width = enc_weight.shape[2]
    rows_each = rows // members
    tile = tile_of(width, 512)
    return pl.pallas_call(
        functools.partial(encode_body, members, order, width // tile),
        grid_spec=pltpu.PrefetchScalarGridSpec(
            num_scalar_prefetch=1,
            grid=(width // tile,),
            in_specs=[whole(near.shape)] * 2 + in_hbm(1) + unread(after),
            out_specs=[pl.BlockSpec((rows_each, tile), lambda j, *_: (0, j))] * members,
            scratch_shapes=[pltpu.VMEM((rows, depth), BF16)] + slots(depth, tile, width // tile),
        ),
        out_shape=[jax.ShapeDtypeStruct((rows_each, width), F32)]
        + [jax.ShapeDtypeStruct((rows_each, width), BF16)] * (members - 1),
        compiler_params=params(),
        cost_estimate=NO_COST,
    )(rank, near, far, enc_weight, *after)


def chunk_rows(total, unit):
    units = total // unit
    if units < 8:
        return [total]
    most = 3 * (units // 8)
    return [most * unit, most * unit, (units - 2 * most) * unit]


def on_device(
    owners, members, ranks, tokens, norm_gain, gate_weight, up_weight, down_weight, enc_weight,
    enc_bias, adjoint,
):
    row_at = lax.axis_index("rows")
    member_at = lax.axis_index("mp")
    rank_at = lax.axis_index("hid")
    rank = rank_at.astype(jnp.int32).reshape(1)
    per_device = adjoint.shape[0]
    cut = tokens.shape[1]
    half_cuts = ranks // owners
    model_width = cut * ranks

    gain = lax.dynamic_slice_in_dim(
        norm_gain[0], row_at * (model_width // owners), model_width // owners, 0
    ).reshape(half_cuts, 1, cut)
    own_tokens = lax.dynamic_slice_in_dim(tokens, member_at * per_device, per_device, 0)

    bits, order = doubling(ranks)

    def from_all(value, axis, size):
        return jnp.stack([value] + [shift(value, axis, size, hop) for hop in range(1, size)])

    def place_of(offset):
        place = 0
        for at in range(len(bits)):
            place = place + ((offset >> at) & 1) * bits[at]
        return place

    def after(values, others):
        return lax.optimization_barrier((values, others))[0]

    def doubled(gathered, bit):
        return jnp.concatenate((gathered, swap(gathered, "hid", ranks, bit)))

    def from_owners(gathered):
        wide = gathered.astype(F32)
        squares = jnp.sum(wide * wide, axis=(0, 2))
        inverse = lax.rsqrt(squares / model_width + 1e-05)
        columns = []
        for hop in range(owners):
            target = lax.rem(row_at + owners - hop, owners)
            half = jnp.concatenate(
                [
                    lax.dynamic_slice_in_dim(
                        gathered, place_of(rank_at ^ (target * half_cuts + at)), 1, 0
                    )
                    for at in range(half_cuts)
                ]
            )
            columns.append(half if hop == 0 else shift(half, "rows", owners, hop))
        return columns, inverse

    def from_members(columns):
        return from_all(jnp.stack(columns), "mp", members)

    def normed(columns, inverses):
        return (columns.astype(F32) * inverses[:, :, None, :, None] * gain).astype(BF16)

    sizes = chunk_rows(per_device, 16 * max(1, ranks // (owners * members)))
    starts = [sum(sizes[:at]) for at in range(len(sizes))]
    chunks = len(sizes)
    head = sizes[0]

    gathered = own_tokens[:head][None]
    for bit in bits:
        gathered = doubled(gathered, bit)
    columns, inverse = from_owners(gathered)
    inverses = from_all(inverse, "rows", owners)
    columns, inverses = after((columns, inverses), (columns, inverses))
    xs = [normed(from_members(columns), from_all(inverses, "mp", members))]
    rest = None
    if chunks > 1:
        rest = after(own_tokens[head:][None], gathered)
        rest = [rest, swap(rest, "hid", ranks, bits[0])]

    sums, hidden, layer, blocks, outs = ({} for _ in range(5))
    last = []

    def gate_up_of(t):
        tiles = gate_weight.shape[2] // tile_of(gate_weight.shape[2], 256)
        early = tiles * 5 // 14 if t == 0 and chunks > 1 else 0
        sums[t] = []
        for first, count in ((0, early), (early, tiles - early)):
            if not count:
                continue
            own, *sends = gate_up(xs[t], gate_weight, up_weight, first, count, list(last))
            last[:] = [own]
            others = [send(sends[hop - 1], "rows", owners, hop) for hop in range(1, owners)]
            sums[t].append((own, others))

    def rest_of(units):
        gathered = jnp.concatenate(after(rest, sums[0][-1][0]))
        for bit in bits[1:]:
            gathered = doubled(after(gathered, sums[0][-1][0]), bit)
        gathered = after(gathered, units)
        columns, inverse = from_owners(gathered)
        inverses = from_all(inverse, "rows", owners)
        columns, inverses = after((columns, inverses), (columns, inverses))
        columns, inverses = from_members(columns), from_all(inverses, "mp", members)
        for start, q in zip(starts[1:], sizes[1:]):
            rows = slice(start - head, start - head + q)
            xs.append(normed(columns[:, :, :, rows], inverses[:, :, rows]))

    def hidden_of(t):
        units = []
        parts = ordered(sums[t]) if 0 < t == chunks - 1 else sums[t]
        for own, others in parts:
            acts = own
            for other in others:
                acts = acts + other.astype(F32)
            units.append((jax.nn.silu(acts[0]) * acts[1]).astype(BF16))
            if t == 0 and chunks > 1 and len(units) == 1:
                rest_of(units[0])
        units = jnp.concatenate(units, axis=1)
        hidden[t] = [units] + [shift(units, "rows", owners, hop) for hop in range(1, owners)]
        last.append(units)

    def ordered(values):
        return after(values, last[0])

    def at_once(t):
        return t == chunks - 1 and ranks == 4

    def down_of(t):
        total, going = down(rank, [[units] for units in hidden[t]], down_weight, members, order, list(last))
        last[:] = [total]
        if at_once(t):
            block = total.shape[0] // 2
            far = total[block:].astype(BF16)
            arrived = [
                swap(part, "hid", ranks, offset)
                for part, offset in ((going[block:], 3), (far, 2), (going[:block], 1))
            ]
            layer[t] = (total[:block], arrived)
        else:
            layer[t] = (total, swap(going, "hid", ranks, 1))

    def halve_of(t):
        if at_once(t):
            return
        total, arrived = ordered(layer[t])
        if chunks > 1 and t == chunks - 2:
            total, arrived = after((total, arrived), hidden[t + 1][0])
        for bit in reversed(bits[:-1]):
            total = total + arrived.astype(F32)
            kept = total.shape[0] // 2
            going = total[kept:].astype(BF16)
            last.append(going)
            total, arrived = total[:kept], swap(going, "hid", ranks, bit)
        layer[t] = (total, arrived)

    def settle_of(t):
        total, arrived = ordered(layer[t])
        for part in arrived if at_once(t) else [arrived]:
            total = total + part.astype(F32)
        block = total.astype(BF16)
        last.append(block)
        if at_once(t):
            blocks[t] = [block] + [swap(block, "hid", ranks, offset) for offset in (1, 2, 3)]
        else:
            layer[t] = (block, swap(block, "hid", ranks, bits[0]))

    def double_of(t):
        if at_once(t):
            return
        near, far = ordered(layer[t])
        if t > 0:
            near, far = after((near, far), sums[t - 1][0])
        elif chunks > 1:
            near, far = after((near, far), hidden[1])
        for bit in bits[1:]:
            near = jnp.concatenate((near, far))
            last.append(near)
            far = swap(near, "hid", ranks, bit)
        blocks[t] = (near, far)

    def features_of(t):
        near_far = blocks[t]
        if at_once(t):
            parts = ordered(near_far)
            near_far = (jnp.concatenate(parts[0::2]), jnp.concatenate(parts[1::2]))
        own, *sends = encode(rank, *near_far, enc_weight, members, order, list(last))
        last[:] = [own]
        sums[t] = (own, [send(sends[hop - 1], "mp", members, hop) for hop in range(1, members)])

    def share_of(t):
        total, others = ordered(sums[t])
        for other in others:
            total = total + other.astype(F32)
        q = sizes[t]
        others = []
        for hop in range(1, owners):
            going = total[hop * q : (hop + 1) * q].astype(BF16)
            last.append(going)
            others.append(send(going, "rows", owners, hop))
        sums[t] = (total[:q], others)

    def shared_of(t):
        last.extend(sums[t][1])

    def finish_of(t):
        pre, others = sums[t]
        for other in others:
            pre = pre + other.astype(F32)
        pre = pre + enc_bias[None, :]
        factor = adjoint[starts[t] : starts[t] + sizes[t]].astype(F32)
        outs[t] = (jnp.maximum(pre, 0.0) * factor).astype(BF16)

    stages = (
        (gate_up_of, 0), (hidden_of, 0), (gate_up_of, 1), (down_of, 0), (halve_of, 0),
        (hidden_of, 1), (settle_of, 0), (gate_up_of, 2), (double_of, 0), (down_of, 1),
        (features_of, 0), (hidden_of, 2), (halve_of, 1), (settle_of, 1), (down_of, 2),
        (share_of, 0), (settle_of, 2), (double_of, 1), (shared_of, 0), (features_of, 1),
        (features_of, 2), (share_of, 1), (share_of, 2), (finish_of, 0), (finish_of, 1),
        (finish_of, 2),
    )
    for stage, t in stages:
        if t < chunks:
            stage(t)
    gated = jnp.zeros(adjoint.shape, BF16)
    for t in range(chunks):
        gated = lax.dynamic_update_slice(gated, outs[t], (starts[t], 0))
    return gated


def solution(mesh):
    placed = (
        P(("groups", "rows"), "hid"),
        P("mp", None),
        P("mp", "rows", "hid"),
        P("mp", "rows", "hid"),
        P("mp", "hid", "rows"),
        P("mp", "rows", "hid"),
        P("hid"),
        P(("groups", "rows", "mp"), "hid"),
    )
    sizes = (mesh.shape["rows"], mesh.shape["mp"], mesh.shape["hid"])
    return jax.shard_map(
        functools.partial(on_device, *sizes),
        mesh=mesh,
        in_specs=placed,
        out_specs=P(("groups", "rows", "mp"), "hid"),
        check_vma=False,
    )
```

```python
import functools

import jax
import jax.numpy as jnp
from jax import lax
from jax.experimental import pallas as pl
from jax.experimental.pallas import tpu as pltpu
from jax.sharding import PartitionSpec as P

BF16 = jnp.bfloat16
F32 = jnp.float32
VMEM_BYTES = 51 * 1024 * 1024
GATE_UP_VMEM_BYTES = 44 * 1024 * 1024
BUFFERS = 8


def shift(value, axis, size, hop):
    return lax.ppermute(value, axis, [((d + hop) % size, d) for d in range(size)])


def send(value, axis, size, hop):
    return lax.ppermute(value, axis, [(d, (d + hop) % size) for d in range(size)])


def swap(value, axis, size, bit):
    return lax.ppermute(value, axis, [(d, d ^ bit) for d in range(size)])


def doubling(size):
    bits = [1 << at for at in reversed(range(size.bit_length() - 1))]
    order = [0]
    for bit in bits:
        order = order + [offset ^ bit for offset in order]
    return bits, order


def tile_of(width, most):
    tile = most
    while tile > 128 and width % tile:
        tile //= 2
    return tile if width % tile == 0 else width


def whole(shape):
    return pl.BlockSpec(shape, lambda j, *_: (0,) * len(shape))


def slots_of(tiles):
    return min(BUFFERS, tiles)


def slots(depth, tile, tiles):
    count = slots_of(tiles)
    return [pltpu.VMEM((count, depth, tile), BF16), pltpu.SemaphoreType.DMA((count,))]


def next_block(weight_ref, slot_ref, slot_sems, tiles, first=0):
    step = pl.program_id(0)
    count, _, tile = slot_ref.shape

    def copy(block, slot):
        columns = pl.ds(pl.multiple_of((first + block) * tile, 128), tile)
        return pltpu.make_async_copy(
            weight_ref.at[0, :, columns], slot_ref.at[slot], slot_sems.at[slot]
        )

    @pl.when(step == 0)
    def _():
        for block in range(count - 1):
            copy(block, block).start()

    ahead = step + count - 1

    @pl.when(ahead < tiles)
    def _():
        copy(ahead, lax.rem(ahead, count)).start()

    slot = lax.rem(step, count)
    copy(step, slot).wait()
    return slot_ref.at[slot]


def in_hbm(count):
    return [pl.BlockSpec(memory_space=pltpu.HBM)] * count


def unread(after):
    return [pl.BlockSpec(memory_space=pl.ANY)] * len(after)


def params(vmem_bytes=VMEM_BYTES):
    return pltpu.CompilerParams(
        dimension_semantics=("arbitrary",), vmem_limit_bytes=vmem_bytes
    )


NO_COST = pl.CostEstimate(flops=1, bytes_accessed=1, transcendentals=0)


def gate_up_body(tiles, first, x_ref, gate_ref, up_ref, *refs):
    members, owners, cuts, q, cut = x_ref.shape
    out_refs = refs[-5 - owners : -5]
    lhs_ref = refs[-5]
    blocks = [
        next_block(gate_ref, refs[-4], refs[-3], tiles, first),
        next_block(up_ref, refs[-2], refs[-1], tiles, first),
    ]

    @pl.when(pl.program_id(0) == 0)
    def _():
        for owner in range(owners):
            for member in range(members):
                row = (owner * members + member) * q
                for at in range(cuts):
                    lhs_ref[row : row + q, at * cut : (at + 1) * cut] = x_ref[member, owner, at]

    rows = members * q
    for at, block_ref in enumerate(blocks):
        acts = jnp.dot(lhs_ref[...], block_ref[...], preferred_element_type=F32)
        for hop in range(owners):
            taken = acts[hop * rows : (hop + 1) * rows]
            out_refs[hop][at] = taken.astype(out_refs[hop].dtype)


def gate_up(x, gate_weight, up_weight, first, tiles, after):
    members, owners, cuts, q, cut = x.shape
    rows, depth, own_rows = members * owners * q, cuts * cut, members * q
    tile = tile_of(gate_weight.shape[2], 256)
    width = tiles * tile
    return pl.pallas_call(
        functools.partial(gate_up_body, tiles, first),
        grid=(tiles,),
        in_specs=[whole(x.shape)] + in_hbm(2) + unread(after),
        out_specs=[pl.BlockSpec((2, own_rows, tile), lambda j: (0, 0, j))] * owners,
        out_shape=[jax.ShapeDtypeStruct((2, own_rows, width), F32)]
        + [jax.ShapeDtypeStruct((2, own_rows, width), BF16)] * (owners - 1),
        scratch_shapes=[pltpu.VMEM((rows, depth), BF16)] + slots(depth, tile, tiles) * 2,
        compiler_params=params(GATE_UP_VMEM_BYTES),
        cost_estimate=NO_COST,
    )(x, gate_weight, up_weight, *after)


def down_body(owners, members, pieces, order, tiles, rank_ref, *refs):
    hidden_refs = refs[: owners * pieces]
    weight_ref = refs[owners * pieces]
    out_refs = refs[-6:-4]
    lhs_ref, acc_ref, slot_ref, slot_sems = refs[-4:]
    block_ref = next_block(weight_ref, slot_ref, slot_sems, tiles)
    q = hidden_refs[0].shape[0] // members
    part = hidden_refs[0].shape[1]
    block = acc_ref.shape[0] // len(order)

    @pl.when(pl.program_id(0) == 0)
    def _():
        for owner in range(owners):
            for piece in range(pieces):
                for member in range(members):
                    row = (member * owners + owner) * q
                    lhs_ref[row : row + q, piece * part : (piece + 1) * part] = hidden_refs[
                        owner * pieces + piece
                    ][member * q : (member + 1) * q]

    acc_ref[...] = jnp.dot(lhs_ref[...], block_ref[...], preferred_element_type=F32)
    half = len(order) // 2
    for slot, offset in enumerate(order):
        at = (rank_ref[0] ^ offset) * block
        taken = acc_ref[pl.ds(pl.multiple_of(at, block), block), :]
        out_ref = out_refs[slot // half]
        row = (slot % half) * block
        out_ref[row : row + block] = taken.astype(out_ref.dtype)


def down(rank, hidden, down_weight, members, order, after):
    owners, pieces = len(hidden), len(hidden[0])
    rows_each, part = hidden[0][0].shape
    rows, depth, width = owners * rows_each, pieces * part, down_weight.shape[2]
    tile = tile_of(width, 256)
    return pl.pallas_call(
        functools.partial(down_body, owners, members, pieces, order, width // tile),
        grid_spec=pltpu.PrefetchScalarGridSpec(
            num_scalar_prefetch=1,
            grid=(width // tile,),
            in_specs=[whole((rows_each, part))] * (owners * pieces)
            + in_hbm(1)
            + unread(after),
            out_specs=[pl.BlockSpec((rows // 2, tile), lambda j, *_: (0, j))] * 2,
            scratch_shapes=[pltpu.VMEM((rows, depth), BF16), pltpu.VMEM((rows, tile), F32)]
            + slots(depth, tile, width // tile),
        ),
        out_shape=[jax.ShapeDtypeStruct((rows // 2, width), kind) for kind in (F32, BF16)],
        compiler_params=params(),
        cost_estimate=NO_COST,
    )(rank, *[piece for of_owner in hidden for piece in of_owner], down_weight, *after)


def encode_body(members, order, tiles, rank_ref, near_ref, far_ref, weight_ref, *refs):
    out_refs = refs[-3 - members : -3]
    lhs_ref, slot_ref, slot_sems = refs[-3:]
    weight_block = next_block(weight_ref, slot_ref, slot_sems, tiles)
    block = lhs_ref.shape[0] // len(order)
    half = len(order) // 2

    @pl.when(pl.program_id(0) == 0)
    def _():
        for slot, offset in enumerate(order):
            at = (rank_ref[0] ^ offset) * block
            row = (slot % half) * block
            from_ref = far_ref if slot >= half else near_ref
            lhs_ref[pl.ds(pl.multiple_of(at, block), block), :] = from_ref[row : row + block]

    pre = jnp.dot(lhs_ref[...], weight_block[...], preferred_element_type=F32)
    rows = pre.shape[0] // members
    for member in range(members):
        taken = pre[member * rows : (member + 1) * rows]
        out_refs[member][...] = taken.astype(out_refs[member].dtype)


def encode(rank, near, far, enc_weight, members, order, after):
    rows, depth = 2 * near.shape[0], near.shape[1]
    width = enc_weight.shape[2]
    rows_each = rows // members
    tile = tile_of(width, 512)
    return pl.pallas_call(
        functools.partial(encode_body, members, order, width // tile),
        grid_spec=pltpu.PrefetchScalarGridSpec(
            num_scalar_prefetch=1,
            grid=(width // tile,),
            in_specs=[whole(near.shape)] * 2 + in_hbm(1) + unread(after),
            out_specs=[pl.BlockSpec((rows_each, tile), lambda j, *_: (0, j))] * members,
            scratch_shapes=[pltpu.VMEM((rows, depth), BF16)] + slots(depth, tile, width // tile),
        ),
        out_shape=[jax.ShapeDtypeStruct((rows_each, width), F32)]
        + [jax.ShapeDtypeStruct((rows_each, width), BF16)] * (members - 1),
        compiler_params=params(),
        cost_estimate=NO_COST,
    )(rank, near, far, enc_weight, *after)


def chunk_rows(total, unit):
    units = total // unit
    if units < 8:
        return [total]
    most = 3 * (units // 8)
    return [most * unit, most * unit, (units - 2 * most) * unit]


def on_device(
    owners, members, ranks, tokens, norm_gain, gate_weight, up_weight, down_weight, enc_weight,
    enc_bias, adjoint,
):
    row_at = lax.axis_index("rows")
    member_at = lax.axis_index("mp")
    rank_at = lax.axis_index("hid")
    rank = rank_at.astype(jnp.int32).reshape(1)
    per_device = adjoint.shape[0]
    cut = tokens.shape[1]
    half_cuts = ranks // owners
    model_width = cut * ranks

    gain = lax.dynamic_slice_in_dim(
        norm_gain[0], row_at * (model_width // owners), model_width // owners, 0
    ).reshape(half_cuts, 1, cut)
    own_tokens = lax.dynamic_slice_in_dim(tokens, member_at * per_device, per_device, 0)

    bits, order = doubling(ranks)

    def from_all(value, axis, size):
        return jnp.stack([value] + [shift(value, axis, size, hop) for hop in range(1, size)])

    def place_of(offset):
        place = 0
        for at in range(len(bits)):
            place = place + ((offset >> at) & 1) * bits[at]
        return place

    def after(values, others):
        return lax.optimization_barrier((values, others))[0]

    def doubled(gathered, bit):
        return jnp.concatenate((gathered, swap(gathered, "hid", ranks, bit)))

    def from_owners(gathered):
        wide = gathered.astype(F32)
        squares = jnp.sum(wide * wide, axis=(0, 2))
        inverse = lax.rsqrt(squares / model_width + 1e-05)
        columns = []
        for hop in range(owners):
            target = lax.rem(row_at + owners - hop, owners)
            half = jnp.concatenate(
                [
                    lax.dynamic_slice_in_dim(
                        gathered, place_of(rank_at ^ (target * half_cuts + at)), 1, 0
                    )
                    for at in range(half_cuts)
                ]
            )
            columns.append(half if hop == 0 else shift(half, "rows", owners, hop))
        return columns, inverse

    def from_members(columns):
        return from_all(jnp.stack(columns), "mp", members)

    def normed(columns, inverses):
        return (columns.astype(F32) * inverses[:, :, None, :, None] * gain).astype(BF16)

    sizes = chunk_rows(per_device, 16 * max(1, ranks // (owners * members)))
    starts = [sum(sizes[:at]) for at in range(len(sizes))]
    chunks = len(sizes)
    head = sizes[0]

    gathered = own_tokens[:head][None]
    for bit in bits:
        gathered = doubled(gathered, bit)
    columns, inverse = from_owners(gathered)
    inverses = from_all(inverse, "rows", owners)
    columns, inverses = after((columns, inverses), (columns, inverses))
    xs = [normed(from_members(columns), from_all(inverses, "mp", members))]
    rest = None
    if chunks > 1:
        rest = after(own_tokens[head:][None], gathered)
        rest = [rest, swap(rest, "hid", ranks, bits[0])]

    sums, hidden, layer, blocks, outs = ({} for _ in range(5))
    last = []

    def gate_up_of(t):
        tiles = gate_weight.shape[2] // tile_of(gate_weight.shape[2], 256)
        early = tiles * 5 // 14 if t == 0 and chunks > 1 else 0
        sums[t] = []
        for first, count in ((0, early), (early, tiles - early)):
            if not count:
                continue
            own, *sends = gate_up(xs[t], gate_weight, up_weight, first, count, list(last))
            last[:] = [own]
            others = [send(sends[hop - 1], "rows", owners, hop) for hop in range(1, owners)]
            sums[t].append((own, others))

    def rest_of(units):
        gathered = jnp.concatenate(after(rest, sums[0][-1][0]))
        for bit in bits[1:]:
            gathered = doubled(after(gathered, sums[0][-1][0]), bit)
        gathered = after(gathered, units)
        columns, inverse = from_owners(gathered)
        inverses = from_all(inverse, "rows", owners)
        columns, inverses = after((columns, inverses), (columns, inverses))
        columns, inverses = from_members(columns), from_all(inverses, "mp", members)
        for start, q in zip(starts[1:], sizes[1:]):
            rows = slice(start - head, start - head + q)
            xs.append(normed(columns[:, :, :, rows], inverses[:, :, rows]))

    def hidden_of(t):
        units = []
        parts = ordered(sums[t]) if 0 < t == chunks - 1 else sums[t]
        for own, others in parts:
            acts = own
            for other in others:
                acts = acts + other.astype(F32)
            units.append((jax.nn.silu(acts[0]) * acts[1]).astype(BF16))
            if t == 0 and chunks > 1 and len(units) == 1:
                rest_of(units[0])
        units = jnp.concatenate(units, axis=1)
        hidden[t] = [units] + [shift(units, "rows", owners, hop) for hop in range(1, owners)]
        last.append(units)

    def ordered(values):
        return after(values, last[0])

    def at_once(t):
        return t == chunks - 1 and ranks == 4

    def down_of(t):
        total, going = down(rank, [[units] for units in hidden[t]], down_weight, members, order, list(last))
        last[:] = [total]
        if at_once(t):
            block = total.shape[0] // 2
            far = total[block:].astype(BF16)
            arrived = [
                swap(part, "hid", ranks, offset)
                for part, offset in ((going[block:], 3), (far, 2), (going[:block], 1))
            ]
            layer[t] = (total[:block], arrived)
        else:
            layer[t] = (total, swap(going, "hid", ranks, 1))

    def halve_of(t):
        if at_once(t):
            return
        total, arrived = ordered(layer[t])
        if chunks > 1 and t == chunks - 2:
            total, arrived = after((total, arrived), hidden[t + 1][0])
        for bit in reversed(bits[:-1]):
            total = total + arrived.astype(F32)
            kept = total.shape[0] // 2
            going = total[kept:].astype(BF16)
            last.append(going)
            total, arrived = total[:kept], swap(going, "hid", ranks, bit)
        layer[t] = (total, arrived)

    def settle_of(t):
        total, arrived = ordered(layer[t])
        for part in arrived if at_once(t) else [arrived]:
            total = total + part.astype(F32)
        block = total.astype(BF16)
        last.append(block)
        if at_once(t):
            blocks[t] = [block] + [swap(block, "hid", ranks, offset) for offset in (1, 2, 3)]
        else:
            layer[t] = (block, swap(block, "hid", ranks, bits[0]))

    def double_of(t):
        if at_once(t):
            return
        near, far = ordered(layer[t])
        if t > 0:
            near, far = after((near, far), sums[t - 1][0])
        elif chunks > 1:
            near, far = after((near, far), hidden[1])
        for bit in bits[1:]:
            near = jnp.concatenate((near, far))
            last.append(near)
            far = swap(near, "hid", ranks, bit)
        blocks[t] = (near, far)

    def features_of(t):
        near_far = blocks[t]
        if at_once(t):
            parts = ordered(near_far)
            near_far = (jnp.concatenate(parts[0::2]), jnp.concatenate(parts[1::2]))
        own, *sends = encode(rank, *near_far, enc_weight, members, order, list(last))
        last[:] = [own]
        sums[t] = (own, [send(sends[hop - 1], "mp", members, hop) for hop in range(1, members)])

    def share_of(t):
        total, others = ordered(sums[t])
        for other in others:
            total = total + other.astype(F32)
        q = sizes[t]
        others = []
        for hop in range(1, owners):
            going = total[hop * q : (hop + 1) * q].astype(BF16)
            last.append(going)
            others.append(send(going, "rows", owners, hop))
        sums[t] = (total[:q], others)

    def shared_of(t):
        last.extend(sums[t][1])

    def finish_of(t):
        pre, others = sums[t]
        for other in others:
            pre = pre + other.astype(F32)
        pre = pre + enc_bias[None, :]
        factor = adjoint[starts[t] : starts[t] + sizes[t]].astype(F32)
        outs[t] = (jnp.maximum(pre, 0.0) * factor).astype(BF16)

    stages = (
        (gate_up_of, 0), (hidden_of, 0), (gate_up_of, 1), (down_of, 0), (halve_of, 0),
        (hidden_of, 1), (settle_of, 0), (gate_up_of, 2), (double_of, 0), (down_of, 1),
        (features_of, 0), (hidden_of, 2), (halve_of, 1), (settle_of, 1), (down_of, 2),
        (share_of, 0), (settle_of, 2), (double_of, 1), (shared_of, 0), (features_of, 1),
        (features_of, 2), (share_of, 1), (share_of, 2), (finish_of, 0), (finish_of, 1),
        (finish_of, 2),
    )
    for stage, t in stages:
        if t < chunks:
            stage(t)
    gated = jnp.zeros(adjoint.shape, BF16)
    for t in range(chunks):
        gated = lax.dynamic_update_slice(gated, outs[t], (starts[t], 0))
    return gated


def solution(mesh):
    placed = (
        P(("groups", "rows"), "hid"),
        P("mp", None),
        P("mp", "rows", "hid"),
        P("mp", "rows", "hid"),
        P("mp", "hid", "rows"),
        P("mp", "rows", "hid"),
        P("hid"),
        P(("groups", "rows", "mp"), "hid"),
    )
    sizes = (mesh.shape["rows"], mesh.shape["mp"], mesh.shape["hid"])
    return jax.shard_map(
        functools.partial(on_device, *sizes),
        mesh=mesh,
        in_specs=placed,
        out_specs=P(("groups", "rows", "mp"), "hid"),
        check_vma=False,
    )
```

```python
import functools

import jax
import jax.numpy as jnp
from jax import lax
from jax.experimental import pallas as pl
from jax.experimental.pallas import tpu as pltpu
from jax.sharding import PartitionSpec as P

BF16 = jnp.bfloat16
F32 = jnp.float32
VMEM_BYTES = 51 * 1024 * 1024
GATE_UP_VMEM_BYTES = 44 * 1024 * 1024
BUFFERS = 8
GATE_UP_BUFFERS = 4


def shift(value, axis, size, hop):
    return lax.ppermute(value, axis, [((d + hop) % size, d) for d in range(size)])


def send(value, axis, size, hop):
    return lax.ppermute(value, axis, [(d, (d + hop) % size) for d in range(size)])


def swap(value, axis, size, bit):
    return lax.ppermute(value, axis, [(d, d ^ bit) for d in range(size)])


def doubling(size):
    bits = [1 << at for at in reversed(range(size.bit_length() - 1))]
    order = [0]
    for bit in bits:
        order = order + [offset ^ bit for offset in order]
    return bits, order


def tile_of(width, most):
    tile = most
    while tile > 128 and width % tile:
        tile //= 2
    return tile if width % tile == 0 else width


def whole(shape):
    return pl.BlockSpec(shape, lambda j, *_: (0,) * len(shape))


def slots(depth, tile, tiles, most=BUFFERS):
    count = min(most, tiles)
    return [pltpu.VMEM((count, depth, tile), BF16), pltpu.SemaphoreType.DMA((count,))]


def next_block(weight_ref, slot_ref, slot_sems, tiles, first=0):
    step = pl.program_id(0)
    count, _, tile = slot_ref.shape

    def copy(block, slot):
        columns = pl.ds(pl.multiple_of((first + block) * tile, 128), tile)
        return pltpu.make_async_copy(
            weight_ref.at[0, :, columns], slot_ref.at[slot], slot_sems.at[slot]
        )

    @pl.when(step == 0)
    def _():
        for block in range(count - 1):
            copy(block, block).start()

    ahead = step + count - 1

    @pl.when(ahead < tiles)
    def _():
        copy(ahead, lax.rem(ahead, count)).start()

    slot = lax.rem(step, count)
    copy(step, slot).wait()
    return slot_ref.at[slot]


def in_hbm(count):
    return [pl.BlockSpec(memory_space=pltpu.HBM)] * count


def unread(after):
    return [pl.BlockSpec(memory_space=pl.ANY)] * len(after)


def params(vmem_bytes=VMEM_BYTES):
    return pltpu.CompilerParams(
        dimension_semantics=("arbitrary",), vmem_limit_bytes=vmem_bytes
    )


NO_COST = pl.CostEstimate(flops=1, bytes_accessed=1, transcendentals=0)


def gate_up_body(tiles, first, x_ref, gate_ref, up_ref, *refs):
    members, owners, cuts, q, cut = x_ref.shape
    out_refs = refs[-5 - owners : -5]
    lhs_ref = refs[-5]
    blocks = [
        next_block(gate_ref, refs[-4], refs[-3], tiles, first),
        next_block(up_ref, refs[-2], refs[-1], tiles, first),
    ]

    @pl.when(pl.program_id(0) == 0)
    def _():
        for owner in range(owners):
            for member in range(members):
                row = (owner * members + member) * q
                for at in range(cuts):
                    lhs_ref[row : row + q, at * cut : (at + 1) * cut] = x_ref[member, owner, at]

    rows = members * q
    for at, block_ref in enumerate(blocks):
        acts = jnp.dot(lhs_ref[...], block_ref[...], preferred_element_type=F32)
        for hop in range(owners):
            taken = acts[hop * rows : (hop + 1) * rows]
            out_refs[hop][at] = taken.astype(out_refs[hop].dtype)


def gate_up(x, gate_weight, up_weight, first, tiles, after):
    members, owners, cuts, q, cut = x.shape
    rows, depth, own_rows = members * owners * q, cuts * cut, members * q
    tile = tile_of(gate_weight.shape[2], 256)
    width = tiles * tile
    return pl.pallas_call(
        functools.partial(gate_up_body, tiles, first),
        grid=(tiles,),
        in_specs=[whole(x.shape)] + in_hbm(2) + unread(after),
        out_specs=[pl.BlockSpec((2, own_rows, tile), lambda j: (0, 0, j))] * owners,
        out_shape=[jax.ShapeDtypeStruct((2, own_rows, width), F32)]
        + [jax.ShapeDtypeStruct((2, own_rows, width), BF16)] * (owners - 1),
        scratch_shapes=[pltpu.VMEM((rows, depth), BF16)] + slots(depth, tile, tiles, GATE_UP_BUFFERS) * 2,
        compiler_params=params(GATE_UP_VMEM_BYTES),
        cost_estimate=NO_COST,
    )(x, gate_weight, up_weight, *after)


def down_body(owners, members, pieces, order, tiles, rank_ref, *refs):
    hidden_refs = refs[: owners * pieces]
    weight_ref = refs[owners * pieces]
    out_refs = refs[-6:-4]
    lhs_ref, acc_ref, slot_ref, slot_sems = refs[-4:]
    block_ref = next_block(weight_ref, slot_ref, slot_sems, tiles)
    q = hidden_refs[0].shape[0] // members
    part = hidden_refs[0].shape[1]
    block = acc_ref.shape[0] // len(order)

    @pl.when(pl.program_id(0) == 0)
    def _():
        for owner in range(owners):
            for piece in range(pieces):
                for member in range(members):
                    row = (member * owners + owner) * q
                    lhs_ref[row : row + q, piece * part : (piece + 1) * part] = hidden_refs[
                        owner * pieces + piece
                    ][member * q : (member + 1) * q]

    acc_ref[...] = jnp.dot(lhs_ref[...], block_ref[...], preferred_element_type=F32)
    half = len(order) // 2
    for slot, offset in enumerate(order):
        at = (rank_ref[0] ^ offset) * block
        taken = acc_ref[pl.ds(pl.multiple_of(at, block), block), :]
        out_ref = out_refs[slot // half]
        row = (slot % half) * block
        out_ref[row : row + block] = taken.astype(out_ref.dtype)


def down(rank, hidden, down_weight, members, order, after):
    owners, pieces = len(hidden), len(hidden[0])
    rows_each, part = hidden[0][0].shape
    rows, depth, width = owners * rows_each, pieces * part, down_weight.shape[2]
    tile = tile_of(width, 256)
    return pl.pallas_call(
        functools.partial(down_body, owners, members, pieces, order, width // tile),
        grid_spec=pltpu.PrefetchScalarGridSpec(
            num_scalar_prefetch=1,
            grid=(width // tile,),
            in_specs=[whole((rows_each, part))] * (owners * pieces)
            + in_hbm(1)
            + unread(after),
            out_specs=[pl.BlockSpec((rows // 2, tile), lambda j, *_: (0, j))] * 2,
            scratch_shapes=[pltpu.VMEM((rows, depth), BF16), pltpu.VMEM((rows, tile), F32)]
            + slots(depth, tile, width // tile),
        ),
        out_shape=[jax.ShapeDtypeStruct((rows // 2, width), kind) for kind in (F32, BF16)],
        compiler_params=params(),
        cost_estimate=NO_COST,
    )(rank, *[piece for of_owner in hidden for piece in of_owner], down_weight, *after)


def encode_body(members, order, tiles, rank_ref, near_ref, far_ref, weight_ref, *refs):
    out_refs = refs[-3 - members : -3]
    lhs_ref, slot_ref, slot_sems = refs[-3:]
    weight_block = next_block(weight_ref, slot_ref, slot_sems, tiles)
    block = lhs_ref.shape[0] // len(order)
    half = len(order) // 2

    @pl.when(pl.program_id(0) == 0)
    def _():
        for slot, offset in enumerate(order):
            at = (rank_ref[0] ^ offset) * block
            row = (slot % half) * block
            from_ref = far_ref if slot >= half else near_ref
            lhs_ref[pl.ds(pl.multiple_of(at, block), block), :] = from_ref[row : row + block]

    pre = jnp.dot(lhs_ref[...], weight_block[...], preferred_element_type=F32)
    rows = pre.shape[0] // members
    for member in range(members):
        taken = pre[member * rows : (member + 1) * rows]
        out_refs[member][...] = taken.astype(out_refs[member].dtype)


def encode(rank, near, far, enc_weight, members, order, after):
    rows, depth = 2 * near.shape[0], near.shape[1]
    width = enc_weight.shape[2]
    rows_each = rows // members
    tile = tile_of(width, 512)
    tiles = width // tile
    return pl.pallas_call(
        functools.partial(encode_body, members, order, tiles),
        grid_spec=pltpu.PrefetchScalarGridSpec(
            num_scalar_prefetch=1,
            grid=(width // tile,),
            in_specs=[whole(near.shape)] * 2 + in_hbm(1) + unread(after),
            out_specs=[pl.BlockSpec((rows_each, tile), lambda j, *_: (0, j))] * members,
            scratch_shapes=[pltpu.VMEM((rows, depth), BF16)] + slots(depth, tile, width // tile),
        ),
        out_shape=[jax.ShapeDtypeStruct((rows_each, width), F32)]
        + [jax.ShapeDtypeStruct((rows_each, width), BF16)] * (members - 1),
        compiler_params=params(),
        cost_estimate=NO_COST,
    )(rank, near, far, enc_weight, *after)


def chunk_rows(total, unit):
    units = total // unit
    if units < 8:
        return [total]
    most = 3 * (units // 8)
    return [most * unit, most * unit, (units - 2 * most) * unit]


def on_device(
    owners, members, ranks, tokens, norm_gain, gate_weight, up_weight, down_weight, enc_weight,
    enc_bias, adjoint,
):
    row_at = lax.axis_index("rows")
    member_at = lax.axis_index("mp")
    rank_at = lax.axis_index("hid")
    rank = rank_at.astype(jnp.int32).reshape(1)
    per_device = adjoint.shape[0]
    cut = tokens.shape[1]
    half_cuts = ranks // owners
    model_width = cut * ranks

    gain = lax.dynamic_slice_in_dim(
        norm_gain[0], row_at * (model_width // owners), model_width // owners, 0
    ).reshape(half_cuts, 1, cut)
    own_tokens = lax.dynamic_slice_in_dim(tokens, member_at * per_device, per_device, 0)

    bits, order = doubling(ranks)

    def from_all(value, axis, size):
        return jnp.stack([value] + [shift(value, axis, size, hop) for hop in range(1, size)])

    def place_of(offset):
        place = 0
        for at in range(len(bits)):
            place = place + ((offset >> at) & 1) * bits[at]
        return place

    def after(values, others):
        return lax.optimization_barrier((values, others))[0]

    def doubled(gathered, bit):
        return jnp.concatenate((gathered, swap(gathered, "hid", ranks, bit)))

    def from_owners(gathered):
        wide = gathered.astype(F32)
        squares = jnp.sum(wide * wide, axis=(0, 2))
        inverse = lax.rsqrt(squares / model_width + 1e-05)
        columns = []
        for hop in range(owners):
            target = lax.rem(row_at + owners - hop, owners)
            half = jnp.concatenate(
                [
                    lax.dynamic_slice_in_dim(
                        gathered, place_of(rank_at ^ (target * half_cuts + at)), 1, 0
                    )
                    for at in range(half_cuts)
                ]
            )
            columns.append(half if hop == 0 else shift(half, "rows", owners, hop))
        return columns, inverse

    def from_members(columns):
        return from_all(jnp.stack(columns), "mp", members)

    def normed(columns, inverses):
        return (columns.astype(F32) * inverses[:, :, None, :, None] * gain).astype(BF16)

    sizes = chunk_rows(per_device, 16 * max(1, ranks // (owners * members)))
    starts = [sum(sizes[:at]) for at in range(len(sizes))]
    chunks = len(sizes)
    head = sizes[0]

    gathered = own_tokens[:head][None]
    rest = own_tokens[head:][None] if chunks > 1 else None
    for bit in bits:
        gathered = doubled(gathered, bit)
        if rest is not None:
            rest = doubled(after(rest, gathered), bit)
    columns, inverse = from_owners(gathered)
    if rest is not None:
        rest = from_owners(after(rest, (columns, inverse)))
    inverses = from_all(inverse, "rows", owners)
    columns, inverses = after((columns, inverses), (columns, inverses))
    xs = [normed(from_members(columns), from_all(inverses, "mp", members))]

    sums, hidden, layer, blocks, outs = ({} for _ in range(5))
    last = []

    def gate_up_of(t):
        tiles = gate_weight.shape[2] // tile_of(gate_weight.shape[2], 256)
        early = tiles * 3 // 7 if t == 0 and chunks > 1 else 0
        sums[t] = []
        for first, count in ((0, early), (early, tiles - early)):
            if not count:
                continue
            own, *sends = gate_up(xs[t], gate_weight, up_weight, first, count, list(last))
            last[:] = [own]
            if t == 0 and rest is not None:
                last.extend(rest[0])
            others = [send(sends[hop - 1], "rows", owners, hop) for hop in range(1, owners)]
            sums[t].append((own, others))

    def rest_of():
        columns, inverse = rest
        inverses = from_all(after(inverse, sums[0][-1][0]), "rows", owners)
        columns, inverses = after((columns, inverses), (columns, inverses))
        columns, inverses = from_members(columns), from_all(inverses, "mp", members)
        for start, q in zip(starts[1:], sizes[1:]):
            rows = slice(start - head, start - head + q)
            xs.append(normed(columns[:, :, :, rows], inverses[:, :, rows]))

    def hidden_of(t):
        units = []
        parts = ordered(sums[t]) if 0 < t == chunks - 1 else sums[t]
        for own, others in parts:
            acts = own
            for other in others:
                acts = acts + other.astype(F32)
            units.append((jax.nn.silu(acts[0]) * acts[1]).astype(BF16))
        if t == 0 and rest is not None:
            rest_of()
        units = jnp.concatenate(units, axis=1)
        hidden[t] = [units] + [shift(units, "rows", owners, hop) for hop in range(1, owners)]
        last.append(units)

    def ordered(values):
        return after(values, last[0])

    def at_once(t):
        return t == chunks - 1 and ranks == 4

    def down_of(t):
        total, going = down(rank, [[units] for units in hidden[t]], down_weight, members, order, list(last))
        last[:] = [total]
        if at_once(t):
            block = total.shape[0] // 2
            far = total[block:].astype(BF16)
            arrived = [
                swap(part, "hid", ranks, offset)
                for part, offset in ((going[block:], 3), (far, 2), (going[:block], 1))
            ]
            layer[t] = (total[:block], arrived)
        else:
            layer[t] = (total, swap(going, "hid", ranks, 1))

    def halve_of(t):
        if at_once(t):
            return
        total, arrived = ordered(layer[t])
        if chunks > 1 and t == chunks - 2:
            total, arrived = after((total, arrived), hidden[t + 1][0])
        for bit in reversed(bits[:-1]):
            total = total + arrived.astype(F32)
            kept = total.shape[0] // 2
            going = total[kept:].astype(BF16)
            last.append(going)
            total, arrived = total[:kept], swap(going, "hid", ranks, bit)
        layer[t] = (total, arrived)

    def settle_of(t):
        total, arrived = ordered(layer[t])
        for part in arrived if at_once(t) else [arrived]:
            total = total + part.astype(F32)
        block = total.astype(BF16)
        last.append(block)
        if at_once(t):
            blocks[t] = [block] + [swap(block, "hid", ranks, offset) for offset in (1, 2, 3)]
        else:
            layer[t] = (block, swap(block, "hid", ranks, bits[0]))

    def double_of(t):
        if at_once(t):
            return
        near, far = ordered(layer[t])
        if t > 0:
            near, far = after((near, far), sums[t - 1][0])
        elif chunks > 1:
            near, far = after((near, far), hidden[1])
        for bit in bits[1:]:
            near = jnp.concatenate((near, far))
            last.append(near)
            far = swap(near, "hid", ranks, bit)
        blocks[t] = (near, far)

    def features_of(t):
        near_far = blocks[t]
        if at_once(t):
            parts = ordered(near_far)
            near_far = (jnp.concatenate(parts[0::2]), jnp.concatenate(parts[1::2]))
        own, *sends = encode(rank, *near_far, enc_weight, members, order, list(last))
        last[:] = [own]
        sums[t] = (own, [send(sends[hop - 1], "mp", members, hop) for hop in range(1, members)])

    def share_of(t):
        total, others = ordered(sums[t])
        for other in others:
            total = total + other.astype(F32)
        q = sizes[t]
        others = []
        for hop in range(1, owners):
            going = total[hop * q : (hop + 1) * q].astype(BF16)
            last.append(going)
            others.append(send(going, "rows", owners, hop))
        sums[t] = (total[:q], others)

    def shared_of(t):
        last.extend(sums[t][1])

    def finish_of(t):
        pre, others = sums[t]
        for other in others:
            pre = pre + other.astype(F32)
        pre = pre + enc_bias[None, :]
        factor = adjoint[starts[t] : starts[t] + sizes[t]].astype(F32)
        outs[t] = (jnp.maximum(pre, 0.0) * factor).astype(BF16)

    stages = (
        (gate_up_of, 0), (hidden_of, 0), (gate_up_of, 1), (down_of, 0), (halve_of, 0),
        (hidden_of, 1), (settle_of, 0), (gate_up_of, 2), (double_of, 0), (down_of, 1),
        (features_of, 0), (hidden_of, 2), (halve_of, 1), (settle_of, 1), (down_of, 2),
        (share_of, 0), (settle_of, 2), (double_of, 1), (shared_of, 0), (features_of, 1),
        (features_of, 2), (share_of, 1), (share_of, 2), (finish_of, 0), (finish_of, 1),
        (finish_of, 2),
    )
    for stage, t in stages:
        if t < chunks:
            stage(t)
    gated = jnp.zeros(adjoint.shape, BF16)
    for t in range(chunks):
        gated = lax.dynamic_update_slice(gated, outs[t], (starts[t], 0))
    return gated


def solution(mesh):
    placed = (
        P(("groups", "rows"), "hid"),
        P("mp", None),
        P("mp", "rows", "hid"),
        P("mp", "rows", "hid"),
        P("mp", "hid", "rows"),
        P("mp", "rows", "hid"),
        P("hid"),
        P(("groups", "rows", "mp"), "hid"),
    )
    sizes = (mesh.shape["rows"], mesh.shape["mp"], mesh.shape["hid"])
    return jax.shard_map(
        functools.partial(on_device, *sizes),
        mesh=mesh,
        in_specs=placed,
        out_specs=P(("groups", "rows", "mp"), "hid"),
        check_vma=False,
    )
```

```python
import functools

import jax
import jax.numpy as jnp
from jax import lax
from jax.experimental import pallas as pl
from jax.experimental.pallas import tpu as pltpu
from jax.sharding import PartitionSpec as P

BF16 = jnp.bfloat16
F32 = jnp.float32
VMEM_BYTES = 51 * 1024 * 1024
GATE_UP_VMEM_BYTES = 44 * 1024 * 1024
BUFFERS = 8
GATE_UP_BUFFERS = 4


def shift(value, axis, size, hop):
    return lax.ppermute(value, axis, [((d + hop) % size, d) for d in range(size)])


def send(value, axis, size, hop):
    return lax.ppermute(value, axis, [(d, (d + hop) % size) for d in range(size)])


def swap(value, axis, size, bit):
    return lax.ppermute(value, axis, [(d, d ^ bit) for d in range(size)])


def doubling(size):
    bits = [1 << at for at in reversed(range(size.bit_length() - 1))]
    order = [0]
    for bit in bits:
        order = order + [offset ^ bit for offset in order]
    return bits, order


def tile_of(width, most):
    tile = most
    while tile > 128 and width % tile:
        tile //= 2
    return tile if width % tile == 0 else width


def whole(shape):
    return pl.BlockSpec(shape, lambda j, *_: (0,) * len(shape))


def slots(depth, tile, tiles, most=BUFFERS):
    count = min(most, tiles)
    return [pltpu.VMEM((count, depth, tile), BF16), pltpu.SemaphoreType.DMA((count,))]


def next_block(weight_ref, slot_ref, slot_sems, tiles, first=0):
    step = pl.program_id(0)
    count, _, tile = slot_ref.shape

    def copy(block, slot):
        columns = pl.ds(pl.multiple_of((first + block) * tile, 128), tile)
        return pltpu.make_async_copy(
            weight_ref.at[0, :, columns], slot_ref.at[slot], slot_sems.at[slot]
        )

    @pl.when(step == 0)
    def _():
        for block in range(count - 1):
            copy(block, block).start()

    ahead = step + count - 1

    @pl.when(ahead < tiles)
    def _():
        copy(ahead, lax.rem(ahead, count)).start()

    slot = lax.rem(step, count)
    copy(step, slot).wait()
    return slot_ref.at[slot]


def in_hbm(count):
    return [pl.BlockSpec(memory_space=pltpu.HBM)] * count


def unread(after):
    return [pl.BlockSpec(memory_space=pl.ANY)] * len(after)


def params(vmem_bytes=VMEM_BYTES):
    return pltpu.CompilerParams(
        dimension_semantics=("arbitrary",), vmem_limit_bytes=vmem_bytes
    )


NO_COST = pl.CostEstimate(flops=1, bytes_accessed=1, transcendentals=0)


def gate_up_body(tiles, first, x_ref, gate_ref, up_ref, *refs):
    members, owners, cuts, q, cut = x_ref.shape
    out_refs = refs[-5 - owners : -5]
    lhs_ref = refs[-5]
    blocks = [
        next_block(gate_ref, refs[-4], refs[-3], tiles, first),
        next_block(up_ref, refs[-2], refs[-1], tiles, first),
    ]

    @pl.when(pl.program_id(0) == 0)
    def _():
        for owner in range(owners):
            for member in range(members):
                row = (owner * members + member) * q
                for at in range(cuts):
                    lhs_ref[row : row + q, at * cut : (at + 1) * cut] = x_ref[member, owner, at]

    rows = members * q
    for at, block_ref in enumerate(blocks):
        acts = jnp.dot(lhs_ref[...], block_ref[...], preferred_element_type=F32)
        for hop in range(owners):
            taken = acts[hop * rows : (hop + 1) * rows]
            out_refs[hop][at] = taken.astype(out_refs[hop].dtype)


def gate_up(x, gate_weight, up_weight, first, tiles, after):
    members, owners, cuts, q, cut = x.shape
    rows, depth, own_rows = members * owners * q, cuts * cut, members * q
    tile = tile_of(gate_weight.shape[2], 256)
    width = tiles * tile
    return pl.pallas_call(
        functools.partial(gate_up_body, tiles, first),
        grid=(tiles,),
        in_specs=[whole(x.shape)] + in_hbm(2) + unread(after),
        out_specs=[pl.BlockSpec((2, own_rows, tile), lambda j: (0, 0, j))] * owners,
        out_shape=[jax.ShapeDtypeStruct((2, own_rows, width), F32)]
        + [jax.ShapeDtypeStruct((2, own_rows, width), BF16)] * (owners - 1),
        scratch_shapes=[pltpu.VMEM((rows, depth), BF16)] + slots(depth, tile, tiles, GATE_UP_BUFFERS) * 2,
        compiler_params=params(GATE_UP_VMEM_BYTES),
        cost_estimate=NO_COST,
    )(x, gate_weight, up_weight, *after)


def down_body(owners, members, pieces, order, tiles, rank_ref, *refs):
    hidden_refs = refs[: owners * pieces]
    weight_ref = refs[owners * pieces]
    out_refs = refs[-6:-4]
    lhs_ref, acc_ref, slot_ref, slot_sems = refs[-4:]
    block_ref = next_block(weight_ref, slot_ref, slot_sems, tiles)
    q = hidden_refs[0].shape[0] // members
    part = hidden_refs[0].shape[1]
    block = acc_ref.shape[0] // len(order)

    @pl.when(pl.program_id(0) == 0)
    def _():
        for owner in range(owners):
            for piece in range(pieces):
                for member in range(members):
                    row = (member * owners + owner) * q
                    lhs_ref[row : row + q, piece * part : (piece + 1) * part] = hidden_refs[
                        owner * pieces + piece
                    ][member * q : (member + 1) * q]

    acc_ref[...] = jnp.dot(lhs_ref[...], block_ref[...], preferred_element_type=F32)
    half = len(order) // 2
    for slot, offset in enumerate(order):
        at = (rank_ref[0] ^ offset) * block
        taken = acc_ref[pl.ds(pl.multiple_of(at, block), block), :]
        out_ref = out_refs[slot // half]
        row = (slot % half) * block
        out_ref[row : row + block] = taken.astype(out_ref.dtype)


def down(rank, hidden, down_weight, members, order, after):
    owners, pieces = len(hidden), len(hidden[0])
    rows_each, part = hidden[0][0].shape
    rows, depth, width = owners * rows_each, pieces * part, down_weight.shape[2]
    tile = tile_of(width, 256)
    return pl.pallas_call(
        functools.partial(down_body, owners, members, pieces, order, width // tile),
        grid_spec=pltpu.PrefetchScalarGridSpec(
            num_scalar_prefetch=1,
            grid=(width // tile,),
            in_specs=[whole((rows_each, part))] * (owners * pieces)
            + in_hbm(1)
            + unread(after),
            out_specs=[pl.BlockSpec((rows // 2, tile), lambda j, *_: (0, j))] * 2,
            scratch_shapes=[pltpu.VMEM((rows, depth), BF16), pltpu.VMEM((rows, tile), F32)]
            + slots(depth, tile, width // tile),
        ),
        out_shape=[jax.ShapeDtypeStruct((rows // 2, width), kind) for kind in (F32, BF16)],
        compiler_params=params(),
        cost_estimate=NO_COST,
    )(rank, *[piece for of_owner in hidden for piece in of_owner], down_weight, *after)


def encode_body(members, order, tiles, rank_ref, near_ref, far_ref, weight_ref, *refs):
    out_refs = refs[-3 - members : -3]
    lhs_ref, slot_ref, slot_sems = refs[-3:]
    weight_block = next_block(weight_ref, slot_ref, slot_sems, tiles)
    block = lhs_ref.shape[0] // len(order)
    half = len(order) // 2

    @pl.when(pl.program_id(0) == 0)
    def _():
        for slot, offset in enumerate(order):
            at = (rank_ref[0] ^ offset) * block
            row = (slot % half) * block
            from_ref = far_ref if slot >= half else near_ref
            lhs_ref[pl.ds(pl.multiple_of(at, block), block), :] = from_ref[row : row + block]

    pre = jnp.dot(lhs_ref[...], weight_block[...], preferred_element_type=F32)
    rows = pre.shape[0] // members
    for member in range(members):
        taken = pre[member * rows : (member + 1) * rows]
        out_refs[member][...] = taken.astype(out_refs[member].dtype)


def encode(rank, near, far, enc_weight, members, order, after):
    rows, depth = 2 * near.shape[0], near.shape[1]
    width = enc_weight.shape[2]
    rows_each = rows // members
    tile = tile_of(width, 512)
    tiles = width // tile
    return pl.pallas_call(
        functools.partial(encode_body, members, order, tiles),
        grid_spec=pltpu.PrefetchScalarGridSpec(
            num_scalar_prefetch=1,
            grid=(width // tile,),
            in_specs=[whole(near.shape)] * 2 + in_hbm(1) + unread(after),
            out_specs=[pl.BlockSpec((rows_each, tile), lambda j, *_: (0, j))] * members,
            scratch_shapes=[pltpu.VMEM((rows, depth), BF16)] + slots(depth, tile, width // tile),
        ),
        out_shape=[jax.ShapeDtypeStruct((rows_each, width), F32)]
        + [jax.ShapeDtypeStruct((rows_each, width), BF16)] * (members - 1),
        compiler_params=params(),
        cost_estimate=NO_COST,
    )(rank, near, far, enc_weight, *after)


def chunk_rows(total, unit):
    units = total // unit
    if units < 8:
        return [total]
    most = 3 * (units // 8)
    return [most * unit, most * unit, (units - 2 * most) * unit]


def on_device(
    owners, members, ranks, tokens, norm_gain, gate_weight, up_weight, down_weight, enc_weight,
    enc_bias, adjoint,
):
    row_at = lax.axis_index("rows")
    member_at = lax.axis_index("mp")
    rank_at = lax.axis_index("hid")
    rank = rank_at.astype(jnp.int32).reshape(1)
    per_device = adjoint.shape[0]
    cut = tokens.shape[1]
    half_cuts = ranks // owners
    model_width = cut * ranks

    gain = lax.dynamic_slice_in_dim(
        norm_gain[0], row_at * (model_width // owners), model_width // owners, 0
    ).reshape(half_cuts, 1, cut)
    own_tokens = lax.dynamic_slice_in_dim(tokens, member_at * per_device, per_device, 0)

    bits, order = doubling(ranks)

    def from_all(value, axis, size):
        return jnp.stack([value] + [shift(value, axis, size, hop) for hop in range(1, size)])

    def place_of(offset):
        place = 0
        for at in range(len(bits)):
            place = place + ((offset >> at) & 1) * bits[at]
        return place

    def after(values, others):
        return lax.optimization_barrier((values, others))[0]

    def doubled(gathered, bit):
        return jnp.concatenate((gathered, swap(gathered, "hid", ranks, bit)))

    def from_owners(gathered):
        wide = gathered.astype(F32)
        squares = jnp.sum(wide * wide, axis=(0, 2))
        inverse = lax.rsqrt(squares / model_width + 1e-05)
        columns = []
        for hop in range(owners):
            target = lax.rem(row_at + owners - hop, owners)
            half = jnp.concatenate(
                [
                    lax.dynamic_slice_in_dim(
                        gathered, place_of(rank_at ^ (target * half_cuts + at)), 1, 0
                    )
                    for at in range(half_cuts)
                ]
            )
            columns.append(half if hop == 0 else shift(half, "rows", owners, hop))
        return columns, inverse

    def from_members(columns):
        return from_all(jnp.stack(columns), "mp", members)

    def normed(columns, inverses):
        return (columns.astype(F32) * inverses[:, :, None, :, None] * gain).astype(BF16)

    sizes = chunk_rows(per_device, 16 * max(1, ranks // (owners * members)))
    starts = [sum(sizes[:at]) for at in range(len(sizes))]
    chunks = len(sizes)
    head = sizes[0]

    gathered = own_tokens[:head][None]
    rest = own_tokens[head:][None] if chunks > 1 else None
    for bit in bits:
        gathered = doubled(gathered, bit)
        if rest is not None:
            rest = doubled(after(rest, gathered), bit)
    columns, inverse = from_owners(gathered)
    if rest is not None:
        rest_columns, rest_inverse = from_owners(after(rest, (columns, inverse)))
        rest = [rest_columns, rest_inverse]
    inverses = from_all(inverse, "rows", owners)
    columns, inverses = after((columns, inverses), (columns, inverses))
    xs = [normed(from_members(columns), from_all(inverses, "mp", members))]

    sums, hidden, layer, blocks, outs = ({} for _ in range(5))
    last = []

    def gate_up_of(t):
        tiles = gate_weight.shape[2] // tile_of(gate_weight.shape[2], 256)
        early = tiles // 2 if t == 0 and chunks > 1 else 0
        sums[t] = []
        for first, count in ((0, early), (early, tiles - early)):
            if not count:
                continue
            own, *sends = gate_up(xs[t], gate_weight, up_weight, first, count, list(last))
            last[:] = [own]
            if t == 0 and rest is not None:
                if not first:
                    rest[1] = from_all(after(rest[1], own), "mp", members)
                last.extend(rest[0])
                last.append(rest[1])
            others = [send(sends[hop - 1], "rows", owners, hop) for hop in range(1, owners)]
            sums[t].append((own, others))

    def rest_of():
        inverses = from_all(after(rest[1], sums[0][-1][0]), "rows", owners).transpose(1, 0, 2)
        sums[0][-1] = after(sums[0][-1], inverses)
        columns = from_members(rest[0])
        for start, q in zip(starts[1:], sizes[1:]):
            rows = slice(start - head, start - head + q)
            xs.append(normed(columns[:, :, :, rows], inverses[:, :, rows]))

    def hidden_of(t):
        if t == 0 and rest is not None:
            rest_of()
        units = []
        parts = ordered(sums[t]) if 0 < t == chunks - 1 else sums[t]
        for own, others in parts:
            acts = own
            for other in others:
                acts = acts + other.astype(F32)
            units.append((jax.nn.silu(acts[0]) * acts[1]).astype(BF16))
        units = jnp.concatenate(units, axis=1)
        hidden[t] = [units] + [shift(units, "rows", owners, hop) for hop in range(1, owners)]
        last.append(units)

    def ordered(values):
        return after(values, last[0])

    def at_once(t):
        return t == chunks - 1 and ranks == 4

    def down_of(t):
        total, going = down(rank, [[units] for units in hidden[t]], down_weight, members, order, list(last))
        last[:] = [total]
        if at_once(t):
            block = total.shape[0] // 2
            far = total[block:].astype(BF16)
            arrived = [
                swap(part, "hid", ranks, offset)
                for part, offset in ((going[block:], 3), (far, 2), (going[:block], 1))
            ]
            layer[t] = (total[:block], arrived)
        else:
            layer[t] = (total, swap(going, "hid", ranks, 1))

    def halve_of(t):
        if at_once(t):
            return
        total, arrived = ordered(layer[t])
        if chunks > 1 and t == chunks - 2:
            total, arrived = after((total, arrived), hidden[t + 1][0])
        for bit in reversed(bits[:-1]):
            total = total + arrived.astype(F32)
            kept = total.shape[0] // 2
            going = total[kept:].astype(BF16)
            last.append(going)
            total, arrived = total[:kept], swap(going, "hid", ranks, bit)
        layer[t] = (total, arrived)

    def settle_of(t):
        total, arrived = ordered(layer[t])
        for part in arrived if at_once(t) else [arrived]:
            total = total + part.astype(F32)
        block = total.astype(BF16)
        last.append(block)
        if at_once(t):
            blocks[t] = [block] + [swap(block, "hid", ranks, offset) for offset in (1, 2, 3)]
        else:
            layer[t] = (block, swap(block, "hid", ranks, bits[0]))

    def double_of(t):
        if at_once(t):
            return
        near, far = ordered(layer[t])
        if t > 0:
            near, far = after((near, far), sums[t - 1][0])
        elif chunks > 1:
            near, far = after((near, far), hidden[1])
        for bit in bits[1:]:
            near = jnp.concatenate((near, far))
            last.append(near)
            far = swap(near, "hid", ranks, bit)
        blocks[t] = (near, far)

    def features_of(t):
        near_far = blocks[t]
        if at_once(t):
            parts = ordered(near_far)
            near_far = (jnp.concatenate(parts[0::2]), jnp.concatenate(parts[1::2]))
        own, *sends = encode(rank, *near_far, enc_weight, members, order, list(last))
        last[:] = [own]
        sums[t] = (own, [send(sends[hop - 1], "mp", members, hop) for hop in range(1, members)])

    def share_of(t):
        total, others = ordered(sums[t])
        for other in others:
            total = total + other.astype(F32)
        q = sizes[t]
        others = []
        for hop in range(1, owners):
            going = total[hop * q : (hop + 1) * q].astype(BF16)
            last.append(going)
            others.append(send(going, "rows", owners, hop))
        sums[t] = (total[:q], others)

    def shared_of(t):
        last.extend(sums[t][1])

    def finish_of(t):
        pre, others = sums[t]
        for other in others:
            pre = pre + other.astype(F32)
        pre = pre + enc_bias[None, :]
        factor = adjoint[starts[t] : starts[t] + sizes[t]].astype(F32)
        outs[t] = (jnp.maximum(pre, 0.0) * factor).astype(BF16)

    stages = (
        (gate_up_of, 0), (hidden_of, 0), (gate_up_of, 1), (down_of, 0), (halve_of, 0),
        (hidden_of, 1), (settle_of, 0), (gate_up_of, 2), (double_of, 0), (down_of, 1),
        (features_of, 0), (hidden_of, 2), (halve_of, 1), (settle_of, 1), (down_of, 2),
        (share_of, 0), (settle_of, 2), (double_of, 1), (shared_of, 0), (features_of, 1),
        (features_of, 2), (share_of, 1), (share_of, 2), (finish_of, 0), (finish_of, 1),
        (finish_of, 2),
    )
    for stage, t in stages:
        if t < chunks:
            stage(t)
    gated = jnp.zeros(adjoint.shape, BF16)
    for t in range(chunks):
        gated = lax.dynamic_update_slice(gated, outs[t], (starts[t], 0))
    return gated


def solution(mesh):
    placed = (
        P(("groups", "rows"), "hid"),
        P("mp", None),
        P("mp", "rows", "hid"),
        P("mp", "rows", "hid"),
        P("mp", "hid", "rows"),
        P("mp", "rows", "hid"),
        P("hid"),
        P(("groups", "rows", "mp"), "hid"),
    )
    sizes = (mesh.shape["rows"], mesh.shape["mp"], mesh.shape["hid"])
    return jax.shard_map(
        functools.partial(on_device, *sizes),
        mesh=mesh,
        in_specs=placed,
        out_specs=P(("groups", "rows", "mp"), "hid"),
        check_vma=False,
    )
```

```python
import functools

import jax
import jax.numpy as jnp
from jax import lax
from jax.experimental import pallas as pl
from jax.experimental.pallas import tpu as pltpu
from jax.sharding import PartitionSpec as P

BF16 = jnp.bfloat16
F32 = jnp.float32
VMEM_BYTES = 51 * 1024 * 1024
GATE_UP_VMEM_BYTES = 44 * 1024 * 1024
BUFFERS = 8
GATE_UP_BUFFERS = 4


def shift(value, axis, size, hop):
    return lax.ppermute(value, axis, [((d + hop) % size, d) for d in range(size)])


def send(value, axis, size, hop):
    return lax.ppermute(value, axis, [(d, (d + hop) % size) for d in range(size)])


def swap(value, axis, size, bit):
    return lax.ppermute(value, axis, [(d, d ^ bit) for d in range(size)])


def doubling(size):
    bits = [1 << at for at in reversed(range(size.bit_length() - 1))]
    order = [0]
    for bit in bits:
        order = order + [offset ^ bit for offset in order]
    return bits, order


def tile_of(width, most):
    tile = most
    while tile > 128 and width % tile:
        tile //= 2
    return tile if width % tile == 0 else width


def whole(shape):
    return pl.BlockSpec(shape, lambda j, *_: (0,) * len(shape))


def slots(depth, tile, tiles, most=BUFFERS):
    count = min(most, tiles)
    return [pltpu.VMEM((count, depth, tile), BF16), pltpu.SemaphoreType.DMA((count,))]


def next_block(weight_ref, slot_ref, slot_sems, tiles, first=0):
    step = pl.program_id(0)
    count, _, tile = slot_ref.shape

    def copy(block, slot):
        columns = pl.ds(pl.multiple_of((first + block) * tile, 128), tile)
        return pltpu.make_async_copy(
            weight_ref.at[0, :, columns], slot_ref.at[slot], slot_sems.at[slot]
        )

    @pl.when(step == 0)
    def _():
        for block in range(count - 1):
            copy(block, block).start()

    ahead = step + count - 1

    @pl.when(ahead < tiles)
    def _():
        copy(ahead, lax.rem(ahead, count)).start()

    slot = lax.rem(step, count)
    copy(step, slot).wait()
    return slot_ref.at[slot]


def in_hbm(count):
    return [pl.BlockSpec(memory_space=pltpu.HBM)] * count


def unread(after):
    return [pl.BlockSpec(memory_space=pl.ANY)] * len(after)


def params(vmem_bytes=VMEM_BYTES):
    return pltpu.CompilerParams(
        dimension_semantics=("arbitrary",), vmem_limit_bytes=vmem_bytes
    )


NO_COST = pl.CostEstimate(flops=1, bytes_accessed=1, transcendentals=0)


def gate_up_body(tiles, first, x_ref, gate_ref, up_ref, *refs):
    members, owners, cuts, q, cut = x_ref.shape
    out_refs = refs[-5 - owners : -5]
    lhs_ref = refs[-5]
    blocks = [
        next_block(gate_ref, refs[-4], refs[-3], tiles, first),
        next_block(up_ref, refs[-2], refs[-1], tiles, first),
    ]

    @pl.when(pl.program_id(0) == 0)
    def _():
        for owner in range(owners):
            for member in range(members):
                row = (owner * members + member) * q
                for at in range(cuts):
                    lhs_ref[row : row + q, at * cut : (at + 1) * cut] = x_ref[member, owner, at]

    rows = members * q
    for at, block_ref in enumerate(blocks):
        acts = jnp.dot(lhs_ref[...], block_ref[...], preferred_element_type=F32)
        for hop in range(owners):
            taken = acts[hop * rows : (hop + 1) * rows]
            out_refs[hop][at] = taken.astype(out_refs[hop].dtype)


def gate_up(x, gate_weight, up_weight, first, tiles, after):
    members, owners, cuts, q, cut = x.shape
    rows, depth, own_rows = members * owners * q, cuts * cut, members * q
    tile = tile_of(gate_weight.shape[2], 256)
    width = tiles * tile
    return pl.pallas_call(
        functools.partial(gate_up_body, tiles, first),
        grid=(tiles,),
        in_specs=[whole(x.shape)] + in_hbm(2) + unread(after),
        out_specs=[pl.BlockSpec((2, own_rows, tile), lambda j: (0, 0, j))] * owners,
        out_shape=[jax.ShapeDtypeStruct((2, own_rows, width), F32)]
        + [jax.ShapeDtypeStruct((2, own_rows, width), BF16)] * (owners - 1),
        scratch_shapes=[pltpu.VMEM((rows, depth), BF16)] + slots(depth, tile, tiles, GATE_UP_BUFFERS) * 2,
        compiler_params=params(GATE_UP_VMEM_BYTES),
        cost_estimate=NO_COST,
    )(x, gate_weight, up_weight, *after)


def down_body(owners, members, pieces, order, tiles, rank_ref, *refs):
    hidden_refs = refs[: owners * pieces]
    weight_ref = refs[owners * pieces]
    out_refs = refs[-6:-4]
    lhs_ref, acc_ref, slot_ref, slot_sems = refs[-4:]
    block_ref = next_block(weight_ref, slot_ref, slot_sems, tiles)
    q = hidden_refs[0].shape[0] // members
    part = hidden_refs[0].shape[1]
    block = acc_ref.shape[0] // len(order)

    @pl.when(pl.program_id(0) == 0)
    def _():
        for owner in range(owners):
            for piece in range(pieces):
                for member in range(members):
                    row = (member * owners + owner) * q
                    lhs_ref[row : row + q, piece * part : (piece + 1) * part] = hidden_refs[
                        owner * pieces + piece
                    ][member * q : (member + 1) * q]

    acc_ref[...] = jnp.dot(lhs_ref[...], block_ref[...], preferred_element_type=F32)
    half = len(order) // 2
    for slot, offset in enumerate(order):
        at = (rank_ref[0] ^ offset) * block
        taken = acc_ref[pl.ds(pl.multiple_of(at, block), block), :]
        out_ref = out_refs[slot // half]
        row = (slot % half) * block
        out_ref[row : row + block] = taken.astype(out_ref.dtype)


def down(rank, hidden, down_weight, members, order, after):
    owners, pieces = len(hidden), len(hidden[0])
    rows_each, part = hidden[0][0].shape
    rows, depth, width = owners * rows_each, pieces * part, down_weight.shape[2]
    tile = tile_of(width, 256)
    return pl.pallas_call(
        functools.partial(down_body, owners, members, pieces, order, width // tile),
        grid_spec=pltpu.PrefetchScalarGridSpec(
            num_scalar_prefetch=1,
            grid=(width // tile,),
            in_specs=[whole((rows_each, part))] * (owners * pieces)
            + in_hbm(1)
            + unread(after),
            out_specs=[pl.BlockSpec((rows // 2, tile), lambda j, *_: (0, j))] * 2,
            scratch_shapes=[pltpu.VMEM((rows, depth), BF16), pltpu.VMEM((rows, tile), F32)]
            + slots(depth, tile, width // tile),
        ),
        out_shape=[jax.ShapeDtypeStruct((rows // 2, width), kind) for kind in (F32, BF16)],
        compiler_params=params(),
        cost_estimate=NO_COST,
    )(rank, *[piece for of_owner in hidden for piece in of_owner], down_weight, *after)


def encode_body(members, order, tiles, rank_ref, near_ref, far_ref, weight_ref, *refs):
    out_refs = refs[-3 - members : -3]
    lhs_ref, slot_ref, slot_sems = refs[-3:]
    weight_block = next_block(weight_ref, slot_ref, slot_sems, tiles)
    block = lhs_ref.shape[0] // len(order)
    half = len(order) // 2

    @pl.when(pl.program_id(0) == 0)
    def _():
        for slot, offset in enumerate(order):
            at = (rank_ref[0] ^ offset) * block
            row = (slot % half) * block
            from_ref = far_ref if slot >= half else near_ref
            lhs_ref[pl.ds(pl.multiple_of(at, block), block), :] = from_ref[row : row + block]

    pre = jnp.dot(lhs_ref[...], weight_block[...], preferred_element_type=F32)
    rows = pre.shape[0] // members
    for member in range(members):
        taken = pre[member * rows : (member + 1) * rows]
        out_refs[member][...] = taken.astype(out_refs[member].dtype)


def encode(rank, near, far, enc_weight, members, order, after):
    rows, depth = 2 * near.shape[0], near.shape[1]
    width = enc_weight.shape[2]
    rows_each = rows // members
    tile = tile_of(width, 512)
    tiles = width // tile
    return pl.pallas_call(
        functools.partial(encode_body, members, order, tiles),
        grid_spec=pltpu.PrefetchScalarGridSpec(
            num_scalar_prefetch=1,
            grid=(width // tile,),
            in_specs=[whole(near.shape)] * 2 + in_hbm(1) + unread(after),
            out_specs=[pl.BlockSpec((rows_each, tile), lambda j, *_: (0, j))] * members,
            scratch_shapes=[pltpu.VMEM((rows, depth), BF16)] + slots(depth, tile, width // tile),
        ),
        out_shape=[jax.ShapeDtypeStruct((rows_each, width), F32)]
        + [jax.ShapeDtypeStruct((rows_each, width), BF16)] * (members - 1),
        compiler_params=params(),
        cost_estimate=NO_COST,
    )(rank, near, far, enc_weight, *after)


def chunk_rows(total, unit):
    units = total // unit
    if units < 8:
        return [total]
    most = 3 * (units // 8)
    return [most * unit, most * unit, (units - 2 * most) * unit]


def on_device(
    owners, members, ranks, tokens, norm_gain, gate_weight, up_weight, down_weight, enc_weight,
    enc_bias, adjoint,
):
    row_at = lax.axis_index("rows")
    member_at = lax.axis_index("mp")
    rank_at = lax.axis_index("hid")
    rank = rank_at.astype(jnp.int32).reshape(1)
    per_device = adjoint.shape[0]
    cut = tokens.shape[1]
    half_cuts = ranks // owners
    model_width = cut * ranks

    gain = lax.dynamic_slice_in_dim(
        norm_gain[0], row_at * (model_width // owners), model_width // owners, 0
    ).reshape(half_cuts, 1, cut)
    own_tokens = lax.dynamic_slice_in_dim(tokens, member_at * per_device, per_device, 0)

    bits, order = doubling(ranks)

    def from_all(value, axis, size):
        return jnp.stack([value] + [shift(value, axis, size, hop) for hop in range(1, size)])

    def place_of(offset):
        place = 0
        for at in range(len(bits)):
            place = place + ((offset >> at) & 1) * bits[at]
        return place

    def after(values, others):
        return lax.optimization_barrier((values, others))[0]

    def doubled(gathered, bit):
        return jnp.concatenate((gathered, swap(gathered, "hid", ranks, bit)))

    def from_owners(gathered):
        wide = gathered.astype(F32)
        squares = jnp.sum(wide * wide, axis=(0, 2))
        inverse = lax.rsqrt(squares / model_width + 1e-05)
        columns = []
        for hop in range(owners):
            target = lax.rem(row_at + owners - hop, owners)
            half = jnp.concatenate(
                [
                    lax.dynamic_slice_in_dim(
                        gathered, place_of(rank_at ^ (target * half_cuts + at)), 1, 0
                    )
                    for at in range(half_cuts)
                ]
            )
            columns.append(half if hop == 0 else shift(half, "rows", owners, hop))
        return columns, inverse

    def from_members(columns):
        return from_all(jnp.stack(columns), "mp", members)

    def normed(columns, inverses):
        return (columns.astype(F32) * inverses[:, :, None, :, None] * gain).astype(BF16)

    sizes = chunk_rows(per_device, 16 * max(1, ranks // (owners * members)))
    starts = [sum(sizes[:at]) for at in range(len(sizes))]
    chunks = len(sizes)
    head = sizes[0]

    gathered = own_tokens[:head][None]
    rest = own_tokens[head:][None] if chunks > 1 else None
    for bit in bits:
        gathered = doubled(gathered, bit)
        if rest is not None:
            rest = doubled(after(rest, gathered), bit)
    columns, inverse = from_owners(gathered)
    if rest is not None:
        rest_columns, rest_inverse = from_owners(after(rest, (columns, inverse)))
        rest = [rest_columns, rest_inverse]
    inverses = from_all(inverse, "rows", owners)
    columns, inverses = after((columns, inverses), (columns, inverses))
    xs = [normed(from_members(columns), from_all(inverses, "mp", members))]

    sums, hidden, layer, blocks, outs = ({} for _ in range(5))
    last = []

    def gate_up_of(t):
        tiles = gate_weight.shape[2] // tile_of(gate_weight.shape[2], 256)
        early = tiles // 2 if t == 0 and chunks > 1 else 0
        sums[t] = []
        for first, count in ((0, early), (early, tiles - early)):
            if not count:
                continue
            own, *sends = gate_up(xs[t], gate_weight, up_weight, first, count, list(last))
            last[:] = [own]
            if t == 0 and rest is not None:
                if not first:
                    rest[1] = from_all(after(rest[1], own), "mp", members)
                last.extend(rest[0])
                last.append(rest[1])
            others = [send(sends[hop - 1], "rows", owners, hop) for hop in range(1, owners)]
            sums[t].append((own, others))

    def rest_of():
        inverses = from_all(after(rest[1], sums[0][-1][0]), "rows", owners).transpose(1, 0, 2)
        sums[0][-1] = after(sums[0][-1], inverses)
        columns = from_members(rest[0])
        for start, q in zip(starts[1:], sizes[1:]):
            rows = slice(start - head, start - head + q)
            xs.append(normed(columns[:, :, :, rows], inverses[:, :, rows]))

    def hidden_of(t):
        if t == 0 and rest is not None:
            rest_of()
        units = []
        parts = ordered(sums[t]) if 0 < t == chunks - 1 else sums[t]
        for own, others in parts:
            acts = own
            for other in others:
                acts = acts + other.astype(F32)
            units.append((jax.nn.silu(acts[0]) * acts[1]).astype(BF16))
        units = jnp.concatenate(units, axis=1)
        hidden[t] = [units] + [shift(units, "rows", owners, hop) for hop in range(1, owners)]
        last.append(units)

    def ordered(values):
        return after(values, last[0])

    def at_once(t):
        return t == chunks - 1 and ranks == 4

    def down_of(t):
        total, going = down(rank, [[units] for units in hidden[t]], down_weight, members, order, list(last))
        last[:] = [total]
        if at_once(t):
            block = total.shape[0] // 2
            far = total[block:].astype(BF16)
            arrived = [
                swap(part, "hid", ranks, offset)
                for part, offset in ((going[block:], 3), (far, 2), (going[:block], 1))
            ]
            layer[t] = (total[:block], arrived)
        else:
            layer[t] = (total, swap(going, "hid", ranks, 1))

    def halve_of(t):
        if at_once(t):
            return
        total, arrived = ordered(layer[t])
        if chunks > 1 and t == chunks - 2:
            total, arrived = after((total, arrived), hidden[t + 1][0])
        for bit in reversed(bits[:-1]):
            total = total + arrived.astype(F32)
            kept = total.shape[0] // 2
            going = total[kept:].astype(BF16)
            last.append(going)
            total, arrived = total[:kept], swap(going, "hid", ranks, bit)
        layer[t] = (total, arrived)

    def settle_of(t):
        total, arrived = ordered(layer[t])
        for part in arrived if at_once(t) else [arrived]:
            total = total + part.astype(F32)
        block = total.astype(BF16)
        last.append(block)
        if at_once(t):
            blocks[t] = [block] + [swap(block, "hid", ranks, offset) for offset in (1, 2, 3)]
        else:
            layer[t] = (block, swap(block, "hid", ranks, bits[0]))

    def double_of(t):
        if at_once(t):
            return
        near, far = ordered(layer[t])
        if t > 0:
            near, far = after((near, far), sums[t - 1][0])
        elif chunks > 1:
            near, far = after((near, far), hidden[1])
        for bit in bits[1:]:
            near = jnp.concatenate((near, far))
            last.append(near)
            far = swap(near, "hid", ranks, bit)
        blocks[t] = (near, far)

    def features_of(t):
        near_far = blocks[t]
        if at_once(t):
            parts = ordered(near_far)
            near_far = (jnp.concatenate(parts[0::2]), jnp.concatenate(parts[1::2]))
        own, *sends = encode(rank, *near_far, enc_weight, members, order, list(last))
        last[:] = [own]
        sums[t] = (own, [send(sends[hop - 1], "mp", members, hop) for hop in range(1, members)])

    def share_of(t):
        total, others = ordered(sums[t])
        for other in others:
            total = total + other.astype(F32)
        q = sizes[t]
        others = []
        for hop in range(1, owners):
            going = total[hop * q : (hop + 1) * q].astype(BF16)
            last.append(going)
            others.append(send(going, "rows", owners, hop))
        sums[t] = (total[:q], others)

    def shared_of(t):
        last.extend(sums[t][1])

    def finish_of(t):
        pre, others = sums[t]
        for other in others:
            pre = pre + other.astype(F32)
        pre = pre + enc_bias[None, :]
        factor = adjoint[starts[t] : starts[t] + sizes[t]].astype(F32)
        outs[t] = (jnp.maximum(pre, 0.0) * factor).astype(BF16)

    stages = (
        (gate_up_of, 0), (hidden_of, 0), (gate_up_of, 1), (down_of, 0), (halve_of, 0),
        (hidden_of, 1), (gate_up_of, 2), (settle_of, 0), (down_of, 1), (double_of, 0),
        (hidden_of, 2), (halve_of, 1), (features_of, 0), (settle_of, 1), (down_of, 2),
        (share_of, 0), (settle_of, 2), (double_of, 1), (features_of, 1), (shared_of, 0),
        (features_of, 2), (share_of, 1), (share_of, 2), (finish_of, 0), (finish_of, 1),
        (finish_of, 2),
    )
    for stage, t in stages:
        if t < chunks:
            stage(t)
    gated = jnp.zeros(adjoint.shape, BF16)
    for t in range(chunks):
        gated = lax.dynamic_update_slice(gated, outs[t], (starts[t], 0))
    return gated


def solution(mesh):
    placed = (
        P(("groups", "rows"), "hid"),
        P("mp", None),
        P("mp", "rows", "hid"),
        P("mp", "rows", "hid"),
        P("mp", "hid", "rows"),
        P("mp", "rows", "hid"),
        P("hid"),
        P(("groups", "rows", "mp"), "hid"),
    )
    sizes = (mesh.shape["rows"], mesh.shape["mp"], mesh.shape["hid"])
    return jax.shard_map(
        functools.partial(on_device, *sizes),
        mesh=mesh,
        in_specs=placed,
        out_specs=P(("groups", "rows", "mp"), "hid"),
        check_vma=False,
    )
```

```python
import functools

import jax
import jax.numpy as jnp
from jax import lax
from jax.experimental import pallas as pl
from jax.experimental.pallas import tpu as pltpu
from jax.sharding import PartitionSpec as P

BF16 = jnp.bfloat16
F32 = jnp.float32
VMEM_BYTES = 51 * 1024 * 1024
GATE_UP_VMEM_BYTES = 44 * 1024 * 1024
BUFFERS = 8
GATE_UP_BUFFERS = 4


def shift(value, axis, size, hop):
    return lax.ppermute(value, axis, [((d + hop) % size, d) for d in range(size)])


def send(value, axis, size, hop):
    return lax.ppermute(value, axis, [(d, (d + hop) % size) for d in range(size)])


def swap(value, axis, size, bit):
    return lax.ppermute(value, axis, [(d, d ^ bit) for d in range(size)])


def doubling(size):
    bits = [1 << at for at in reversed(range(size.bit_length() - 1))]
    order = [0]
    for bit in bits:
        order = order + [offset ^ bit for offset in order]
    return bits, order


def tile_of(width, most):
    tile = most
    while tile > 128 and width % tile:
        tile //= 2
    return tile if width % tile == 0 else width


def whole(shape):
    return pl.BlockSpec(shape, lambda j, *_: (0,) * len(shape))


def slots(depth, tile, tiles, most=BUFFERS):
    count = min(most, tiles)
    return [pltpu.VMEM((count, depth, tile), BF16), pltpu.SemaphoreType.DMA((count,))]


def next_block(weight_ref, slot_ref, slot_sems, tiles, first=0):
    step = pl.program_id(0)
    count, _, tile = slot_ref.shape

    def copy(block, slot):
        columns = pl.ds(pl.multiple_of((first + block) * tile, 128), tile)
        return pltpu.make_async_copy(
            weight_ref.at[0, :, columns], slot_ref.at[slot], slot_sems.at[slot]
        )

    @pl.when(step == 0)
    def _():
        for block in range(count - 1):
            copy(block, block).start()

    ahead = step + count - 1

    @pl.when(ahead < tiles)
    def _():
        copy(ahead, lax.rem(ahead, count)).start()

    slot = lax.rem(step, count)
    copy(step, slot).wait()
    return slot_ref.at[slot]


def in_hbm(count):
    return [pl.BlockSpec(memory_space=pltpu.HBM)] * count


def unread(after):
    return [pl.BlockSpec(memory_space=pl.ANY)] * len(after)


def params(vmem_bytes=VMEM_BYTES):
    return pltpu.CompilerParams(
        dimension_semantics=("arbitrary",), vmem_limit_bytes=vmem_bytes
    )


NO_COST = pl.CostEstimate(flops=1, bytes_accessed=1, transcendentals=0)


def gate_up_body(tiles, first, x_ref, gate_ref, up_ref, *refs):
    members, owners, cuts, q, cut = x_ref.shape
    out_refs = refs[-5 - owners : -5]
    lhs_ref = refs[-5]
    blocks = [
        next_block(gate_ref, refs[-4], refs[-3], tiles, first),
        next_block(up_ref, refs[-2], refs[-1], tiles, first),
    ]

    @pl.when(pl.program_id(0) == 0)
    def _():
        for owner in range(owners):
            for member in range(members):
                row = (owner * members + member) * q
                for at in range(cuts):
                    lhs_ref[row : row + q, at * cut : (at + 1) * cut] = x_ref[member, owner, at]

    rows = members * q
    for at, block_ref in enumerate(blocks):
        acts = jnp.dot(lhs_ref[...], block_ref[...], preferred_element_type=F32)
        for hop in range(owners):
            taken = acts[hop * rows : (hop + 1) * rows]
            out_refs[hop][at] = taken.astype(out_refs[hop].dtype)


def gate_up(x, gate_weight, up_weight, first, tiles, after):
    members, owners, cuts, q, cut = x.shape
    rows, depth, own_rows = members * owners * q, cuts * cut, members * q
    tile = tile_of(gate_weight.shape[2], 256)
    width = tiles * tile
    return pl.pallas_call(
        functools.partial(gate_up_body, tiles, first),
        grid=(tiles,),
        in_specs=[whole(x.shape)] + in_hbm(2) + unread(after),
        out_specs=[pl.BlockSpec((2, own_rows, tile), lambda j: (0, 0, j))] * owners,
        out_shape=[jax.ShapeDtypeStruct((2, own_rows, width), F32)]
        + [jax.ShapeDtypeStruct((2, own_rows, width), BF16)] * (owners - 1),
        scratch_shapes=[pltpu.VMEM((rows, depth), BF16)] + slots(depth, tile, tiles, GATE_UP_BUFFERS) * 2,
        compiler_params=params(GATE_UP_VMEM_BYTES),
        cost_estimate=NO_COST,
    )(x, gate_weight, up_weight, *after)


def down_body(owners, members, pieces, order, tiles, rank_ref, *refs):
    hidden_refs = refs[: owners * pieces]
    weight_ref = refs[owners * pieces]
    out_refs = refs[-6:-4]
    lhs_ref, acc_ref, slot_ref, slot_sems = refs[-4:]
    block_ref = next_block(weight_ref, slot_ref, slot_sems, tiles)
    q = hidden_refs[0].shape[0] // members
    part = hidden_refs[0].shape[1]
    block = acc_ref.shape[0] // len(order)

    @pl.when(pl.program_id(0) == 0)
    def _():
        for owner in range(owners):
            for piece in range(pieces):
                for member in range(members):
                    row = (member * owners + owner) * q
                    lhs_ref[row : row + q, piece * part : (piece + 1) * part] = hidden_refs[
                        owner * pieces + piece
                    ][member * q : (member + 1) * q]

    acc_ref[...] = jnp.dot(lhs_ref[...], block_ref[...], preferred_element_type=F32)
    half = len(order) // 2
    for slot, offset in enumerate(order):
        at = (rank_ref[0] ^ offset) * block
        taken = acc_ref[pl.ds(pl.multiple_of(at, block), block), :]
        out_ref = out_refs[slot // half]
        row = (slot % half) * block
        out_ref[row : row + block] = taken.astype(out_ref.dtype)


def down(rank, hidden, down_weight, members, order, after):
    owners, pieces = len(hidden), len(hidden[0])
    rows_each, part = hidden[0][0].shape
    rows, depth, width = owners * rows_each, pieces * part, down_weight.shape[2]
    tile = tile_of(width, 256)
    return pl.pallas_call(
        functools.partial(down_body, owners, members, pieces, order, width // tile),
        grid_spec=pltpu.PrefetchScalarGridSpec(
            num_scalar_prefetch=1,
            grid=(width // tile,),
            in_specs=[whole((rows_each, part))] * (owners * pieces)
            + in_hbm(1)
            + unread(after),
            out_specs=[pl.BlockSpec((rows // 2, tile), lambda j, *_: (0, j))] * 2,
            scratch_shapes=[pltpu.VMEM((rows, depth), BF16), pltpu.VMEM((rows, tile), F32)]
            + slots(depth, tile, width // tile),
        ),
        out_shape=[jax.ShapeDtypeStruct((rows // 2, width), kind) for kind in (F32, BF16)],
        compiler_params=params(),
        cost_estimate=NO_COST,
    )(rank, *[piece for of_owner in hidden for piece in of_owner], down_weight, *after)


def encode_body(members, order, tiles, rank_ref, near_ref, far_ref, weight_ref, *refs):
    out_refs = refs[-3 - members : -3]
    lhs_ref, slot_ref, slot_sems = refs[-3:]
    weight_block = next_block(weight_ref, slot_ref, slot_sems, tiles)
    block = lhs_ref.shape[0] // len(order)
    half = len(order) // 2

    @pl.when(pl.program_id(0) == 0)
    def _():
        for slot, offset in enumerate(order):
            at = (rank_ref[0] ^ offset) * block
            row = (slot % half) * block
            from_ref = far_ref if slot >= half else near_ref
            lhs_ref[pl.ds(pl.multiple_of(at, block), block), :] = from_ref[row : row + block]

    pre = jnp.dot(lhs_ref[...], weight_block[...], preferred_element_type=F32)
    rows = pre.shape[0] // members
    for member in range(members):
        taken = pre[member * rows : (member + 1) * rows]
        out_refs[member][...] = taken.astype(out_refs[member].dtype)


def encode(rank, near, far, enc_weight, members, order, after):
    rows, depth = 2 * near.shape[0], near.shape[1]
    width = enc_weight.shape[2]
    rows_each = rows // members
    tile = tile_of(width, 512)
    tiles = width // tile
    return pl.pallas_call(
        functools.partial(encode_body, members, order, tiles),
        grid_spec=pltpu.PrefetchScalarGridSpec(
            num_scalar_prefetch=1,
            grid=(width // tile,),
            in_specs=[whole(near.shape)] * 2 + in_hbm(1) + unread(after),
            out_specs=[pl.BlockSpec((rows_each, tile), lambda j, *_: (0, j))] * members,
            scratch_shapes=[pltpu.VMEM((rows, depth), BF16)] + slots(depth, tile, width // tile),
        ),
        out_shape=[jax.ShapeDtypeStruct((rows_each, width), F32)]
        + [jax.ShapeDtypeStruct((rows_each, width), BF16)] * (members - 1),
        compiler_params=params(),
        cost_estimate=NO_COST,
    )(rank, near, far, enc_weight, *after)


def chunk_rows(total, unit):
    units = total // unit
    if units < 8:
        return [total]
    most = 3 * (units // 8)
    return [most * unit, most * unit, (units - 2 * most) * unit]


def on_device(
    owners, members, ranks, tokens, norm_gain, gate_weight, up_weight, down_weight, enc_weight,
    enc_bias, adjoint,
):
    row_at = lax.axis_index("rows")
    member_at = lax.axis_index("mp")
    rank_at = lax.axis_index("hid")
    rank = rank_at.astype(jnp.int32).reshape(1)
    per_device = adjoint.shape[0]
    cut = tokens.shape[1]
    half_cuts = ranks // owners
    model_width = cut * ranks

    gain = lax.dynamic_slice_in_dim(
        norm_gain[0], row_at * (model_width // owners), model_width // owners, 0
    ).reshape(half_cuts, 1, cut)
    own_tokens = lax.dynamic_slice_in_dim(tokens, member_at * per_device, per_device, 0)

    bits, order = doubling(ranks)

    def from_all(value, axis, size):
        return jnp.stack([value] + [shift(value, axis, size, hop) for hop in range(1, size)])

    def place_of(offset):
        place = 0
        for at in range(len(bits)):
            place = place + ((offset >> at) & 1) * bits[at]
        return place

    def after(values, others):
        return lax.optimization_barrier((values, others))[0]

    def doubled(gathered, bit):
        return jnp.concatenate((gathered, swap(gathered, "hid", ranks, bit)))

    def from_owners(gathered):
        wide = gathered.astype(F32)
        squares = jnp.sum(wide * wide, axis=(0, 2))
        inverse = lax.rsqrt(squares / model_width + 1e-05)
        columns = []
        for hop in range(owners):
            target = lax.rem(row_at + owners - hop, owners)
            half = jnp.concatenate(
                [
                    lax.dynamic_slice_in_dim(
                        gathered, place_of(rank_at ^ (target * half_cuts + at)), 1, 0
                    )
                    for at in range(half_cuts)
                ]
            )
            columns.append(half if hop == 0 else shift(half, "rows", owners, hop))
        return columns, inverse

    def from_members(columns):
        return from_all(jnp.stack(columns), "mp", members)

    def normed(columns, inverses):
        return (columns.astype(F32) * inverses[:, :, None, :, None] * gain).astype(BF16)

    sizes = chunk_rows(per_device, 16 * max(1, ranks // (owners * members)))
    starts = [sum(sizes[:at]) for at in range(len(sizes))]
    chunks = len(sizes)
    head = sizes[0]

    gathered = own_tokens[:head][None]
    rest = own_tokens[head:][None] if chunks > 1 else None
    for bit in bits:
        gathered = doubled(gathered, bit)
        if rest is not None:
            rest = doubled(after(rest, gathered), bit)
    columns, inverse = from_owners(gathered)
    if rest is not None:
        rest_columns, rest_inverse = from_owners(after(rest, (columns, inverse)))
        rest = [rest_columns, rest_inverse]
    inverses = from_all(inverse, "rows", owners)
    columns, inverses = after((columns, inverses), (columns, inverses))
    xs = [normed(from_members(columns), from_all(inverses, "mp", members))]

    sums, hidden, layer, blocks, outs = ({} for _ in range(5))
    last = []

    def gate_up_of(t):
        tiles = gate_weight.shape[2] // tile_of(gate_weight.shape[2], 256)
        early = tiles // 2 if t == 0 and chunks > 1 else 0
        sums[t] = []
        for first, count in ((0, early), (early, tiles - early)):
            if not count:
                continue
            own, *sends = gate_up(xs[t], gate_weight, up_weight, first, count, list(last))
            last[:] = [own]
            if t == 0 and rest is not None:
                if not first:
                    rest[1] = from_all(after(rest[1], own), "mp", members)
                last.extend(rest[0])
                last.append(rest[1])
            others = [send(sends[hop - 1], "rows", owners, hop) for hop in range(1, owners)]
            sums[t].append((own, others))

    def rest_of():
        inverses = from_all(after(rest[1], sums[0][-1][0]), "rows", owners).transpose(1, 0, 2)
        sums[0][-1] = after(sums[0][-1], inverses)
        columns = from_members(rest[0])
        for start, q in zip(starts[1:], sizes[1:]):
            rows = slice(start - head, start - head + q)
            xs.append(normed(columns[:, :, :, rows], inverses[:, :, rows]))

    def hidden_of(t):
        if t == 0 and rest is not None:
            rest_of()
        units = []
        parts = ordered(sums[t]) if 0 < t == chunks - 1 else sums[t]
        for own, others in parts:
            acts = own
            for other in others:
                acts = acts + other.astype(F32)
            units.append((jax.nn.silu(acts[0]) * acts[1]).astype(BF16))
        units = jnp.concatenate(units, axis=1)
        hidden[t] = [units] + [shift(units, "rows", owners, hop) for hop in range(1, owners)]
        last.append(units)

    def ordered(values):
        return after(values, last[0])

    def at_once(t):
        return t == chunks - 1 and ranks == 4

    def down_of(t):
        total, going = down(rank, [[units] for units in hidden[t]], down_weight, members, order, list(last))
        last[:] = [total]
        if at_once(t):
            block = total.shape[0] // 2
            far = total[block:].astype(BF16)
            arrived = [
                swap(part, "hid", ranks, offset)
                for part, offset in ((going[block:], 3), (far, 2), (going[:block], 1))
            ]
            layer[t] = (total[:block], arrived)
        else:
            layer[t] = (total, swap(going, "hid", ranks, 1))

    def halve_of(t):
        if at_once(t):
            return
        total, arrived = ordered(layer[t])
        if chunks > 1 and t == chunks - 2:
            total, arrived = after((total, arrived), hidden[t + 1][0])
        for bit in reversed(bits[:-1]):
            total = total + arrived.astype(F32)
            kept = total.shape[0] // 2
            going = total[kept:].astype(BF16)
            last.append(going)
            total, arrived = total[:kept], swap(going, "hid", ranks, bit)
        layer[t] = (total, arrived)

    def settle_of(t):
        total, arrived = ordered(layer[t])
        for part in arrived if at_once(t) else [arrived]:
            total = total + part.astype(F32)
        block = total.astype(BF16)
        last.append(block)
        if at_once(t):
            blocks[t] = [block] + [swap(block, "hid", ranks, offset) for offset in (1, 2, 3)]
        else:
            layer[t] = (block, swap(block, "hid", ranks, bits[0]))

    def double_of(t):
        if at_once(t):
            return
        near, far = ordered(layer[t])
        if t > 0:
            near, far = after((near, far), sums[t - 1][0])
        elif chunks > 1:
            near, far = after((near, far), hidden[1])
        for bit in bits[1:]:
            near = jnp.concatenate((near, far))
            last.append(near)
            far = swap(near, "hid", ranks, bit)
        blocks[t] = (near, far)

    def features_of(t):
        near_far = blocks[t]
        if at_once(t):
            parts = ordered(near_far)
            near_far = (jnp.concatenate(parts[0::2]), jnp.concatenate(parts[1::2]))
        own, *sends = encode(rank, *near_far, enc_weight, members, order, list(last))
        last[:] = [own]
        sums[t] = (own, [send(sends[hop - 1], "mp", members, hop) for hop in range(1, members)])

    def share_of(t):
        total, others = ordered(sums[t])
        for other in others:
            total = total + other.astype(F32)
        q = sizes[t]
        others = []
        for hop in range(1, owners):
            going = total[hop * q : (hop + 1) * q].astype(BF16)
            last.append(going)
            others.append(send(going, "rows", owners, hop))
        sums[t] = (total[:q], others)

    def shared_of(t):
        last.extend(sums[t][1])

    def finish_of(t):
        pre, others = sums[t]
        for other in others:
            pre = pre + other.astype(F32)
        pre = pre + enc_bias[None, :]
        factor = adjoint[starts[t] : starts[t] + sizes[t]].astype(F32)
        outs[t] = (jnp.maximum(pre, 0.0) * factor).astype(BF16)

    stages = (
        (gate_up_of, 0), (hidden_of, 0), (gate_up_of, 1), (down_of, 0), (halve_of, 0),
        (hidden_of, 1), (settle_of, 0), (gate_up_of, 2), (double_of, 0), (down_of, 1),
        (features_of, 0), (hidden_of, 2), (halve_of, 1), (settle_of, 1), (down_of, 2),
        (share_of, 0), (settle_of, 2), (double_of, 1), (features_of, 1), (shared_of, 0),
        (features_of, 2), (share_of, 1), (share_of, 2), (finish_of, 0), (finish_of, 1),
        (finish_of, 2),
    )
    for stage, t in stages:
        if t < chunks:
            stage(t)
    gated = jnp.zeros(adjoint.shape, BF16)
    for t in range(chunks):
        gated = lax.dynamic_update_slice(gated, outs[t], (starts[t], 0))
    return gated


def solution(mesh):
    placed = (
        P(("groups", "rows"), "hid"),
        P("mp", None),
        P("mp", "rows", "hid"),
        P("mp", "rows", "hid"),
        P("mp", "hid", "rows"),
        P("mp", "rows", "hid"),
        P("hid"),
        P(("groups", "rows", "mp"), "hid"),
    )
    sizes = (mesh.shape["rows"], mesh.shape["mp"], mesh.shape["hid"])
    return jax.shard_map(
        functools.partial(on_device, *sizes),
        mesh=mesh,
        in_specs=placed,
        out_specs=P(("groups", "rows", "mp"), "hid"),
        check_vma=False,
    )
```

```python
import functools

import jax
import jax.numpy as jnp
from jax import lax
from jax.experimental import pallas as pl
from jax.experimental.pallas import tpu as pltpu
from jax.sharding import PartitionSpec as P

BF16 = jnp.bfloat16
F32 = jnp.float32
VMEM_BYTES = 51 * 1024 * 1024
GATE_UP_VMEM_BYTES = 44 * 1024 * 1024
BUFFERS = 8
GATE_UP_BUFFERS = 4


def shift(value, axis, size, hop):
    return lax.ppermute(value, axis, [((d + hop) % size, d) for d in range(size)])


def send(value, axis, size, hop):
    return lax.ppermute(value, axis, [(d, (d + hop) % size) for d in range(size)])


def swap(value, axis, size, bit):
    return lax.ppermute(value, axis, [(d, d ^ bit) for d in range(size)])


def doubling(size):
    bits = [1 << at for at in reversed(range(size.bit_length() - 1))]
    order = [0]
    for bit in bits:
        order = order + [offset ^ bit for offset in order]
    return bits, order


def tile_of(width, most):
    tile = most
    while tile > 128 and width % tile:
        tile //= 2
    return tile if width % tile == 0 else width


def whole(shape):
    return pl.BlockSpec(shape, lambda j, *_: (0,) * len(shape))


def slots(depth, tile, tiles, most=BUFFERS):
    count = min(most, tiles)
    return [pltpu.VMEM((count, depth, tile), BF16), pltpu.SemaphoreType.DMA((count,))]


def next_block(weight_ref, slot_ref, slot_sems, tiles, first=0):
    step = pl.program_id(0)
    count, _, tile = slot_ref.shape

    def copy(block, slot):
        columns = pl.ds(pl.multiple_of((first + block) * tile, 128), tile)
        return pltpu.make_async_copy(
            weight_ref.at[0, :, columns], slot_ref.at[slot], slot_sems.at[slot]
        )

    @pl.when(step == 0)
    def _():
        for block in range(count - 1):
            copy(block, block).start()

    ahead = step + count - 1

    @pl.when(ahead < tiles)
    def _():
        copy(ahead, lax.rem(ahead, count)).start()

    slot = lax.rem(step, count)
    copy(step, slot).wait()
    return slot_ref.at[slot]


def in_hbm(count):
    return [pl.BlockSpec(memory_space=pltpu.HBM)] * count


def unread(after):
    return [pl.BlockSpec(memory_space=pl.ANY)] * len(after)


def params(vmem_bytes=VMEM_BYTES):
    return pltpu.CompilerParams(
        dimension_semantics=("arbitrary",), vmem_limit_bytes=vmem_bytes
    )


NO_COST = pl.CostEstimate(flops=1, bytes_accessed=1, transcendentals=0)


def gate_up_body(tiles, first, x_ref, gate_ref, up_ref, *refs):
    members, owners, cuts, q, cut = x_ref.shape
    out_refs = refs[-5 - owners : -5]
    lhs_ref = refs[-5]
    blocks = [
        next_block(gate_ref, refs[-4], refs[-3], tiles, first),
        next_block(up_ref, refs[-2], refs[-1], tiles, first),
    ]

    @pl.when(pl.program_id(0) == 0)
    def _():
        for owner in range(owners):
            for member in range(members):
                row = (owner * members + member) * q
                for at in range(cuts):
                    lhs_ref[row : row + q, at * cut : (at + 1) * cut] = x_ref[member, owner, at]

    rows = members * q
    for at, block_ref in enumerate(blocks):
        acts = jnp.dot(lhs_ref[...], block_ref[...], preferred_element_type=F32)
        for hop in range(owners):
            taken = acts[hop * rows : (hop + 1) * rows]
            out_refs[hop][at] = taken.astype(out_refs[hop].dtype)


def gate_up(x, gate_weight, up_weight, first, tiles, after):
    members, owners, cuts, q, cut = x.shape
    rows, depth, own_rows = members * owners * q, cuts * cut, members * q
    tile = tile_of(gate_weight.shape[2], 256)
    width = tiles * tile
    return pl.pallas_call(
        functools.partial(gate_up_body, tiles, first),
        grid=(tiles,),
        in_specs=[whole(x.shape)] + in_hbm(2) + unread(after),
        out_specs=[pl.BlockSpec((2, own_rows, tile), lambda j: (0, 0, j))] * owners,
        out_shape=[jax.ShapeDtypeStruct((2, own_rows, width), F32)]
        + [jax.ShapeDtypeStruct((2, own_rows, width), BF16)] * (owners - 1),
        scratch_shapes=[pltpu.VMEM((rows, depth), BF16)] + slots(depth, tile, tiles, GATE_UP_BUFFERS) * 2,
        compiler_params=params(GATE_UP_VMEM_BYTES),
        cost_estimate=NO_COST,
    )(x, gate_weight, up_weight, *after)


def down_body(owners, members, pieces, order, tiles, rank_ref, *refs):
    hidden_refs = refs[: owners * pieces]
    weight_ref = refs[owners * pieces]
    out_refs = refs[-6:-4]
    lhs_ref, acc_ref, slot_ref, slot_sems = refs[-4:]
    block_ref = next_block(weight_ref, slot_ref, slot_sems, tiles)
    q = hidden_refs[0].shape[0] // members
    part = hidden_refs[0].shape[1]
    block = acc_ref.shape[0] // len(order)

    @pl.when(pl.program_id(0) == 0)
    def _():
        for owner in range(owners):
            for piece in range(pieces):
                for member in range(members):
                    row = (member * owners + owner) * q
                    lhs_ref[row : row + q, piece * part : (piece + 1) * part] = hidden_refs[
                        owner * pieces + piece
                    ][member * q : (member + 1) * q]

    acc_ref[...] = jnp.dot(lhs_ref[...], block_ref[...], preferred_element_type=F32)
    half = len(order) // 2
    for slot, offset in enumerate(order):
        at = (rank_ref[0] ^ offset) * block
        taken = acc_ref[pl.ds(pl.multiple_of(at, block), block), :]
        out_ref = out_refs[slot // half]
        row = (slot % half) * block
        out_ref[row : row + block] = taken.astype(out_ref.dtype)


def down(rank, hidden, down_weight, members, order, after):
    owners, pieces = len(hidden), len(hidden[0])
    rows_each, part = hidden[0][0].shape
    rows, depth, width = owners * rows_each, pieces * part, down_weight.shape[2]
    tile = tile_of(width, 256)
    return pl.pallas_call(
        functools.partial(down_body, owners, members, pieces, order, width // tile),
        grid_spec=pltpu.PrefetchScalarGridSpec(
            num_scalar_prefetch=1,
            grid=(width // tile,),
            in_specs=[whole((rows_each, part))] * (owners * pieces)
            + in_hbm(1)
            + unread(after),
            out_specs=[pl.BlockSpec((rows // 2, tile), lambda j, *_: (0, j))] * 2,
            scratch_shapes=[pltpu.VMEM((rows, depth), BF16), pltpu.VMEM((rows, tile), F32)]
            + slots(depth, tile, width // tile),
        ),
        out_shape=[jax.ShapeDtypeStruct((rows // 2, width), kind) for kind in (F32, BF16)],
        compiler_params=params(),
        cost_estimate=NO_COST,
    )(rank, *[piece for of_owner in hidden for piece in of_owner], down_weight, *after)


def encode_body(members, order, tiles, rank_ref, near_ref, far_ref, weight_ref, *refs):
    out_refs = refs[-3 - members : -3]
    lhs_ref, slot_ref, slot_sems = refs[-3:]
    weight_block = next_block(weight_ref, slot_ref, slot_sems, tiles)
    block = lhs_ref.shape[0] // len(order)
    half = len(order) // 2

    @pl.when(pl.program_id(0) == 0)
    def _():
        for slot, offset in enumerate(order):
            at = (rank_ref[0] ^ offset) * block
            row = (slot % half) * block
            from_ref = far_ref if slot >= half else near_ref
            lhs_ref[pl.ds(pl.multiple_of(at, block), block), :] = from_ref[row : row + block]

    pre = jnp.dot(lhs_ref[...], weight_block[...], preferred_element_type=F32)
    rows = pre.shape[0] // members
    for member in range(members):
        taken = pre[member * rows : (member + 1) * rows]
        out_refs[member][...] = taken.astype(out_refs[member].dtype)


def encode(rank, near, far, enc_weight, members, order, after):
    rows, depth = 2 * near.shape[0], near.shape[1]
    width = enc_weight.shape[2]
    rows_each = rows // members
    tile = tile_of(width, 256)
    tiles = width // tile
    return pl.pallas_call(
        functools.partial(encode_body, members, order, tiles),
        grid_spec=pltpu.PrefetchScalarGridSpec(
            num_scalar_prefetch=1,
            grid=(width // tile,),
            in_specs=[whole(near.shape)] * 2 + in_hbm(1) + unread(after),
            out_specs=[pl.BlockSpec((rows_each, tile), lambda j, *_: (0, j))] * members,
            scratch_shapes=[pltpu.VMEM((rows, depth), BF16)] + slots(depth, tile, width // tile),
        ),
        out_shape=[jax.ShapeDtypeStruct((rows_each, width), F32)]
        + [jax.ShapeDtypeStruct((rows_each, width), BF16)] * (members - 1),
        compiler_params=params(),
        cost_estimate=NO_COST,
    )(rank, near, far, enc_weight, *after)


def chunk_rows(total, unit):
    units = total // unit
    if units < 8:
        return [total]
    most = 3 * (units // 8)
    return [most * unit, most * unit, (units - 2 * most) * unit]


def on_device(
    owners, members, ranks, tokens, norm_gain, gate_weight, up_weight, down_weight, enc_weight,
    enc_bias, adjoint,
):
    row_at = lax.axis_index("rows")
    member_at = lax.axis_index("mp")
    rank_at = lax.axis_index("hid")
    rank = rank_at.astype(jnp.int32).reshape(1)
    per_device = adjoint.shape[0]
    cut = tokens.shape[1]
    half_cuts = ranks // owners
    model_width = cut * ranks

    gain = lax.dynamic_slice_in_dim(
        norm_gain[0], row_at * (model_width // owners), model_width // owners, 0
    ).reshape(half_cuts, 1, cut)
    own_tokens = lax.dynamic_slice_in_dim(tokens, member_at * per_device, per_device, 0)

    bits, order = doubling(ranks)

    def from_all(value, axis, size):
        return jnp.stack([value] + [shift(value, axis, size, hop) for hop in range(1, size)])

    def place_of(offset):
        place = 0
        for at in range(len(bits)):
            place = place + ((offset >> at) & 1) * bits[at]
        return place

    def after(values, others):
        return lax.optimization_barrier((values, others))[0]

    def doubled(gathered, bit):
        return jnp.concatenate((gathered, swap(gathered, "hid", ranks, bit)))

    def from_owners(gathered):
        wide = gathered.astype(F32)
        squares = jnp.sum(wide * wide, axis=(0, 2))
        inverse = lax.rsqrt(squares / model_width + 1e-05)
        columns = []
        for hop in range(owners):
            target = lax.rem(row_at + owners - hop, owners)
            half = jnp.concatenate(
                [
                    lax.dynamic_slice_in_dim(
                        gathered, place_of(rank_at ^ (target * half_cuts + at)), 1, 0
                    )
                    for at in range(half_cuts)
                ]
            )
            columns.append(half if hop == 0 else shift(half, "rows", owners, hop))
        return columns, inverse

    def from_members(columns):
        return from_all(jnp.stack(columns), "mp", members)

    def normed(columns, inverses):
        return (columns.astype(F32) * inverses[:, :, None, :, None] * gain).astype(BF16)

    sizes = chunk_rows(per_device, 16 * max(1, ranks // (owners * members)))
    starts = [sum(sizes[:at]) for at in range(len(sizes))]
    chunks = len(sizes)
    head = sizes[0]

    gathered = own_tokens[:head][None]
    rest = own_tokens[head:][None] if chunks > 1 else None
    for bit in bits:
        gathered = doubled(gathered, bit)
        if rest is not None:
            rest = doubled(after(rest, gathered), bit)
    columns, inverse = from_owners(gathered)
    if rest is not None:
        rest_columns, rest_inverse = from_owners(after(rest, (columns, inverse)))
        rest = [rest_columns, rest_inverse]
    inverses = from_all(inverse, "rows", owners)
    columns, inverses = after((columns, inverses), (columns, inverses))
    xs = [normed(from_members(columns), from_all(inverses, "mp", members))]

    sums, hidden, layer, blocks, outs = ({} for _ in range(5))
    last = []

    def gate_up_of(t):
        tiles = gate_weight.shape[2] // tile_of(gate_weight.shape[2], 256)
        early = tiles // 2 if t == 0 and chunks > 1 else 0
        sums[t] = []
        for first, count in ((0, early), (early, tiles - early)):
            if not count:
                continue
            own, *sends = gate_up(xs[t], gate_weight, up_weight, first, count, list(last))
            last[:] = [own]
            if t == 0 and rest is not None:
                if not first:
                    rest[1] = from_all(after(rest[1], own), "mp", members)
                last.extend(rest[0])
                last.append(rest[1])
            others = [send(sends[hop - 1], "rows", owners, hop) for hop in range(1, owners)]
            sums[t].append((own, others))

    def rest_of():
        inverses = from_all(after(rest[1], sums[0][-1][0]), "rows", owners).transpose(1, 0, 2)
        sums[0][-1] = after(sums[0][-1], inverses)
        columns = from_members(rest[0])
        for start, q in zip(starts[1:], sizes[1:]):
            rows = slice(start - head, start - head + q)
            xs.append(normed(columns[:, :, :, rows], inverses[:, :, rows]))

    def hidden_of(t):
        if t == 0 and rest is not None:
            rest_of()
        units = []
        parts = ordered(sums[t]) if 0 < t == chunks - 1 else sums[t]
        for own, others in parts:
            acts = own
            for other in others:
                acts = acts + other.astype(F32)
            units.append((jax.nn.silu(acts[0]) * acts[1]).astype(BF16))
        units = jnp.concatenate(units, axis=1)
        hidden[t] = [units] + [shift(units, "rows", owners, hop) for hop in range(1, owners)]
        last.append(units)

    def ordered(values):
        return after(values, last[0])

    def at_once(t):
        return t == chunks - 1 and ranks == 4

    def down_of(t):
        total, going = down(rank, [[units] for units in hidden[t]], down_weight, members, order, list(last))
        last[:] = [total]
        if at_once(t):
            block = total.shape[0] // 2
            far = total[block:].astype(BF16)
            arrived = [
                swap(part, "hid", ranks, offset)
                for part, offset in ((going[block:], 3), (far, 2), (going[:block], 1))
            ]
            layer[t] = (total[:block], arrived)
        else:
            layer[t] = (total, swap(going, "hid", ranks, 1))

    def halve_of(t):
        if at_once(t):
            return
        total, arrived = ordered(layer[t])
        if chunks > 1 and t == chunks - 2:
            total, arrived = after((total, arrived), hidden[t + 1][0])
        for bit in reversed(bits[:-1]):
            total = total + arrived.astype(F32)
            kept = total.shape[0] // 2
            going = total[kept:].astype(BF16)
            last.append(going)
            total, arrived = total[:kept], swap(going, "hid", ranks, bit)
        layer[t] = (total, arrived)

    def settle_of(t):
        total, arrived = ordered(layer[t])
        for part in arrived if at_once(t) else [arrived]:
            total = total + part.astype(F32)
        block = total.astype(BF16)
        last.append(block)
        if at_once(t):
            blocks[t] = [block] + [swap(block, "hid", ranks, offset) for offset in (1, 2, 3)]
        else:
            layer[t] = (block, swap(block, "hid", ranks, bits[0]))

    def double_of(t):
        if at_once(t):
            return
        near, far = ordered(layer[t])
        if t > 0:
            near, far = after((near, far), sums[t - 1][0])
        elif chunks > 1:
            near, far = after((near, far), hidden[1])
        for bit in bits[1:]:
            near = jnp.concatenate((near, far))
            last.append(near)
            far = swap(near, "hid", ranks, bit)
        blocks[t] = (near, far)

    def features_of(t):
        near_far = blocks[t]
        if at_once(t):
            parts = ordered(near_far)
            near_far = (jnp.concatenate(parts[0::2]), jnp.concatenate(parts[1::2]))
        own, *sends = encode(rank, *near_far, enc_weight, members, order, list(last))
        last[:] = [own]
        sums[t] = (own, [send(sends[hop - 1], "mp", members, hop) for hop in range(1, members)])

    def share_of(t):
        total, others = ordered(sums[t])
        for other in others:
            total = total + other.astype(F32)
        q = sizes[t]
        others = []
        for hop in range(1, owners):
            going = total[hop * q : (hop + 1) * q].astype(BF16)
            last.append(going)
            others.append(send(going, "rows", owners, hop))
        sums[t] = (total[:q], others)

    def shared_of(t):
        last.extend(sums[t][1])

    def finish_of(t):
        pre, others = sums[t]
        for other in others:
            pre = pre + other.astype(F32)
        pre = pre + enc_bias[None, :]
        factor = adjoint[starts[t] : starts[t] + sizes[t]].astype(F32)
        outs[t] = (jnp.maximum(pre, 0.0) * factor).astype(BF16)

    stages = (
        (gate_up_of, 0), (hidden_of, 0), (gate_up_of, 1), (down_of, 0), (halve_of, 0),
        (hidden_of, 1), (settle_of, 0), (gate_up_of, 2), (double_of, 0), (down_of, 1),
        (features_of, 0), (hidden_of, 2), (halve_of, 1), (settle_of, 1), (down_of, 2),
        (share_of, 0), (settle_of, 2), (double_of, 1), (features_of, 1), (shared_of, 0),
        (features_of, 2), (share_of, 1), (share_of, 2), (finish_of, 0), (finish_of, 1),
        (finish_of, 2),
    )
    for stage, t in stages:
        if t < chunks:
            stage(t)
    gated = jnp.zeros(adjoint.shape, BF16)
    for t in range(chunks):
        gated = lax.dynamic_update_slice(gated, outs[t], (starts[t], 0))
    return gated


def solution(mesh):
    placed = (
        P(("groups", "rows"), "hid"),
        P("mp", None),
        P("mp", "rows", "hid"),
        P("mp", "rows", "hid"),
        P("mp", "hid", "rows"),
        P("mp", "rows", "hid"),
        P("hid"),
        P(("groups", "rows", "mp"), "hid"),
    )
    sizes = (mesh.shape["rows"], mesh.shape["mp"], mesh.shape["hid"])
    return jax.shard_map(
        functools.partial(on_device, *sizes),
        mesh=mesh,
        in_specs=placed,
        out_specs=P(("groups", "rows", "mp"), "hid"),
        check_vma=False,
    )
```

```python
import functools

import jax
import jax.numpy as jnp
from jax import lax
from jax.experimental import pallas as pl
from jax.experimental.pallas import tpu as pltpu
from jax.sharding import PartitionSpec as P

BF16 = jnp.bfloat16
F32 = jnp.float32
VMEM_BYTES = 51 * 1024 * 1024
GATE_UP_VMEM_BYTES = 44 * 1024 * 1024
BUFFERS = 8
GATE_UP_BUFFERS = 4


def shift(value, axis, size, hop):
    return lax.ppermute(value, axis, [((d + hop) % size, d) for d in range(size)])


def send(value, axis, size, hop):
    return lax.ppermute(value, axis, [(d, (d + hop) % size) for d in range(size)])


def swap(value, axis, size, bit):
    return lax.ppermute(value, axis, [(d, d ^ bit) for d in range(size)])


def doubling(size):
    bits = [1 << at for at in reversed(range(size.bit_length() - 1))]
    order = [0]
    for bit in bits:
        order = order + [offset ^ bit for offset in order]
    return bits, order


def tile_of(width, most):
    tile = most
    while tile > 128 and width % tile:
        tile //= 2
    return tile if width % tile == 0 else width


def whole(shape):
    return pl.BlockSpec(shape, lambda j, *_: (0,) * len(shape))


def slots(depth, tile, tiles, most=BUFFERS):
    count = min(most, tiles)
    return [pltpu.VMEM((count, depth, tile), BF16), pltpu.SemaphoreType.DMA((count,))]


def next_block(weight_ref, slot_ref, slot_sems, tiles, first=0):
    step = pl.program_id(0)
    count, _, tile = slot_ref.shape

    def copy(block, slot):
        columns = pl.ds(pl.multiple_of((first + block) * tile, 128), tile)
        return pltpu.make_async_copy(
            weight_ref.at[0, :, columns], slot_ref.at[slot], slot_sems.at[slot]
        )

    @pl.when(step == 0)
    def _():
        for block in range(count - 1):
            copy(block, block).start()

    ahead = step + count - 1

    @pl.when(ahead < tiles)
    def _():
        copy(ahead, lax.rem(ahead, count)).start()

    slot = lax.rem(step, count)
    copy(step, slot).wait()
    return slot_ref.at[slot]


def in_hbm(count):
    return [pl.BlockSpec(memory_space=pltpu.HBM)] * count


def unread(after):
    return [pl.BlockSpec(memory_space=pl.ANY)] * len(after)


def params(vmem_bytes=VMEM_BYTES):
    return pltpu.CompilerParams(
        dimension_semantics=("arbitrary",), vmem_limit_bytes=vmem_bytes
    )


NO_COST = pl.CostEstimate(flops=1, bytes_accessed=1, transcendentals=0)


def gate_up_body(tiles, first, x_ref, gate_ref, up_ref, *refs):
    members, owners, cuts, q, cut = x_ref.shape
    out_refs = refs[-5 - owners : -5]
    lhs_ref = refs[-5]
    blocks = [
        next_block(gate_ref, refs[-4], refs[-3], tiles, first),
        next_block(up_ref, refs[-2], refs[-1], tiles, first),
    ]

    @pl.when(pl.program_id(0) == 0)
    def _():
        for owner in range(owners):
            for member in range(members):
                row = (owner * members + member) * q
                for at in range(cuts):
                    lhs_ref[row : row + q, at * cut : (at + 1) * cut] = x_ref[member, owner, at]

    rows = members * q
    for at, block_ref in enumerate(blocks):
        acts = jnp.dot(lhs_ref[...], block_ref[...], preferred_element_type=F32)
        for hop in range(owners):
            taken = acts[hop * rows : (hop + 1) * rows]
            out_refs[hop][at] = taken.astype(out_refs[hop].dtype)


def gate_up(x, gate_weight, up_weight, first, tiles, after):
    members, owners, cuts, q, cut = x.shape
    rows, depth, own_rows = members * owners * q, cuts * cut, members * q
    tile = tile_of(gate_weight.shape[2], 256)
    width = tiles * tile
    return pl.pallas_call(
        functools.partial(gate_up_body, tiles, first),
        grid=(tiles,),
        in_specs=[whole(x.shape)] + in_hbm(2) + unread(after),
        out_specs=[pl.BlockSpec((2, own_rows, tile), lambda j: (0, 0, j))] * owners,
        out_shape=[jax.ShapeDtypeStruct((2, own_rows, width), F32)]
        + [jax.ShapeDtypeStruct((2, own_rows, width), BF16)] * (owners - 1),
        scratch_shapes=[pltpu.VMEM((rows, depth), BF16)] + slots(depth, tile, tiles, GATE_UP_BUFFERS) * 2,
        compiler_params=params(GATE_UP_VMEM_BYTES),
        cost_estimate=NO_COST,
    )(x, gate_weight, up_weight, *after)


def down_body(owners, members, pieces, order, tiles, rank_ref, *refs):
    hidden_refs = refs[: owners * pieces]
    weight_ref = refs[owners * pieces]
    out_refs = refs[-6:-4]
    lhs_ref, acc_ref, slot_ref, slot_sems = refs[-4:]
    block_ref = next_block(weight_ref, slot_ref, slot_sems, tiles)
    q = hidden_refs[0].shape[0] // members
    part = hidden_refs[0].shape[1]
    block = acc_ref.shape[0] // len(order)

    @pl.when(pl.program_id(0) == 0)
    def _():
        for owner in range(owners):
            for piece in range(pieces):
                for member in range(members):
                    row = (member * owners + owner) * q
                    lhs_ref[row : row + q, piece * part : (piece + 1) * part] = hidden_refs[
                        owner * pieces + piece
                    ][member * q : (member + 1) * q]

    acc_ref[...] = jnp.dot(lhs_ref[...], block_ref[...], preferred_element_type=F32)
    half = len(order) // 2
    for slot, offset in enumerate(order):
        at = (rank_ref[0] ^ offset) * block
        taken = acc_ref[pl.ds(pl.multiple_of(at, block), block), :]
        out_ref = out_refs[slot // half]
        row = (slot % half) * block
        out_ref[row : row + block] = taken.astype(out_ref.dtype)


def down(rank, hidden, down_weight, members, order, after):
    owners, pieces = len(hidden), len(hidden[0])
    rows_each, part = hidden[0][0].shape
    rows, depth, width = owners * rows_each, pieces * part, down_weight.shape[2]
    tile = tile_of(width, 256)
    return pl.pallas_call(
        functools.partial(down_body, owners, members, pieces, order, width // tile),
        grid_spec=pltpu.PrefetchScalarGridSpec(
            num_scalar_prefetch=1,
            grid=(width // tile,),
            in_specs=[whole((rows_each, part))] * (owners * pieces)
            + in_hbm(1)
            + unread(after),
            out_specs=[pl.BlockSpec((rows // 2, tile), lambda j, *_: (0, j))] * 2,
            scratch_shapes=[pltpu.VMEM((rows, depth), BF16), pltpu.VMEM((rows, tile), F32)]
            + slots(depth, tile, width // tile),
        ),
        out_shape=[jax.ShapeDtypeStruct((rows // 2, width), kind) for kind in (F32, BF16)],
        compiler_params=params(),
        cost_estimate=NO_COST,
    )(rank, *[piece for of_owner in hidden for piece in of_owner], down_weight, *after)


def encode_body(members, order, tiles, rank_ref, near_ref, far_ref, weight_ref, *refs):
    out_refs = refs[-3 - members : -3]
    lhs_ref, slot_ref, slot_sems = refs[-3:]
    weight_block = next_block(weight_ref, slot_ref, slot_sems, tiles)
    block = lhs_ref.shape[0] // len(order)
    half = len(order) // 2

    @pl.when(pl.program_id(0) == 0)
    def _():
        for slot, offset in enumerate(order):
            at = (rank_ref[0] ^ offset) * block
            row = (slot % half) * block
            from_ref = far_ref if slot >= half else near_ref
            lhs_ref[pl.ds(pl.multiple_of(at, block), block), :] = from_ref[row : row + block]

    pre = jnp.dot(lhs_ref[...], weight_block[...], preferred_element_type=F32)
    rows = pre.shape[0] // members
    for member in range(members):
        taken = pre[member * rows : (member + 1) * rows]
        out_refs[member][...] = taken.astype(out_refs[member].dtype)


def encode(rank, near, far, enc_weight, members, order, after):
    rows, depth = 2 * near.shape[0], near.shape[1]
    width = enc_weight.shape[2]
    rows_each = rows // members
    tile = tile_of(width, 1024)
    tiles = width // tile
    return pl.pallas_call(
        functools.partial(encode_body, members, order, tiles),
        grid_spec=pltpu.PrefetchScalarGridSpec(
            num_scalar_prefetch=1,
            grid=(width // tile,),
            in_specs=[whole(near.shape)] * 2 + in_hbm(1) + unread(after),
            out_specs=[pl.BlockSpec((rows_each, tile), lambda j, *_: (0, j))] * members,
            scratch_shapes=[pltpu.VMEM((rows, depth), BF16)] + slots(depth, tile, width // tile),
        ),
        out_shape=[jax.ShapeDtypeStruct((rows_each, width), F32)]
        + [jax.ShapeDtypeStruct((rows_each, width), BF16)] * (members - 1),
        compiler_params=params(),
        cost_estimate=NO_COST,
    )(rank, near, far, enc_weight, *after)


def chunk_rows(total, unit):
    units = total // unit
    if units < 8:
        return [total]
    most = 3 * (units // 8)
    return [most * unit, most * unit, (units - 2 * most) * unit]


def on_device(
    owners, members, ranks, tokens, norm_gain, gate_weight, up_weight, down_weight, enc_weight,
    enc_bias, adjoint,
):
    row_at = lax.axis_index("rows")
    member_at = lax.axis_index("mp")
    rank_at = lax.axis_index("hid")
    rank = rank_at.astype(jnp.int32).reshape(1)
    per_device = adjoint.shape[0]
    cut = tokens.shape[1]
    half_cuts = ranks // owners
    model_width = cut * ranks

    gain = lax.dynamic_slice_in_dim(
        norm_gain[0], row_at * (model_width // owners), model_width // owners, 0
    ).reshape(half_cuts, 1, cut)
    own_tokens = lax.dynamic_slice_in_dim(tokens, member_at * per_device, per_device, 0)

    bits, order = doubling(ranks)

    def from_all(value, axis, size):
        return jnp.stack([value] + [shift(value, axis, size, hop) for hop in range(1, size)])

    def place_of(offset):
        place = 0
        for at in range(len(bits)):
            place = place + ((offset >> at) & 1) * bits[at]
        return place

    def after(values, others):
        return lax.optimization_barrier((values, others))[0]

    def doubled(gathered, bit):
        return jnp.concatenate((gathered, swap(gathered, "hid", ranks, bit)))

    def from_owners(gathered):
        wide = gathered.astype(F32)
        squares = jnp.sum(wide * wide, axis=(0, 2))
        inverse = lax.rsqrt(squares / model_width + 1e-05)
        columns = []
        for hop in range(owners):
            target = lax.rem(row_at + owners - hop, owners)
            half = jnp.concatenate(
                [
                    lax.dynamic_slice_in_dim(
                        gathered, place_of(rank_at ^ (target * half_cuts + at)), 1, 0
                    )
                    for at in range(half_cuts)
                ]
            )
            columns.append(half if hop == 0 else shift(half, "rows", owners, hop))
        return columns, inverse

    def from_members(columns):
        return from_all(jnp.stack(columns), "mp", members)

    def normed(columns, inverses):
        return (columns.astype(F32) * inverses[:, :, None, :, None] * gain).astype(BF16)

    sizes = chunk_rows(per_device, 16 * max(1, ranks // (owners * members)))
    starts = [sum(sizes[:at]) for at in range(len(sizes))]
    chunks = len(sizes)
    head = sizes[0]

    gathered = own_tokens[:head][None]
    rest = own_tokens[head:][None] if chunks > 1 else None
    for bit in bits:
        gathered = doubled(gathered, bit)
        if rest is not None:
            rest = doubled(after(rest, gathered), bit)
    columns, inverse = from_owners(gathered)
    if rest is not None:
        rest_columns, rest_inverse = from_owners(after(rest, (columns, inverse)))
        rest = [rest_columns, rest_inverse]
    inverses = from_all(inverse, "rows", owners)
    columns, inverses = after((columns, inverses), (columns, inverses))
    xs = [normed(from_members(columns), from_all(inverses, "mp", members))]

    sums, hidden, layer, blocks, outs = ({} for _ in range(5))
    last = []

    def gate_up_of(t):
        tiles = gate_weight.shape[2] // tile_of(gate_weight.shape[2], 256)
        early = tiles // 2 if t == 0 and chunks > 1 else 0
        sums[t] = []
        for first, count in ((0, early), (early, tiles - early)):
            if not count:
                continue
            own, *sends = gate_up(xs[t], gate_weight, up_weight, first, count, list(last))
            last[:] = [own]
            if t == 0 and rest is not None:
                if not first:
                    rest[1] = from_all(after(rest[1], own), "mp", members)
                last.extend(rest[0])
                last.append(rest[1])
            others = [send(sends[hop - 1], "rows", owners, hop) for hop in range(1, owners)]
            sums[t].append((own, others))

    def rest_of():
        inverses = from_all(after(rest[1], sums[0][-1][0]), "rows", owners).transpose(1, 0, 2)
        sums[0][-1] = after(sums[0][-1], inverses)
        columns = from_members(rest[0])
        for start, q in zip(starts[1:], sizes[1:]):
            rows = slice(start - head, start - head + q)
            xs.append(normed(columns[:, :, :, rows], inverses[:, :, rows]))

    def hidden_of(t):
        if t == 0 and rest is not None:
            rest_of()
        units = []
        parts = ordered(sums[t]) if 0 < t == chunks - 1 else sums[t]
        for own, others in parts:
            acts = own
            for other in others:
                acts = acts + other.astype(F32)
            units.append((jax.nn.silu(acts[0]) * acts[1]).astype(BF16))
        units = jnp.concatenate(units, axis=1)
        hidden[t] = [units] + [shift(units, "rows", owners, hop) for hop in range(1, owners)]
        last.append(units)

    def ordered(values):
        return after(values, last[0])

    def at_once(t):
        return t == chunks - 1 and ranks == 4

    def down_of(t):
        total, going = down(rank, [[units] for units in hidden[t]], down_weight, members, order, list(last))
        last[:] = [total]
        if at_once(t):
            block = total.shape[0] // 2
            far = total[block:].astype(BF16)
            arrived = [
                swap(part, "hid", ranks, offset)
                for part, offset in ((going[block:], 3), (far, 2), (going[:block], 1))
            ]
            layer[t] = (total[:block], arrived)
        else:
            layer[t] = (total, swap(going, "hid", ranks, 1))

    def halve_of(t):
        if at_once(t):
            return
        total, arrived = ordered(layer[t])
        if chunks > 1 and t == chunks - 2:
            total, arrived = after((total, arrived), hidden[t + 1][0])
        for bit in reversed(bits[:-1]):
            total = total + arrived.astype(F32)
            kept = total.shape[0] // 2
            going = total[kept:].astype(BF16)
            last.append(going)
            total, arrived = total[:kept], swap(going, "hid", ranks, bit)
        layer[t] = (total, arrived)

    def settle_of(t):
        total, arrived = ordered(layer[t])
        for part in arrived if at_once(t) else [arrived]:
            total = total + part.astype(F32)
        block = total.astype(BF16)
        last.append(block)
        if at_once(t):
            blocks[t] = [block] + [swap(block, "hid", ranks, offset) for offset in (1, 2, 3)]
        else:
            layer[t] = (block, swap(block, "hid", ranks, bits[0]))

    def double_of(t):
        if at_once(t):
            return
        near, far = ordered(layer[t])
        if t > 0:
            near, far = after((near, far), sums[t - 1][0])
        elif chunks > 1:
            near, far = after((near, far), hidden[1])
        for bit in bits[1:]:
            near = jnp.concatenate((near, far))
            last.append(near)
            far = swap(near, "hid", ranks, bit)
        blocks[t] = (near, far)

    def features_of(t):
        near_far = blocks[t]
        if at_once(t):
            parts = ordered(near_far)
            near_far = (jnp.concatenate(parts[0::2]), jnp.concatenate(parts[1::2]))
        own, *sends = encode(rank, *near_far, enc_weight, members, order, list(last))
        last[:] = [own]
        sums[t] = (own, [send(sends[hop - 1], "mp", members, hop) for hop in range(1, members)])

    def share_of(t):
        total, others = ordered(sums[t])
        for other in others:
            total = total + other.astype(F32)
        q = sizes[t]
        others = []
        for hop in range(1, owners):
            going = total[hop * q : (hop + 1) * q].astype(BF16)
            last.append(going)
            others.append(send(going, "rows", owners, hop))
        sums[t] = (total[:q], others)

    def shared_of(t):
        last.extend(sums[t][1])

    def finish_of(t):
        pre, others = sums[t]
        for other in others:
            pre = pre + other.astype(F32)
        pre = pre + enc_bias[None, :]
        factor = adjoint[starts[t] : starts[t] + sizes[t]].astype(F32)
        outs[t] = (jnp.maximum(pre, 0.0) * factor).astype(BF16)

    stages = (
        (gate_up_of, 0), (hidden_of, 0), (gate_up_of, 1), (down_of, 0), (halve_of, 0),
        (hidden_of, 1), (settle_of, 0), (gate_up_of, 2), (double_of, 0), (down_of, 1),
        (features_of, 0), (hidden_of, 2), (halve_of, 1), (settle_of, 1), (down_of, 2),
        (share_of, 0), (settle_of, 2), (double_of, 1), (features_of, 1), (shared_of, 0),
        (features_of, 2), (share_of, 1), (share_of, 2), (finish_of, 0), (finish_of, 1),
        (finish_of, 2),
    )
    for stage, t in stages:
        if t < chunks:
            stage(t)
    gated = jnp.zeros(adjoint.shape, BF16)
    for t in range(chunks):
        gated = lax.dynamic_update_slice(gated, outs[t], (starts[t], 0))
    return gated


def solution(mesh):
    placed = (
        P(("groups", "rows"), "hid"),
        P("mp", None),
        P("mp", "rows", "hid"),
        P("mp", "rows", "hid"),
        P("mp", "hid", "rows"),
        P("mp", "rows", "hid"),
        P("hid"),
        P(("groups", "rows", "mp"), "hid"),
    )
    sizes = (mesh.shape["rows"], mesh.shape["mp"], mesh.shape["hid"])
    return jax.shard_map(
        functools.partial(on_device, *sizes),
        mesh=mesh,
        in_specs=placed,
        out_specs=P(("groups", "rows", "mp"), "hid"),
        check_vma=False,
    )
```
